128 devices in a mesh: dp: 8 (over x, y_lo), seq: 16 (over z, y_hi, core).
Axes of the slice: x: 4, y: 4 (y_hi: 2, y_lo: 2; y = y_hi * 2 + y_lo), z: 4, core: 2. Of those that a mesh axis runs over, the one named last changes fastest.
Arguments:
- tokens: bfloat16 [8, 4096, 768], P('dp', 'seq'), may hold values from -6 to 6
- tile_coords: int32 [8, 2, 4096], P('dp', None, 'seq'), may hold values from 0 to 255
- slide_lengths: int32 [8, 4], P('dp'), may hold values from 1 to 3072, 4096 in all within a row
- norm_gain: float32 [768], replicated, may hold values from 0.25 to 1.75
- norm_bias: float32 [768], replicated, may hold values from -3 to 3
- w_qkv: bfloat16 [768, 2304], replicated, may hold values from -3 to 3
- w_out: bfloat16 [768, 768], replicated, may hold values from -0.21875 to 0.21875
- cotangent: bfloat16 [8, 4096, 768], P('dp', 'seq'), may hold values from -6 to 6
Outputs:
- layer_out: bfloat16 [8, 4096, 768], P('dp', 'seq')
- d_tokens: bfloat16 [8, 4096, 768], P('dp', 'seq')
- d_w_qkv: float32 [768, 2304], replicated
- d_w_out: float32 [768, 768], replicated
- d_gain: float32 [768], replicated
- d_bias: float32 [768], replicated
The draws below stay inside these ranges and needn't reach their ends.
Inputs may be any that keep to these rules, and one draw needn't show every extreme that they name: `slide_lengths`: every slide has 1 to 3072 tiles, the largest exactly that many, and the lengths of a sequence add up to 4096.
All inputs are finite; a program needn't handle non-finite values.
Results may differ from the reference program's by a relative error of at most 0.035.
The reference program's roundings to bfloat16 on the way count: a program that leaves them out, or rounds other values in their place, can miss the bound.
Values may be sent and summed in bfloat16 or wider, within the bound.
No kernel may reach another device: no remote copies, remote signals or barrier semaphores. Data moves between devices by JAX's collectives and lax.ppermute only.
A program may use at most 128 MiB of HBM per device.

```python
import math
import jax
import jax.numpy as jnp
import numpy as np
from jax import lax

D = 768
HEADS = 16
HEAD_DIM = 48
TOK_DEV = 256
SLIDES = 4
GRID = 256
GROUP = 4
BATCH = 8
SEQ_LEN = 4096
N_SEQ = 16


def draw_w_qkv(key, part):
    key = jax.random.fold_in(key, 17)
    first_key = jax.random.fold_in(key, 0)
    base = jax.random.normal(first_key, (D, 3 * D), jnp.float32) / D ** 0.5
    query_part = 4.0 * base[:, :D]
    base = jnp.concatenate([query_part, base[:, D:]], axis=1)
    return jnp.clip(base, -3.0, 3.0).astype(jnp.bfloat16)


def touch_ends(values, key, low, top_value):
    extent = values.shape
    spot = [jax.random.randint(jax.random.fold_in(key, axis), (), 0, extent[axis]) for axis in range(len(extent))]
    values = values.at[tuple(spot)].set(low)
    longest = extent.index(max(extent))
    spot[longest] = (spot[longest] + 1) % extent[longest]
    return values.at[tuple(spot)].set(top_value)


def levels(own_key, extent, cuts, low, largest):
    def one(position, parts):
        draws = jax.random.uniform(jax.random.fold_in(jax.random.fold_in(own_key, 6), position), (parts,), jnp.float32, low / len(cuts), largest / len(cuts))
        return jnp.repeat(jnp.exp(draws), extent[position] // parts).reshape((-1,) + (1,) * (len(extent) - position - 1))

    gain = one(*cuts[0])
    for cut in cuts[1:]:
        gain = gain * one(*cut)
    return gain


def profile(count, total, limit, lean):
    loads = [(1 << 20) // math.isqrt(grade ** lean) + 1 for grade in range(2, count + 1)]
    surplus, counts = total - limit - (count - 1), [1] * (count - 1)
    while surplus > 0:
        candidates = [i for i in range(count - 1) if counts[i] < limit]
        whole, left = sum([loads[i] for i in candidates]), surplus
        for i in candidates:
            more = min(limit - counts[i], max(1, left * loads[i] // whole), surplus)
            counts[i] = counts[i] + more
            surplus = surplus - more
    return np.array([limit] + counts)


def uneven(stream_key, count, total, limit, lean):
    if count == 2:
        one = jax.random.randint(stream_key, (), max(1, total - limit), min(limit, total - 1) + 1)
        return jnp.stack([one, total - one])
    sizes = jnp.asarray(profile(count, total, limit, lean), jnp.int32)
    couples = (count - 1) // 2
    giver, sink = sizes[1:1 + 2 * couples:2], sizes[2:2 + 2 * couples:2]
    slack = jnp.minimum(giver - 1, limit - sink)
    shifted = jax.random.randint(jax.random.fold_in(stream_key, 1), (couples,), 0, 1 << 20) % (slack + 1)
    sizes = sizes.at[1:1 + 2 * couples:2].set(giver - shifted).at[2:2 + 2 * couples:2].set(sink + shifted)
    return sizes[jax.random.permutation(jax.random.fold_in(stream_key, 2), count)]


def scatter_about(own_key, dims, width, most, shards=(), kind=jnp.bfloat16):
    level = levels(own_key, dims, shards, -0.22, 0.18) if shards else 1.0
    entries = jax.random.normal(own_key, dims, jnp.float32) * width * level
    return jnp.minimum(jnp.maximum(entries, -most), most).astype(kind)


def setup_inputs(seed: int = 0) -> dict:
    splits = jax.random.split(jax.random.key(seed), 9)
    tokens = scatter_about(splits[0], (BATCH, SEQ_LEN, D), 1.0, 6.0, ((0, 8), (1, 16)))
    tile_coords = touch_ends(jax.random.randint(splits[1], (BATCH, 2, SEQ_LEN), 0, GRID), jax.random.fold_in(splits[1], 1), 0, GRID - 1).astype(jnp.int32)
    slide_lengths = jax.vmap(lambda own: uneven(own, SLIDES, SEQ_LEN, 3 * SEQ_LEN // SLIDES, 2))(jax.random.split(splits[2], BATCH)).reshape((BATCH, SLIDES)).astype(jnp.int32)
    norm_gain = jnp.clip(1.0 + 0.15 * jax.random.normal(splits[3], (D,), jnp.float32), 0.25, 1.75)
    norm_bias = scatter_about(splits[4], (D,), 0.5, 3.0, (), jnp.float32)
    w_qkv = draw_w_qkv(jax.random.fold_in(splits[8], 71), 0)
    w_out = scatter_about(splits[6], (D, D), D ** -0.5, 0.21875)
    cotangent = scatter_about(splits[7], (BATCH, SEQ_LEN, D), 1.0, 6.0, ((0, 8), (1, 16)))
    return dict(tokens=tokens, tile_coords=tile_coords, slide_lengths=slide_lengths, norm_gain=norm_gain, norm_bias=norm_bias, w_qkv=w_qkv, w_out=w_out, cotangent=cotangent)


NEG = -1e+30

def embed_positions(coords):
    quarter = D // 4
    frequency = 1.0 / 10000.0 ** (jnp.arange(quarter, dtype=jnp.float32) / quarter)
    row_angle = coords[0].astype(jnp.float32)[:, None] * frequency[None, :]
    col_angle = coords[1].astype(jnp.float32)[:, None] * frequency[None, :]
    return jnp.concatenate([jnp.sin(row_angle), jnp.cos(row_angle), jnp.sin(col_angle), jnp.cos(col_angle)], axis=1)

def slide_index(lengths, positions):
    ends = jnp.cumsum(lengths, dtype=jnp.int32)
    return lax.optimization_barrier(jnp.sum((positions[:, None] >= ends[None, :]).astype(jnp.int32), axis=1, dtype=jnp.int32))

def pick_rows(source, dilation, residue):
    row_count = source.shape[0]
    shaped = source.reshape((row_count // dilation, dilation) + source.shape[1:])
    return lax.dynamic_index_in_dim(shaped, residue, axis=1, keepdims=False)

def spread_rows(picked, dilation, residue, fill_value):
    marker = jnp.arange(dilation, dtype=jnp.int32) == residue
    marker = marker.reshape((1, dilation) + (1,) * (picked.ndim - 1))
    placed = jnp.where(marker, jnp.expand_dims(picked, 1), fill_value)
    return placed.reshape((picked.shape[0] * dilation,) + picked.shape[1:])

def rounded_copy(values_in):
    return lax.optimization_barrier(values_in.astype(jnp.bfloat16)).astype(jnp.float32)

def level_views(head_index, q_rows, k_rows, v_rows, slide_ids):
    views_list = []
    for segment, dilation in ((TOK_DEV, 1), (GROUP * TOK_DEV, GROUP), (SEQ_LEN, N_SEQ)):
        residue = head_index % dilation
        groups = SEQ_LEN // segment
        per_group = segment // dilation
        q_lv = pick_rows(q_rows, dilation, residue).astype(jnp.float32).reshape(groups, per_group, HEAD_DIM)
        k_lv = pick_rows(k_rows, dilation, residue).astype(jnp.float32).reshape(groups, per_group, HEAD_DIM)
        v_lv = pick_rows(v_rows, dilation, residue).astype(jnp.float32).reshape(groups, per_group, HEAD_DIM)
        ids_lv = pick_rows(slide_ids, dilation, residue).reshape(groups, per_group)
        views_list.append((dilation, residue, q_lv, k_lv, v_lv, ids_lv))
    return views_list

def level_scores(q_lv, k_lv, ids_lv):
    scores = jnp.einsum('gqd,gkd->gqk', q_lv, k_lv, precision=lax.Precision.HIGHEST) * HEAD_DIM ** (-0.5)
    return jnp.where(ids_lv[:, :, None] == ids_lv[:, None, :], scores, NEG)

def head_forward(head_index, q_rows, k_rows, v_rows, slide_ids):
    views_list = level_views(head_index, q_rows, k_rows, v_rows, slide_ids)
    all_scores = []
    highest = None
    for dilation, residue, q_lv, k_lv, v_lv, ids_lv in views_list:
        scores = level_scores(q_lv, k_lv, ids_lv)
        all_scores.append(scores)
        spread = spread_rows(lax.optimization_barrier(jnp.max(scores, axis=2)).reshape(-1), dilation, residue, NEG)
        highest = spread if highest is None else jnp.maximum(highest, spread)
    weighted = jnp.zeros((SEQ_LEN, HEAD_DIM), jnp.float32)
    totals = jnp.zeros((SEQ_LEN,), jnp.float32)
    for view_item, scores in zip(views_list, all_scores):
        dilation, residue, q_lv, k_lv, v_lv, ids_lv = view_item
        level_top = pick_rows(highest, dilation, residue).reshape(scores.shape[:2])
        shares = jnp.exp(scores - level_top[:, :, None])
        totals = totals + spread_rows(lax.optimization_barrier(jnp.sum(shares, axis=2)).reshape(-1), dilation, residue, 0.0)
        level_part = jnp.einsum('gqk,gkd->gqd', rounded_copy(shares), v_lv, precision=lax.Precision.HIGHEST)
        weighted = weighted + spread_rows(level_part.reshape(-1, HEAD_DIM), dilation, residue, 0.0)
    output = (weighted / totals[:, None]).astype(jnp.bfloat16)
    return (output, highest + jnp.log(totals))

def head_backward(head_index, q_rows, k_rows, v_rows, slide_ids, d_output, output, log_total):
    views_list = level_views(head_index, q_rows, k_rows, v_rows, slide_ids)
    deltas = lax.optimization_barrier(jnp.sum(d_output.astype(jnp.float32) * output.astype(jnp.float32), axis=1))
    d_query = jnp.zeros((SEQ_LEN, HEAD_DIM), jnp.float32)
    d_key = jnp.zeros((SEQ_LEN, HEAD_DIM), jnp.float32)
    d_value = jnp.zeros((SEQ_LEN, HEAD_DIM), jnp.float32)
    scale = HEAD_DIM ** (-0.5)
    for dilation, residue, q_lv, k_lv, v_lv, ids_lv in views_list:
        scores = level_scores(q_lv, k_lv, ids_lv)
        lead = scores.shape[:2]
        level_top = pick_rows(log_total, dilation, residue).reshape(lead)
        shares = jnp.exp(scores - level_top[:, :, None])
        d_lv = pick_rows(d_output, dilation, residue).astype(jnp.float32).reshape(q_lv.shape)
        dv_part = jnp.einsum('gqk,gqd->gkd', rounded_copy(shares), d_lv, precision=lax.Precision.HIGHEST)
        d_shares = jnp.einsum('gqd,gkd->gqk', d_lv, v_lv, precision=lax.Precision.HIGHEST)
        level_delta = pick_rows(deltas, dilation, residue).reshape(lead)
        d_scores = rounded_copy(shares * (d_shares - level_delta[:, :, None]))
        dq_part = jnp.einsum('gqk,gkd->gqd', d_scores, k_lv, precision=lax.Precision.HIGHEST) * scale
        dk_part = jnp.einsum('gqk,gqd->gkd', d_scores, q_lv, precision=lax.Precision.HIGHEST) * scale
        d_query = d_query + spread_rows(dq_part.reshape(-1, HEAD_DIM), dilation, residue, 0.0)
        d_key = d_key + spread_rows(dk_part.reshape(-1, HEAD_DIM), dilation, residue, 0.0)
        d_value = d_value + spread_rows(dv_part.reshape(-1, HEAD_DIM), dilation, residue, 0.0)
    return (d_query, d_key, d_value)

def heads_major(block_rows):
    return block_rows.reshape(SEQ_LEN, HEADS, HEAD_DIM).transpose(1, 0, 2)

def rows_major(block_heads):
    return block_heads.transpose(1, 0, 2).reshape(SEQ_LEN, D)

def one_sequence(seq_item, norm_gain, norm_bias, w_qkv, w_out):
    tok_rows, coords, lengths, d_out = seq_item
    inputs = tok_rows.astype(jnp.float32) + embed_positions(coords)
    row_mean = lax.optimization_barrier(jnp.mean(inputs, axis=1, keepdims=True))
    centred = inputs - row_mean
    row_var = lax.optimization_barrier(jnp.mean(centred * centred, axis=1, keepdims=True))
    inv_std = lax.rsqrt(row_var + 1e-05)
    unit_rows = centred * inv_std
    normed = (unit_rows * norm_gain + norm_bias).astype(jnp.bfloat16)
    projected_qkv = jnp.dot(normed, w_qkv, preferred_element_type=jnp.float32).astype(jnp.bfloat16)
    q_heads = heads_major(projected_qkv[:, :D])
    k_heads = heads_major(projected_qkv[:, D:2 * D])
    v_heads = heads_major(projected_qkv[:, 2 * D:])
    slide_ids = slide_index(lengths, jnp.arange(SEQ_LEN, dtype=jnp.int32))
    head_ids = jnp.arange(HEADS, dtype=jnp.int32)
    outputs, log_totals = lax.map(lambda head_item: head_forward(head_item[0], head_item[1], head_item[2], head_item[3], slide_ids), (head_ids, q_heads, k_heads, v_heads))
    attended = rows_major(outputs)
    projected = jnp.dot(attended, w_out, preferred_element_type=jnp.float32)
    layer_out = (inputs + projected).astype(jnp.bfloat16)
    d_w_out = jnp.dot(attended.T, d_out, preferred_element_type=jnp.float32)
    d_attended = jnp.dot(d_out, w_out.T, preferred_element_type=jnp.float32).astype(jnp.bfloat16)
    d_query, d_key, d_value = lax.map(lambda head_item: head_backward(head_item[0], head_item[1], head_item[2], head_item[3], slide_ids, head_item[4], head_item[5], head_item[6]), (head_ids, q_heads, k_heads, v_heads, heads_major(d_attended), outputs, log_totals))
    d_qkv = jnp.concatenate([rows_major(d_query), rows_major(d_key), rows_major(d_value)], axis=1).astype(jnp.bfloat16)
    d_w_qkv = jnp.dot(normed.T, d_qkv, preferred_element_type=jnp.float32)
    d_normed = jnp.dot(d_qkv, w_qkv.T, preferred_element_type=jnp.float32)
    d_gain = lax.optimization_barrier(jnp.sum(d_normed * unit_rows, axis=0))
    d_bias = lax.optimization_barrier(jnp.sum(d_normed, axis=0))
    d_unit = d_normed * norm_gain
    d_inputs = inv_std * (d_unit - lax.optimization_barrier(jnp.mean(d_unit, axis=1, keepdims=True)) - unit_rows * lax.optimization_barrier(jnp.mean(d_unit * unit_rows, axis=1, keepdims=True)))
    d_tokens = (d_out.astype(jnp.float32) + d_inputs).astype(jnp.bfloat16)
    return (layer_out, d_tokens, d_w_qkv, d_w_out, d_gain, d_bias)

def reference(tokens, tile_coords, slide_lengths, norm_gain, norm_bias, w_qkv, w_out, cotangent):
    layer_out, d_tokens, d_w_qkv, d_w_out, d_gain, d_bias = lax.map(lambda seq_item: one_sequence(seq_item, norm_gain, norm_bias, w_qkv, w_out), (tokens, tile_coords, slide_lengths, cotangent))
    return (layer_out, d_tokens, lax.optimization_barrier(jnp.sum(d_w_qkv, axis=0)), lax.optimization_barrier(jnp.sum(d_w_out, axis=0)), lax.optimization_barrier(jnp.sum(d_gain, axis=0)), lax.optimization_barrier(jnp.sum(d_bias, axis=0)))
```

```python
import jax
import jax.numpy as jnp
import numpy as np
from jax import lax
from jax.experimental import pallas as pl
from jax.experimental.pallas import tpu as pltpu
from jax.sharding import PartitionSpec as P

HEADS = 16
HD = 48
D = 768
T = 256
SCALE = HD ** (-0.5)
NEG = -1e30
BF = jnp.bfloat16
F32 = jnp.float32
AXES = ("dp", "seq")
VMEM_LIMIT = 56 << 20


def iota(shape, dim):
    return lax.broadcasted_iota(jnp.int32, shape, dim)


def tile_of(i):
    return (i >> 6) + ((i >> 4) & 3) * 4 + (i & 15) * 16


def nt(a, b):
    return lax.dot_general(a, b, (((1,), (1,)), ((), ())), preferred_element_type=F32)


def nn(a, b):
    return lax.dot_general(a, b, (((1,), (0,)), ((), ())), preferred_element_type=F32)


def tn(a, b):
    return lax.dot_general(a, b, (((0,), (0,)), ((), ())), preferred_element_type=F32)


def exact(a, b):
    hi = a.astype(BF)
    rest = a - hi.astype(F32)
    mid = rest.astype(BF)
    low = (rest - mid.astype(F32)).astype(BF)
    return nn(hi, b) + nn(mid, b) + nn(low, b)


def sort_matrix():
    return jnp.where(tile_of(iota((T, T), 0)) == iota((T, T), 1), 1.0, 0.0).astype(BF)


def unsort_matrix():
    return jnp.where(iota((T, T), 0) == tile_of(iota((T, T), 1)), 1.0, 0.0).astype(BF)


def span_mask(lo, shape):
    lane = iota(shape, 1)
    return jnp.where((lane >= lo) & (lane < lo + HD), 1.0, 0.0)


def head_window(h):
    start = HD * h // 128 * 128
    width = 128 if HD * h - start + HD <= 128 else 256
    return start, width


def head_mask(h):
    start, width = head_window(h)
    return span_mask(HD * h - start, (1, width)).astype(BF)


def group_window(g):
    return 192 * g // 128 * 128


def group_mask(g):
    lo = 192 * g - group_window(g) + HD * (iota((T, 256), 0) >> 6)
    return span_mask(lo, (T, 256)).astype(BF)


def far_mask():
    row = iota((T, D), 0)
    lo = HD * ((row >> 6) + 4 * ((row >> 4) & 3))
    return span_mask(lo, (T, D)).astype(BF)


def slide_of(meta, pos):
    end = meta[1]
    out = jnp.where(pos >= end, 1, 0)
    for n in range(2, 5):
        end = end + meta[n]
        out = out + jnp.where(pos >= end, 1, 0)
    return out


def row_ids(meta):
    return slide_of(meta, meta[0] * T + tile_of(iota((T, 1), 0)))


def bias_of(meta, pos):
    return jnp.where(row_ids(meta) == slide_of(meta, pos), 0.0, NEG)


def local_bias(meta):
    return bias_of(meta, meta[0] * T + tile_of(iota((1, T), 1)))


def mid_bias(meta):
    t = iota((T, T), 1)
    slot = t >> 6
    dev = meta[0] ^ (((slot & 1) << 1) | (slot >> 1))
    pos = dev * T + ((t >> 4) & 3) * 4 + (t & 15) * 16 + (iota((T, T), 0) >> 6)
    return bias_of(meta, pos)


def far_bias(meta):
    t = iota((T, T), 1)
    s = t >> 4
    code = ((s & 1) << 1) ^ (((s >> 1) & 1) << 2) ^ (((s >> 2) & 1) * 12) ^ (s >> 3)
    row = iota((T, T), 0)
    pos = (meta[0] ^ code) * T + (t & 15) * 16 + (row >> 6) + 4 * ((row >> 4) & 3)
    return bias_of(meta, pos)


def far_head(b):
    return b // 4 + 4 * (b % 4)


def fold_mid(x, masks):
    out = x[0:64] * masks[0]
    for c in range(1, 4):
        out = out + x[64 * c : 64 * c + 64] * masks[c]
    return out


def fold_far(x, masks):
    out = x[0:16] * masks[0]
    for b in range(1, 16):
        out = out + x[16 * b : 16 * b + 16] * masks[far_head(b)]
    return out


def pack_rows(x, head_masks):
    mids = [
        head_masks[c] + head_masks[4 + c] + head_masks[8 + c] + head_masks[12 + c]
        for c in range(4)
    ]
    return jnp.concatenate([fold_mid(x, mids), fold_far(x, head_masks)], axis=0)


def norm_parts(inputs):
    mean = jnp.mean(inputs, axis=1, keepdims=True)
    centred = inputs - mean
    var = jnp.mean(centred * centred, axis=1, keepdims=True)
    inv_std = lax.rsqrt(var + 1e-05)
    return centred * inv_std, inv_std


def pre_kernel(tok, coords, table, gain, bias, w_qkv, w_out, cot,
               inp_o, norm_o, qkv_o, da_o, cot_o, kv_o, qd_o):
    sort = sort_matrix()
    tok_s = nn(sort, tok[...])
    cot_s = nn(sort, cot[...]).astype(BF)
    grid = iota((T, T), 0)
    parts = []
    for axis in range(2):
        hot = jnp.where(grid == coords[axis : axis + 1, :], 1.0, 0.0).astype(BF)
        hot = nt(sort, hot).astype(BF)
        found = nn(hot, table[...])
        parts.append(found[:, :384] + found[:, 384:768] + found[:, 768:])
    inputs = tok_s + jnp.concatenate(parts, axis=1)
    inp_o[...] = inputs
    unit, _ = norm_parts(inputs)
    normed = (unit * gain[...] + bias[...]).astype(BF)
    norm_o[...] = normed
    qkv = nn(normed, w_qkv[...]).astype(BF)
    qkv_o[...] = qkv
    cot_o[...] = cot_s
    d_att = nt(cot_s, w_out[...]).astype(BF)
    da_o[...] = d_att
    masks = [span_mask(HD * h, (1, D)).astype(BF) for h in range(HEADS)]
    kv_o[:, :D] = pack_rows(qkv[:, D : 2 * D], masks)
    kv_o[:, D:] = pack_rows(qkv[:, 2 * D :], masks)
    qd_o[:, :D] = pack_rows(qkv[:, :D], masks)
    qd_o[:, D:] = pack_rows(d_att, masks)


def soft(scores):
    top = jnp.max(scores, axis=1, keepdims=True)
    shares = jnp.exp(scores - top)
    return top, jnp.sum(shares, axis=1, keepdims=True), shares.astype(BF)


def local_forward_kernel(meta, qkv, o_o, top_o, sum_o):
    bias = local_bias(meta)
    o_o[...] = jnp.zeros_like(o_o)
    lane = iota((T, 128), 1)
    tops = jnp.full((T, 128), NEG, F32)
    sums = jnp.zeros((T, 128), F32)
    for h in range(HEADS):
        s, w = head_window(h)
        mask = head_mask(h)
        q = qkv[:, s : s + w] * mask
        scores = nt(q, qkv[:, D + s : D + s + w]) * SCALE + bias
        top, total, shares = soft(scores)
        tops = jnp.where(lane == h, top, tops)
        sums = jnp.where(lane == h, total, sums)
        o_o[:, s : s + w] += nn(shares, qkv[:, 2 * D + s : 2 * D + s + w] * mask)
    top_o[...] = tops
    sum_o[...] = sums


def pick_all(mine, other, base, lo, width):
    return jnp.concatenate(
        [mine[base : base + 128, lo : lo + width], other[base : base + 128, lo : lo + width]],
        axis=0,
    )


def expand_matrix():
    head = iota((128, D), 0)
    lane = iota((128, D), 1)
    return jnp.where((lane >= head * HD) & (lane < head * HD + HD), 1.0, 0.0).astype(BF)


def gather_matrix():
    lane = iota((D, 128), 0)
    head = iota((D, 128), 1)
    return jnp.where((lane >= head * HD) & (lane < head * HD + HD), 1.0, 0.0).astype(BF)


def remote_forward_kernel(meta, qkv, kv_a, kv_b, o_l, top_l, sum_l, inp, d_att, w_out, cot,
                          att_o, out_o, stat_o, send_o, dw_o):
    lane = iota((T, 128), 1)
    row = iota((T, 128), 0)
    tops_m = jnp.full((T, 128), NEG, F32)
    sums_m = jnp.zeros((T, 128), F32)
    mid = mid_bias(meta)
    mid_parts = []
    for g in range(4):
        s = group_window(g)
        mask = group_mask(g)
        q = qkv[:, s : s + 256] * mask
        scores = nt(q, pick_all(kv_a, kv_b, 0, s, 256)) * SCALE + mid
        top, total, shares = soft(scores)
        here = lane == 4 * g + (row >> 6)
        tops_m = jnp.where(here, top, tops_m)
        sums_m = jnp.where(here, total, sums_m)
        mid_parts.append(nn(shares, pick_all(kv_a, kv_b, 0, D + s, 256)))
    mask = far_mask()
    scores = nt(qkv[:, :D] * mask, pick_all(kv_a, kv_b, 128, 0, D)) * SCALE + far_bias(meta)
    top, total, shares = soft(scores)
    far_part = nn(shares, pick_all(kv_a, kv_b, 128, D, D))
    here = lane == (row >> 6) + 4 * ((row >> 4) & 3)
    tops_f = jnp.where(here, top, NEG)
    sums_f = jnp.where(here, total, 0.0)
    highest = jnp.maximum(jnp.maximum(top_l[...], tops_m), tops_f)
    f_l = jnp.exp(top_l[...] - highest)
    f_m = jnp.exp(tops_m - highest)
    f_f = jnp.exp(tops_f - highest)
    totals = f_l * sum_l[...] + f_m * sums_m + f_f * sums_f
    totals = jnp.where(lane < HEADS, totals, 1.0)
    inverse = 1.0 / totals
    lse = highest + jnp.log(totals)
    w_m = f_m * inverse
    att = o_l[...] * exact(f_l * inverse, expand_matrix())
    w_f = jnp.sum(jnp.where(here, f_f * inverse, 0.0), axis=1, keepdims=True)
    att = att + far_part * w_f * mask.astype(F32)
    att_o[...] = jnp.zeros_like(att_o)
    acc = [att[:, 128 * n : 128 * n + 128] for n in range(6)]
    for g in range(4):
        n = group_window(g) // 128
        w_g = jnp.sum(jnp.where(lane == 4 * g + (row >> 6), w_m, 0.0), axis=1, keepdims=True)
        add = mid_parts[g] * w_g * group_mask(g).astype(F32)
        acc[n] = acc[n] + add[:, :128]
        acc[n + 1] = acc[n + 1] + add[:, 128:]
    att = jnp.concatenate(acc, axis=1).astype(BF)
    att_o[...] = att
    prod = d_att[...].astype(F32) * att.astype(F32)
    delta = exact(prod, gather_matrix())
    stat = jnp.where(lane < HEADS, lse, pltpu.roll(delta, HEADS, 1))
    stat = jnp.where(lane < 2 * HEADS, stat, 0.0)
    stat_o[...] = stat
    one = iota((1, 128), 1)
    send_o[0:64] = fold_mid(stat, [jnp.where((one & 3) == c, 1.0, 0.0) for c in range(4)])
    send_o[64:80] = fold_far(stat, [jnp.where((one & 15) == h, 1.0, 0.0) for h in range(HEADS)])
    layer = (inp[...] + nn(att, w_out[...])).astype(BF)
    out_o[...] = nn(unsort_matrix(), layer).astype(BF)
    dw_o[...] = tn(att, cot[...]).astype(BF)


def pick_mid_column(stat, col):
    return jnp.concatenate(
        [stat[64 * c : 64 * c + 64, col + c : col + c + 1] for c in range(4)], axis=0
    )


def pick_far_column(stat, col):
    return jnp.concatenate(
        [
            stat[16 * b : 16 * b + 16, col + far_head(b) : col + far_head(b) + 1]
            for b in range(16)
        ],
        axis=0,
    )


def query_backward_kernel(meta, qkv, d_att, stat, kv_a, kv_b, dq_o, dk_o, dv_o):
    bias = local_bias(meta)
    dq_o[...] = jnp.zeros_like(dq_o)
    dk_o[...] = jnp.zeros_like(dk_o)
    dv_o[...] = jnp.zeros_like(dv_o)
    for h in range(HEADS):
        s, w = head_window(h)
        mask = head_mask(h)
        q = qkv[:, s : s + w] * mask
        k = qkv[:, D + s : D + s + w] * mask
        da = d_att[:, s : s + w] * mask
        scores = nt(q, k) * SCALE + bias
        shares = jnp.exp(scores - stat[:, h : h + 1])
        d_shares = nt(da, qkv[:, 2 * D + s : 2 * D + s + w])
        ds = (shares * (d_shares - stat[:, HEADS + h : HEADS + h + 1])).astype(BF)
        dq_o[:, s : s + w] += nn(ds, k)
        dk_o[:, s : s + w] += tn(ds, q)
        dv_o[:, s : s + w] += tn(shares.astype(BF), da)
    mid = mid_bias(meta)
    for g in range(4):
        s = group_window(g)
        mask = group_mask(g)
        k = pick_all(kv_a, kv_b, 0, s, 256)
        scores = nt(qkv[:, s : s + 256] * mask, k) * SCALE + mid
        shares = jnp.exp(scores - pick_mid_column(stat, 4 * g))
        d_shares = nt(d_att[:, s : s + 256] * mask, pick_all(kv_a, kv_b, 0, D + s, 256))
        ds = (shares * (d_shares - pick_mid_column(stat, HEADS + 4 * g))).astype(BF)
        dq_o[:, s : s + 256] += nn(ds, k) * mask.astype(F32)
    mask = far_mask()
    k = pick_all(kv_a, kv_b, 128, 0, D)
    scores = nt(qkv[:, :D] * mask, k) * SCALE + far_bias(meta)
    shares = jnp.exp(scores - pick_far_column(stat, 0))
    d_shares = nt(d_att[...] * mask, pick_all(kv_a, kv_b, 128, D, D))
    ds = (shares * (d_shares - pick_far_column(stat, HEADS))).astype(BF)
    dq_o[...] += nn(ds, k) * mask.astype(F32)


def spread_mid(stat_t, row):
    return jnp.concatenate(
        [jnp.broadcast_to(stat_t[row + c : row + c + 1, :], (64, T)) for c in range(4)], axis=0
    )


def spread_far(stat_t, row):
    return jnp.concatenate(
        [
            jnp.broadcast_to(stat_t[row + far_head(b) : row + far_head(b) + 1, :], (16, T))
            for b in range(16)
        ],
        axis=0,
    )


def key_backward_kernel(meta, qkv, qd_a, qd_b, st_a, st_b, dq, dk, dv, inp, normed, gain,
                        w_qkv, cot, tok_o, dw_o, vec_o, dk_s, dv_s):
    dk_s[...] = dk[...]
    dv_s[...] = dv[...]
    stat_t = pick_all(st_a, st_b, 0, 0, 128).T
    mid = mid_bias(meta)
    for g in range(4):
        s = group_window(g)
        mask = group_mask(g)
        mask_f = mask.astype(F32)
        q = pick_all(qd_a, qd_b, 0, s, 256)
        da = pick_all(qd_a, qd_b, 0, D + s, 256)
        scores = nt(qkv[:, D + s : D + s + 256] * mask, q) * SCALE + mid
        shares = jnp.exp(scores - spread_mid(stat_t, 4 * g))
        d_shares = nt(qkv[:, 2 * D + s : 2 * D + s + 256] * mask, da)
        ds = (shares * (d_shares - spread_mid(stat_t, HEADS + 4 * g))).astype(BF)
        dk_s[:, s : s + 256] += nn(ds, q) * mask_f
        dv_s[:, s : s + 256] += nn(shares.astype(BF), da) * mask_f
    stat_t = pick_all(st_a, st_b, 128, 0, 128).T
    mask = far_mask()
    mask_f = mask.astype(F32)
    q = pick_all(qd_a, qd_b, 128, 0, D)
    da = pick_all(qd_a, qd_b, 128, D, D)
    scores = nt(qkv[:, D : 2 * D] * mask, q) * SCALE + far_bias(meta)
    shares = jnp.exp(scores - spread_far(stat_t, 0))
    d_shares = nt(qkv[:, 2 * D :] * mask, da)
    ds = (shares * (d_shares - spread_far(stat_t, HEADS))).astype(BF)
    dk_s[...] += nn(ds, q) * mask_f
    dv_s[...] += nn(shares.astype(BF), da) * mask_f
    d_qkv = jnp.concatenate(
        [
            (dq[...] * SCALE).astype(BF),
            (dk_s[...] * SCALE).astype(BF),
            dv_s[...].astype(BF),
        ],
        axis=1,
    )
    dw_o[...] = tn(normed[...], d_qkv).astype(BF)
    d_normed = nt(d_qkv, w_qkv[...])
    unit, inv_std = norm_parts(inp[...])
    d_gain = jnp.sum(d_normed * unit, axis=0, keepdims=True)
    d_bias = jnp.sum(d_normed, axis=0, keepdims=True)
    vec_o[...] = jnp.concatenate([d_gain, d_bias, jnp.zeros((6, D), F32)], axis=0)
    d_unit = d_normed * gain[...]
    mean_a = jnp.mean(d_unit, axis=1, keepdims=True)
    mean_b = jnp.mean(d_unit * unit, axis=1, keepdims=True)
    d_tok = cot[...].astype(F32) + inv_std * (d_unit - mean_a - unit * mean_b)
    tok_o[...] = nn(unsort_matrix(), d_tok.astype(BF)).astype(BF)


def call(kernel, outs, *args, smem=0, scratch=(), name=None, flops=0):
    specs = [pl.BlockSpec(memory_space=pltpu.SMEM)] * smem
    specs += [pl.BlockSpec(memory_space=pltpu.VMEM)] * (len(args) - smem)
    return pl.pallas_call(
        kernel,
        out_shape=[jax.ShapeDtypeStruct(shape, dtype) for shape, dtype in outs],
        in_specs=specs,
        out_specs=[pl.BlockSpec(memory_space=pltpu.VMEM)] * len(outs),
        scratch_shapes=scratch,
        compiler_params=pltpu.CompilerParams(vmem_limit_bytes=VMEM_LIMIT),
        cost_estimate=pl.CostEstimate(flops=flops, bytes_accessed=4 << 20, transcendentals=0),
        name=name,
    )(*args)


def swap_seq(block, code):
    return lax.ppermute(block, "seq", [(i, i ^ code) for i in range(16)])


def gather_rows(pack):
    from_y = swap_seq(pack, 2)
    far = jnp.concatenate([pack[64:], from_y[64:]], axis=0)
    far = jnp.concatenate([far, swap_seq(far, 4)], axis=0)
    far = jnp.concatenate([far, swap_seq(far, 12)], axis=0)
    mine = jnp.concatenate([pack[:64], from_y[:64], far], axis=0)
    return mine, swap_seq(mine, 1)


def decode(i):
    dp, seq = i // 16, i % 16
    return [dp // 2, (seq // 2) % 2 * 2 + dp % 2, seq // 4, seq % 2]


def encode(x, y, z, core):
    return (x * 2 + y % 2) * 16 + z * 4 + y // 2 * 2 + core


STEPS = [(n // 2, 3 if n % 2 else 1) for n in range(6)]


def step_route(number):
    turn, code = STEPS[number]
    route = []
    for i in range(128):
        place = decode(i)
        axis = (turn + place[3]) % 3
        place[axis] ^= code
        route.append((i, encode(*place)))
    return route


def step_bit(number, coords, core):
    turn, code = STEPS[number]
    v = jnp.where(core == 0, coords[turn % 3], coords[(turn + 1) % 3])
    return (v >> 1) if code == 3 else ((v + 1) >> 1) & 1


SPLITS = [0, 0, 0, 1, 1, 1]


def sum_everywhere(grads, extra):
    dp = lax.axis_index("dp")
    seq = lax.axis_index("seq")
    core = seq & 1
    coords = [dp >> 1, ((seq >> 1) & 1) * 2 + (dp & 1), seq >> 2]
    core_route = [(i, i ^ 1) for i in range(128)]

    def reduce_step(acc, extra, axis, bit, route):
        half = acc.shape[axis] // 2
        keep = lax.dynamic_slice_in_dim(acc, bit * half, half, axis)
        send = lax.dynamic_slice_in_dim(acc, (1 - bit) * half, half, axis).astype(BF)
        rows = jnp.pad(extra.astype(BF), ((0, 0), (0, send.shape[1] - extra.shape[1])))
        got = lax.ppermute(jnp.concatenate([send, rows], axis=0), AXES, route)
        n = send.shape[0]
        return (
            keep.astype(F32) + got[:n].astype(F32),
            extra + got[n:, : extra.shape[1]].astype(F32),
        )

    acc, extra = reduce_step(grads, extra, 0, core, core_route)
    bits = [step_bit(n, coords, core) for n in range(6)]
    for n in range(6):
        acc, extra = reduce_step(acc, extra, SPLITS[n], bits[n], step_route(n))
    block = acc.astype(BF)
    for n in reversed(range(6)):
        got = lax.ppermute(block, AXES, step_route(n))
        axis = SPLITS[n]
        block = jnp.where(
            bits[n] == 1,
            jnp.concatenate([got, block], axis=axis),
            jnp.concatenate([block, got], axis=axis),
        )
    got = lax.ppermute(block, AXES, core_route)
    block = jnp.where(
        core == 1,
        jnp.concatenate([got, block], axis=0),
        jnp.concatenate([block, got], axis=0),
    ).astype(F32)
    return block, extra


def position_table():
    quarter = D // 4
    frequency = 1.0 / 10000.0 ** (np.arange(quarter) / quarter)
    angle = np.arange(256)[:, None] * frequency[None, :]
    exact_values = np.concatenate([np.sin(angle), np.cos(angle)], axis=1).astype(np.float32)
    parts = []
    rest = exact_values
    for _ in range(3):
        part = rest.astype(jnp.bfloat16)
        parts.append(part)
        rest = rest - part.astype(np.float32)
    return np.concatenate(parts, axis=1)


def per_device(tokens, tile_coords, slide_lengths, norm_gain, norm_bias, w_qkv, w_out, cotangent):
    seq = lax.axis_index("seq").astype(jnp.int32)
    meta = jnp.concatenate([seq[None], slide_lengths[0], jnp.zeros((3,), jnp.int32)])
    gain = norm_gain[None]
    table = jnp.asarray(position_table())
    inp, normed, qkv, d_att, cot, kv_pack, qd_pack = call(
        pre_kernel,
        [((T, D), F32), ((T, D), BF), ((T, 3 * D), BF), ((T, D), BF), ((T, D), BF),
         ((80, 2 * D), BF), ((80, 2 * D), BF)],
        tokens[0], tile_coords[0], table, gain, norm_bias[None], w_qkv, w_out, cotangent[0],
        name="pre",
    )
    kv_a, kv_b = gather_rows(kv_pack)
    o_l, top_l, sum_l = call(
        local_forward_kernel,
        [((T, D), F32), ((T, 128), F32), ((T, 128), F32)],
        meta, qkv, smem=1, name="local_forward",
    )
    qd_a, qd_b = gather_rows(qd_pack)
    att, layer_out, stat, stat_pack, dw_out = call(
        remote_forward_kernel,
        [((T, D), BF), ((T, D), BF), ((T, 128), F32), ((80, 128), F32), ((D, D), BF)],
        meta, qkv, kv_a, kv_b, o_l, top_l, sum_l, inp, d_att, w_out, cot,
        smem=1, name="remote_forward",
    )
    st_a, st_b = gather_rows(stat_pack)
    dq, dk, dv = call(
        query_backward_kernel,
        [((T, D), F32)] * 3,
        meta, qkv, d_att, stat, kv_a, kv_b, smem=1, name="query_backward",
    )
    d_tokens, dw_qkv, vecs = call(
        key_backward_kernel,
        [((T, D), BF), ((D, 3 * D), BF), ((8, D), F32)],
        meta, qkv, qd_a, qd_b, st_a, st_b, dq, dk, dv, inp, normed, gain, w_qkv, cot,
        smem=1, name="key_backward",
        scratch=[pltpu.VMEM((T, D), F32), pltpu.VMEM((T, D), F32)],
    )
    extra = jnp.pad(vecs[:2].reshape(4, 384), ((0, 12), (0, 0)))
    total, extra = sum_everywhere(jnp.concatenate([dw_qkv, dw_out], axis=1), extra)
    vec = extra[:4].reshape(2, D)
    return (
        layer_out[None],
        d_tokens[None],
        total[:, : 3 * D],
        total[:, 3 * D :],
        vec[0],
        vec[1],
    )


def solution(mesh):
    return jax.shard_map(
        per_device,
        mesh=mesh,
        in_specs=(
            P("dp", "seq", None),
            P("dp", None, "seq"),
            P("dp", None),
            P(),
            P(),
            P(),
            P(),
            P("dp", "seq", None),
        ),
        out_specs=(P("dp", "seq", None), P("dp", "seq", None), P(), P(), P(), P()),
        check_vma=False,
    )
```

```python
import functools

import jax
import jax.numpy as jnp
import numpy as np
from jax import lax
from jax.experimental import pallas as pl
from jax.experimental.pallas import tpu as pltpu
from jax.sharding import PartitionSpec as P

HEADS = 16
HD = 48
D = 768
T = 256
SCALE = HD ** (-0.5)
NEG = -1e30
BF = jnp.bfloat16
F32 = jnp.float32
AXES = ("dp", "seq")
WIDE = 384


def iota(shape, dim):
    return lax.broadcasted_iota(jnp.int32, shape, dim)


def tile_of(i):
    return (i >> 6) + ((i >> 4) & 3) * 4 + (i & 15) * 16


def nt(a, b):
    return lax.dot_general(a, b, (((1,), (1,)), ((), ())), preferred_element_type=F32)


def nn(a, b):
    return lax.dot_general(a, b, (((1,), (0,)), ((), ())), preferred_element_type=F32)


def tn(a, b):
    return lax.dot_general(a, b, (((0,), (0,)), ((), ())), preferred_element_type=F32)


def exact(a, b):
    hi = a.astype(BF)
    rest = a - hi.astype(F32)
    mid = rest.astype(BF)
    low = (rest - mid.astype(F32)).astype(BF)
    return nn(hi, b) + nn(mid, b) + nn(low, b)


def sort_matrix():
    return jnp.where(tile_of(iota((T, T), 0)) == iota((T, T), 1), 1.0, 0.0).astype(BF)


def unsort_matrix():
    return jnp.where(iota((T, T), 0) == tile_of(iota((T, T), 1)), 1.0, 0.0).astype(BF)


def span_mask(lo, shape):
    lane = iota(shape, 1)
    return jnp.where((lane >= lo) & (lane < lo + HD), 1.0, 0.0)


def head_window(h):
    start = HD * h // 128 * 128
    width = 128 if HD * h - start + HD <= 128 else 256
    return start, width


def head_mask(h):
    start, width = head_window(h)
    return span_mask(HD * h - start, (1, width)).astype(BF)


def group_window(g):
    return 192 * g // 128 * 128


def group_mask(g):
    lo = 192 * g - group_window(g) + HD * (iota((T, 256), 0) >> 6)
    return span_mask(lo, (T, 256)).astype(BF)


def far_mask():
    row = iota((T, D), 0)
    lo = HD * ((row >> 6) + 4 * ((row >> 4) & 3))
    return span_mask(lo, (T, D)).astype(BF)


def slide_of(meta, pos):
    end = meta[1]
    out = jnp.where(pos >= end, 1, 0)
    for n in range(2, 5):
        end = end + meta[n]
        out = out + jnp.where(pos >= end, 1, 0)
    return out


def row_ids(meta):
    return slide_of(meta, meta[0] * T + tile_of(iota((T, 1), 0)))


def bias_of(meta, pos):
    return jnp.where(row_ids(meta) == slide_of(meta, pos), 0.0, NEG)


def local_bias(meta):
    return bias_of(meta, meta[0] * T + tile_of(iota((1, T), 1)))


def mid_bias(meta):
    t = iota((T, T), 1)
    slot = t >> 6
    dev = meta[0] ^ (((slot & 1) << 1) | (slot >> 1))
    pos = dev * T + ((t >> 4) & 3) * 4 + (t & 15) * 16 + (iota((T, T), 0) >> 6)
    return bias_of(meta, pos)


def far_bias(meta):
    t = iota((T, T), 1)
    s = t >> 4
    code = ((s & 1) << 1) ^ (((s >> 1) & 1) << 2) ^ (((s >> 2) & 1) * 12) ^ (s >> 3)
    row = iota((T, T), 0)
    pos = (meta[0] ^ code) * T + (t & 15) * 16 + (row >> 6) + 4 * ((row >> 4) & 3)
    return bias_of(meta, pos)


def far_head(b):
    return b // 4 + 4 * (b % 4)


def fold_mid(x, masks):
    out = x[0:64] * masks[0]
    for c in range(1, 4):
        out = out + x[64 * c : 64 * c + 64] * masks[c]
    return out


def fold_far(x, masks):
    out = x[0:16] * masks[0]
    for b in range(1, 16):
        out = out + x[16 * b : 16 * b + 16] * masks[far_head(b)]
    return out


def pack_rows(x, head_masks):
    mids = [
        head_masks[c] + head_masks[4 + c] + head_masks[8 + c] + head_masks[12 + c]
        for c in range(4)
    ]
    return jnp.concatenate([fold_mid(x, mids), fold_far(x, head_masks)], axis=0)


def norm_parts(inputs):
    mean = jnp.mean(inputs, axis=1, keepdims=True)
    centred = inputs - mean
    var = jnp.mean(centred * centred, axis=1, keepdims=True)
    inv_std = lax.rsqrt(var + 1e-05)
    return centred * inv_std, inv_std


def pack_masks():
    return [span_mask(HD * h, (1, D)).astype(BF) for h in range(HEADS)]


def key_kernel(tok, coords, table, gain, bias, w_k, w_v, inp_o, norm_o, kv_o, pack_o):
    sort = sort_matrix()
    tok_s = nn(sort, tok[...])
    grid = iota((T, T), 0)
    parts = []
    for axis in range(2):
        hot = jnp.where(grid == coords[axis : axis + 1, :], 1.0, 0.0).astype(BF)
        hot = nt(sort, hot).astype(BF)
        found = nn(hot, table[...])
        parts.append(found[:, :384] + found[:, 384:768] + found[:, 768:])
    inputs = tok_s + jnp.concatenate(parts, axis=1)
    inp_o[...] = inputs
    unit, _ = norm_parts(inputs)
    normed = (unit * gain[...].reshape(1, D) + bias[...].reshape(1, D)).astype(BF)
    norm_o[...] = normed
    masks = pack_masks()
    for n, weight in enumerate((w_k, w_v)):
        part = nn(normed, weight[...]).astype(BF)
        kv_o[:, D * n : D * (n + 1)] = part
        pack_o[:, D * n : D * (n + 1)] = pack_rows(part, masks)


def query_kernel(normed, w_qkv, w_out, cot, q_o, da_o, cot_o, pack_o):
    cot_s = nn(sort_matrix(), cot[...]).astype(BF)
    cot_o[...] = cot_s
    q = nn(normed[...], w_qkv[...]).astype(BF)
    q_o[...] = q
    d_att = nt(cot_s, w_out[...]).astype(BF)
    da_o[...] = d_att
    masks = pack_masks()
    pack_o[:, :D] = pack_rows(q, masks)
    pack_o[:, D:] = pack_rows(d_att, masks)


def soft(scores):
    top = jnp.max(scores, axis=1, keepdims=True)
    shares = jnp.exp(scores - top)
    return top, jnp.sum(shares, axis=1, keepdims=True), shares.astype(BF)


def local_forward_kernel(meta, q_r, kv, o_o, top_o, sum_o, *, first):
    bias = local_bias(meta)
    o_o[...] = jnp.zeros_like(o_o)
    lane = iota((T, 128), 1)
    tops = jnp.full((T, 128), NEG, F32)
    sums = jnp.zeros((T, 128), F32)
    base = HD * first
    for h in range(first, first + 8):
        s, w = head_window(h)
        mask = head_mask(h)
        scores = nt(q_r[:, s : s + w] * mask, kv[:, s : s + w]) * SCALE + bias
        top, total, shares = soft(scores)
        tops = jnp.where(lane == h, top, tops)
        sums = jnp.where(lane == h, total, sums)
        o_o[:, s - base : s - base + w] += nn(shares, kv[:, D + s : D + s + w] * mask)
    top_o[...] = tops
    sum_o[...] = sums


def mid_rows(got, lo, width):
    return jnp.concatenate([got[0][:128, lo : lo + width], got[2][:128, lo : lo + width]], axis=0)


def far_rows(got, lo, width):
    at = slice(lo, lo + width)
    return jnp.concatenate([got[0][128:, at], got[1][:, at], got[2][128:, at], got[3][:, at]], axis=0)


def expand_matrix():
    head = iota((128, D), 0)
    lane = iota((128, D), 1)
    return jnp.where((lane >= head * HD) & (lane < head * HD + HD), 1.0, 0.0).astype(BF)


def gather_matrix():
    lane = iota((D, 128), 0)
    head = iota((D, 128), 1)
    return jnp.where((lane >= head * HD) & (lane < head * HD + HD), 1.0, 0.0).astype(BF)


def remote_forward_kernel(meta, q_r, kv_a1, kv_a2, kv_b1, kv_b2, o_1, top_1, sum_1, o_2, top_2, sum_2, d_att,
                          pack, att_o, stat_o, send_o):
    lane = iota((T, 128), 1)
    row = iota((T, 128), 0)
    got = (kv_a1, kv_a2, kv_b1, kv_b2)
    top_l = jnp.where(lane < 8, top_1[...], top_2[...])
    sum_l = jnp.where(lane < 8, sum_1[...], sum_2[...])
    tops_m = jnp.full((T, 128), NEG, F32)
    sums_m = jnp.zeros((T, 128), F32)
    mid = mid_bias(meta)
    mid_parts = []
    for g in range(4):
        s = group_window(g)
        mask = group_mask(g)
        q = q_r[:, s : s + 256] * mask
        scores = nt(q, mid_rows(got, s, 256)) * SCALE + mid
        top, total, shares = soft(scores)
        here = lane == 4 * g + (row >> 6)
        tops_m = jnp.where(here, top, tops_m)
        sums_m = jnp.where(here, total, sums_m)
        mid_parts.append(nn(shares, mid_rows(got, D + s, 256)))
    mask = far_mask()
    scores = nt(q_r[...] * mask, far_rows(got, 0, D)) * SCALE + far_bias(meta)
    top, total, shares = soft(scores)
    far_part = nn(shares, far_rows(got, D, D))
    here = lane == (row >> 6) + 4 * ((row >> 4) & 3)
    tops_f = jnp.where(here, top, NEG)
    sums_f = jnp.where(here, total, 0.0)
    highest = jnp.maximum(jnp.maximum(top_l, tops_m), tops_f)
    f_l = jnp.exp(top_l - highest)
    f_m = jnp.exp(tops_m - highest)
    f_f = jnp.exp(tops_f - highest)
    totals = f_l * sum_l + f_m * sums_m + f_f * sums_f
    totals = jnp.where(lane < HEADS, totals, 1.0)
    inverse = 1.0 / totals
    lse = highest + jnp.log(totals)
    w_m = f_m * inverse
    o_l = jnp.concatenate([o_1[...], o_2[...]], axis=1)
    att = o_l * exact(f_l * inverse, expand_matrix())
    w_f = jnp.sum(jnp.where(here, f_f * inverse, 0.0), axis=1, keepdims=True)
    att = att + far_part * w_f * mask.astype(F32)
    acc = [att[:, 128 * n : 128 * n + 128] for n in range(6)]
    for g in range(4):
        n = group_window(g) // 128
        w_g = jnp.sum(jnp.where(lane == 4 * g + (row >> 6), w_m, 0.0), axis=1, keepdims=True)
        add = mid_parts[g] * w_g * group_mask(g).astype(F32)
        acc[n] = acc[n] + add[:, :128]
        acc[n + 1] = acc[n + 1] + add[:, 128:]
    att = jnp.concatenate(acc, axis=1).astype(BF)
    att_o[...] = att
    prod = d_att[...].astype(F32) * att.astype(F32)
    delta = exact(prod, gather_matrix())
    stat = jnp.where(lane < HEADS, lse, pltpu.roll(delta, HEADS, 1))
    stat = jnp.where(lane < 2 * HEADS, stat, 0.0)
    stat_o[...] = stat
    one = iota((1, 128), 1)
    send_o[:, : 2 * D] = pack[...]
    mids = fold_mid(stat, [jnp.where((one & 3) == c, 1.0, 0.0) for c in range(4)])
    fars = fold_far(stat, [jnp.where((one & 15) == h, 1.0, 0.0) for h in range(HEADS)])
    send_o[:, 2 * D :] = three_parts(jnp.concatenate([mids, fars], axis=0))


def three_parts(x):
    lane = iota(x.shape, 1)
    hi = x.astype(BF).astype(F32)
    mid = (x - hi).astype(BF).astype(F32)
    low = x - hi - mid
    parts = jnp.where(lane < 64, pltpu.roll(mid, 32, 1), pltpu.roll(low, 64, 1))
    return jnp.where(lane < 32, hi, parts).astype(BF)


def out_kernel(att, inp, w_out, out_o):
    layer = (inp[...] + nn(att[...], w_out[...])).astype(BF)
    out_o[...] = nn(unsort_matrix(), layer).astype(BF)


def pick_mid_column(stat, col):
    return jnp.concatenate(
        [stat[64 * c : 64 * c + 64, col + c : col + c + 1] for c in range(4)], axis=0
    )


def pick_far_column(stat, col):
    return jnp.concatenate(
        [
            stat[16 * b : 16 * b + 16, col + far_head(b) : col + far_head(b) + 1]
            for b in range(16)
        ],
        axis=0,
    )


def local_backward_kernel(meta, q_r, kv, d_att, stat, dq_o, dk_o, dv_o, *, first):
    bias = local_bias(meta)
    dq_o[...] = jnp.zeros_like(dq_o)
    dk_o[...] = jnp.zeros_like(dk_o)
    dv_o[...] = jnp.zeros_like(dv_o)
    base = HD * first
    for h in range(first, first + 8):
        s, w = head_window(h)
        t = s - base
        mask = head_mask(h)
        q = q_r[:, s : s + w] * mask
        k = kv[:, s : s + w] * mask
        da = d_att[:, s : s + w] * mask
        scores = nt(q, k) * SCALE + bias
        shares = jnp.exp(scores - stat[:, h : h + 1])
        d_shares = nt(da, kv[:, D + s : D + s + w])
        ds = (shares * (d_shares - stat[:, HEADS + h : HEADS + h + 1])).astype(BF)
        dq_o[:, t : t + w] += nn(ds, k)
        dk_o[:, t : t + w] += tn(ds, q)
        dv_o[:, t : t + w] += tn(shares.astype(BF), da)


def query_backward_kernel(meta, q_r, d_att, stat, kv_a1, kv_a2, kv_b1, kv_b2, dq_o):
    got = (kv_a1, kv_a2, kv_b1, kv_b2)
    dq_o[...] = jnp.zeros_like(dq_o)
    mid = mid_bias(meta)
    for g in range(4):
        s = group_window(g)
        mask = group_mask(g)
        k = mid_rows(got, s, 256)
        scores = nt(q_r[:, s : s + 256] * mask, k) * SCALE + mid
        shares = jnp.exp(scores - pick_mid_column(stat, 4 * g))
        d_shares = nt(d_att[:, s : s + 256] * mask, mid_rows(got, D + s, 256))
        ds = (shares * (d_shares - pick_mid_column(stat, HEADS + 4 * g))).astype(BF)
        dq_o[:, s : s + 256] += nn(ds, k) * mask.astype(F32)
    mask = far_mask()
    k = far_rows(got, 0, D)
    scores = nt(q_r[...] * mask, k) * SCALE + far_bias(meta)
    shares = jnp.exp(scores - pick_far_column(stat, 0))
    d_shares = nt(d_att[...] * mask, far_rows(got, D, D))
    ds = (shares * (d_shares - pick_far_column(stat, HEADS))).astype(BF)
    dq_o[...] += nn(ds, k) * mask.astype(F32)


def spread_mid(stat_t, row):
    return jnp.concatenate(
        [jnp.broadcast_to(stat_t[row + c : row + c + 1, :], (64, T)) for c in range(4)], axis=0
    )


def spread_far(stat_t, row):
    return jnp.concatenate(
        [
            jnp.broadcast_to(stat_t[row + far_head(b) : row + far_head(b) + 1, :], (16, T))
            for b in range(16)
        ],
        axis=0,
    )


def joined_stats(rows):
    x = rows.astype(F32).T
    return x[:32] + (x[32:64] + x[64:96])


def key_backward_kernel(meta, kv, qd_a1, qd_a2, qd_b1, qd_b2, dq_r, dq_1, dk_1, dv_1, dq_2, dk_2, dv_2, cot,
                        all_o, kept_o, sent_o, dk_s, dv_s):
    got = (qd_a1, qd_a2, qd_b1, qd_b2)
    half = D // 2
    dk_s[:, :half] = dk_1[...]
    dk_s[:, half:] = dk_2[...]
    dv_s[:, :half] = dv_1[...]
    dv_s[:, half:] = dv_2[...]
    stat_t = joined_stats(mid_rows(got, 2 * D, 128))
    mid = mid_bias(meta)
    for g in range(4):
        s = group_window(g)
        mask = group_mask(g)
        mask_f = mask.astype(F32)
        q = mid_rows(got, s, 256)
        da = mid_rows(got, D + s, 256)
        scores = nt(kv[:, s : s + 256] * mask, q) * SCALE + mid
        shares = jnp.exp(scores - spread_mid(stat_t, 4 * g))
        d_shares = nt(kv[:, D + s : D + s + 256] * mask, da)
        ds = (shares * (d_shares - spread_mid(stat_t, HEADS + 4 * g))).astype(BF)
        dk_s[:, s : s + 256] += nn(ds, q) * mask_f
        dv_s[:, s : s + 256] += nn(shares.astype(BF), da) * mask_f
    stat_t = joined_stats(far_rows(got, 2 * D, 128))
    mask = far_mask()
    mask_f = mask.astype(F32)
    q = far_rows(got, 0, D)
    da = far_rows(got, D, D)
    scores = nt(kv[:, :D] * mask, q) * SCALE + far_bias(meta)
    shares = jnp.exp(scores - spread_far(stat_t, 0))
    d_shares = nt(kv[:, D:] * mask, da)
    ds = (shares * (d_shares - spread_far(stat_t, HEADS))).astype(BF)
    dk_s[...] += nn(ds, q) * mask_f
    dv_s[...] += nn(shares.astype(BF), da) * mask_f
    dq = jnp.concatenate([dq_1[...], dq_2[...]], axis=1) + dq_r[...]
    d_q = (dq * SCALE).astype(BF)
    d_k = (dk_s[...] * SCALE).astype(BF)
    d_v = dv_s[...].astype(BF)
    all_o[:, :D] = d_q
    all_o[:, D : 2 * D] = d_k
    all_o[:, 2 * D :] = d_v
    first = meta[5] == 0
    kept_o[:, :D] = jnp.where(first, d_q, d_v)
    kept_o[:, D:] = jnp.where(first, d_k, cot[...])
    sent_o[:, :D] = jnp.where(first, d_v, d_q)
    sent_o[:, D:] = jnp.where(first, cot[...], d_k)


def weight_grad_kernel(meta, own, other, norm_a, norm_b, att_a, att_b, keep_o, s1, s2, s3, left):
    left[0] = jnp.concatenate([norm_a[...], norm_b[...]], axis=0).T
    left[1] = left[0]

    @pl.when(meta[5] == 1)
    def _():
        left[1] = jnp.concatenate([att_a[...], att_b[...]], axis=0).T

    for d, out in ((2, s2), (1, s1), (3, s3), (0, keep_o)):
        j = (meta[6] + d) & 3
        cols = pl.ds(pl.multiple_of(j * WIDE, 128), WIDE)
        right = jnp.concatenate([own[:, cols], other[:, cols]], axis=0)
        out[...] = nn(left[j >> 1], right).astype(out.dtype)


def token_grad_kernel(d_qkv, w_qkv, inp, gain, cot, tok_o, ext_o):
    d_normed = nt(d_qkv[...], w_qkv[...])
    unit, inv_std = norm_parts(inp[...])
    d_gain = jnp.sum(d_normed * unit, axis=0, keepdims=True)
    d_bias = jnp.sum(d_normed, axis=0, keepdims=True)
    ext_o[...] = two_parts(jnp.concatenate(
        [d_gain[:, :WIDE], d_gain[:, WIDE:], d_bias[:, :WIDE], d_bias[:, WIDE:],
         jnp.zeros((4, WIDE), F32)], axis=0))
    d_unit = d_normed * gain[...].reshape(1, D)
    mean_a = jnp.mean(d_unit, axis=1, keepdims=True)
    mean_b = jnp.mean(d_unit * unit, axis=1, keepdims=True)
    d_tok = cot[...].astype(F32) + inv_std * (d_unit - mean_a - unit * mean_b)
    tok_o[...] = nn(unsort_matrix(), d_tok.astype(BF)).astype(BF)


def two_parts(ext):
    hi = ext.astype(BF)
    return jnp.concatenate([hi, (ext - hi.astype(F32)).astype(BF)], axis=0)


def whole_of(rows):
    return rows[:8].astype(F32) + rows[8:].astype(F32)


def ring_total(meta, slot, own, got, pad):
    pad[meta[slot]] = own
    for d, piece in enumerate(got, 1):
        pad[(meta[slot] - d) & 3] = piece
    return (pad[0] + pad[1]) + (pad[2] + pad[3])


def add_a_kernel(meta, keep, r1, r2, r3, ext, keep_o, s1, s2, s3):
    rows = D // 4
    for d, out in ((2, s2), (1, s1), (3, s3), (0, keep_o)):
        at = pl.ds(pl.multiple_of(((meta[7] + d) & 3) * rows, 16), rows)
        total = keep[at, :] + (r1[at, :].astype(F32) + r2[at, :].astype(F32) + r3[at, :].astype(F32))
        if d == 0:
            out[...] = total
        else:
            out[:rows] = total.astype(BF)
            out[rows:] = ext[...]


def add_b_kernel(meta, keep, r1, r2, r3, ext, out, pad):
    rows = D // 4
    got = (r1, r2, r3)
    total = keep[...]
    for r in got:
        total = total + r[:rows].astype(F32)
    out[:rows] = total.astype(BF)
    sums = ring_total(meta, 7, whole_of(ext[...]), [whole_of(r[rows:]) for r in got], pad)
    out[rows:] = two_parts(sums)


def add_c_kernel(meta, own, r1, r2, r3, out, ext_o, pad, ext_pad):
    rows = D // 4
    got = (r1, r2, r3)
    total = ring_total(meta, 8, own[:rows].astype(F32), [r[:rows].astype(F32) for r in got], pad)
    out[...] = total.astype(BF)
    sums = ring_total(meta, 8, whole_of(own[rows:]), [whole_of(r[rows:]) for r in got], ext_pad)
    ext_o[...] = two_parts(sums)


def merge_kernel(meta, own, r1, r2, r3, ext, out):
    rows = D // 4
    for d, piece in enumerate((own, r1, r2, r3)):
        at = pl.ds(pl.multiple_of(((meta[7] - d) & 3) * rows, 16), rows)
        out[at, :] = piece[...]
    out[D:] = ext[...]


def finish_kernel(meta, *refs, turns, first, last):
    count = 2 * len(turns)
    pieces, refs = refs[:count], refs[count:]
    if last:
        tails, refs = refs[:8], refs[8:]
    if not first:
        refs = refs[2:]
    qkv_o, out_o, *refs = refs
    if last:
        gain_o, bias_o, *refs = refs
    wide, sems, *refs = refs
    for n, piece in enumerate(pieces):
        half = n // len(turns)
        chunk = (meta[5] ^ half) * 4 + ((meta[6 if half == 0 else 9] - turns[n % len(turns)]) & 3)
        wide[n] = piece[...].astype(F32)

        @pl.when(chunk < 6)
        def _(n=n, chunk=chunk):
            at = pl.ds(pl.multiple_of(chunk * WIDE, 128), WIDE)
            pltpu.make_async_copy(wide.at[n], qkv_o.at[:, at], sems.at[n]).start()

        @pl.when(chunk >= 6)
        def _(n=n, chunk=chunk):
            at = pl.ds(pl.multiple_of((chunk - 6) * WIDE, 128), WIDE)
            pltpu.make_async_copy(wide.at[n], out_o.at[:, at], sems.at[n]).start()

    if last:
        pad = refs[0]
        for n, tail in enumerate(tails):
            half = n // 4
            place = (meta[6 if half == 0 else 9] - n % 4) & 3
            pad[(meta[5] ^ half) * 4 + place] = whole_of(tail[...])
        total = pad[0]
        for n in range(1, 8):
            total = total + pad[n]
        gain_o[...] = jnp.concatenate([total[0:1], total[1:2]], axis=1).reshape(D)
        bias_o[...] = jnp.concatenate([total[2:3], total[3:4]], axis=1).reshape(D)
    for n in range(count):
        pltpu.make_async_copy(wide.at[n], qkv_o.at[:, pl.ds(0, WIDE)], sems.at[n]).wait()


def finish(meta, pieces, turns, tails, outs):
    first, last = outs is None, tails is not None
    smem = pl.BlockSpec(memory_space=pltpu.SMEM)
    anywhere = pl.BlockSpec(memory_space=pl.ANY)
    head = pl.BlockSpec((D, WIDE), lambda i: (0, 0))
    tail = pl.BlockSpec((16, WIDE), lambda i: (D // 16, 0))
    args = [meta, *pieces] + (list(tails) if last else [])
    in_specs = [smem] + [head] * len(pieces) + ([tail] * 8 if last else [])
    aliases = {}
    if not first:
        aliases = {len(args): 0, len(args) + 1: 1}
        args += list(outs)
        in_specs += [anywhere] * 2
    out_shape = [jax.ShapeDtypeStruct((D, 3 * D), F32), jax.ShapeDtypeStruct((D, D), F32)]
    out_specs = [anywhere] * 2
    scratch = [pltpu.VMEM((len(pieces), D, WIDE), F32), pltpu.SemaphoreType.DMA((len(pieces),))]
    if last:
        out_shape += [jax.ShapeDtypeStruct((D,), F32)] * 2
        out_specs += [pl.BlockSpec((D,), lambda i: (0,))] * 2
        scratch += [pltpu.VMEM((8, 8, WIDE), F32)]
    return pl.pallas_call(
        functools.partial(finish_kernel, turns=turns, first=first, last=last),
        grid=(1,),
        in_specs=in_specs,
        out_specs=out_specs,
        out_shape=out_shape,
        scratch_shapes=scratch,
        input_output_aliases=aliases,
        compiler_params=pltpu.CompilerParams(vmem_limit_bytes=24 << 20),
        name="finish",
    )(*args)


def call(kernel, outs, *args, smem=0, scratch=(), name=None, limit=24, windows=None):
    specs = [pl.BlockSpec(memory_space=pltpu.SMEM)] * smem
    specs += [pl.BlockSpec(memory_space=pltpu.VMEM)] * (len(args) - smem)
    for n, (shape, index) in (windows or {}).items():
        specs[n] = pl.BlockSpec(shape, lambda i, index=index: index)
    return pl.pallas_call(
        kernel,
        grid=(1,) if windows else (),
        out_shape=[jax.ShapeDtypeStruct(shape, dtype) for shape, dtype in outs],
        in_specs=specs,
        out_specs=[pl.BlockSpec(memory_space=pltpu.VMEM)] * len(outs),
        scratch_shapes=scratch,
        compiler_params=pltpu.CompilerParams(vmem_limit_bytes=limit << 20),
        name=name,
    )(*args)


def swap_seq(block, code):
    return lax.ppermute(block, "seq", [(i, i ^ code) for i in range(16)])


def after(*values):
    return lax.optimization_barrier(values)


def join(*blocks):
    return jnp.concatenate(blocks, axis=0)


def decode(i):
    dp, seq = i // 16, i % 16
    return [dp // 2, (seq // 2) % 2 * 2 + dp % 2, seq // 4, seq % 2]


def encode(x, y, z, core):
    return (x * 2 + y % 2) * 16 + z * 4 + y // 2 * 2 + core


def ring_route(stage, d):
    route = []
    for i in range(128):
        place = decode(i)
        axis = (stage + place[3]) % 3
        place[axis] = (place[axis] + d) % 4
        route.append((i, encode(*place)))
    return route


def ring_send(blocks, stage):
    got = {d: lax.ppermute(blocks[d - 1], AXES, ring_route(stage, d)) for d in (2, 1, 3)}
    return got[1], got[2], got[3]


def place_meta(lengths):
    dp = lax.axis_index("dp").astype(jnp.int32)
    seq = lax.axis_index("seq").astype(jnp.int32)
    core = seq & 1
    coords = [dp >> 1, (seq & 2) + (dp & 1), seq >> 2]
    turns = [jnp.where(core == 0, coords[n], coords[(n + 1) % 3]) for n in range(3)]
    other = jnp.where(core == 0, coords[1], coords[0])
    values = jnp.stack([core] + turns + [other])
    return jnp.concatenate([seq[None], lengths, values, jnp.zeros((6,), jnp.int32)])


def sum_everywhere(meta, keep, sends, ext, beside):
    cut = D // 4
    pad = pltpu.VMEM((4, 8, WIDE), F32)
    got = ring_send(sends, 0)
    *got, _ = after(*got, beside)
    keep, *sends = call(
        add_a_kernel,
        [((cut, WIDE), F32)] + [((cut + 16, WIDE), BF)] * 3,
        meta, keep, *got, ext, smem=1, name="add_a",
    )
    got = ring_send(sends, 1)
    block = call(
        add_b_kernel, [((cut + 16, WIDE), BF)],
        meta, keep, *got, ext, smem=1, name="add_b", scratch=[pad],
    )[0]
    got = ring_send([block] * 3, 2)
    block, ext = call(
        add_c_kernel, [((cut, WIDE), BF), ((16, WIDE), BF)],
        meta, block, *got, smem=1, name="add_c",
        scratch=[pltpu.VMEM((4, cut, WIDE), F32), pad],
    )
    got = ring_send([block] * 3, 1)
    block = call(
        merge_kernel, [((D + 16, WIDE), BF)],
        meta, block, *got, ext, smem=1, name="merge_b",
    )[0]
    ring = {d: lax.ppermute(block, AXES, ring_route(0, d)) for d in (1, 3, 2)}
    ring[0] = block
    twin = {0: swap_seq(block, 1)}
    outs = finish(meta, [ring[0], twin[0]], (0,), None, None)
    ring[1], ring[3], *outs = after(ring[1], ring[3], *outs)
    twin[1], twin[3] = swap_seq(ring[1], 1), swap_seq(ring[3], 1)
    outs = finish(meta, [ring[1], ring[3], twin[1], twin[3]], (1, 3), None, outs)
    ring[2], *outs = after(ring[2], *outs)
    twin[2] = swap_seq(ring[2], 1)
    tails = [half[d] for half in (ring, twin) for d in range(4)]
    return finish(meta, [ring[2], twin[2]], (2,), tails, outs)


def position_table():
    quarter = D // 4
    frequency = 1.0 / 10000.0 ** (np.arange(quarter) / quarter)
    angle = np.arange(256)[:, None] * frequency[None, :]
    exact_values = np.concatenate([np.sin(angle), np.cos(angle)], axis=1).astype(np.float32)
    parts = []
    rest = exact_values
    for _ in range(3):
        part = rest.astype(jnp.bfloat16)
        parts.append(part)
        rest = rest - part.astype(np.float32)
    return np.concatenate(parts, axis=1)


def per_device(tokens, tile_coords, slide_lengths, norm_gain, norm_bias, w_qkv, w_out, cotangent):
    meta = place_meta(slide_lengths[0])
    table = jnp.asarray(position_table())
    inp, normed, kv, kv_pack = call(
        key_kernel,
        [((T, D), F32), ((T, D), BF), ((T, 2 * D), BF), ((80, 2 * D), BF)],
        tokens[0], tile_coords[0], table, norm_gain, norm_bias, w_qkv, w_qkv, name="keys",
        windows={5: ((D, D), (0, 1)), 6: ((D, D), (0, 2))},
    )
    from_y = swap_seq(kv_pack, 2)
    norm_b = swap_seq(normed, 1)
    q, d_att, cot, qd_pack = call(
        query_kernel,
        [((T, D), BF), ((T, D), BF), ((T, D), BF), ((80, 2 * D), BF)],
        normed, w_qkv, w_out, cotangent[0], name="queries",
        windows={1: ((D, D), (0, 0))},
    )
    from_y, q, norm_b = after(from_y, q, norm_b)
    far = join(kv_pack[64:], from_y[64:])
    from_z = swap_seq(far, 4)
    o_1, top_1, sum_1 = call(
        functools.partial(local_forward_kernel, first=0),
        [((T, D // 2), F32), ((T, 128), F32), ((T, 128), F32)],
        meta, q, kv, smem=1, name="local_forward",
    )
    from_z, o_1 = after(from_z, o_1)
    part = join(kv_pack[:64], from_y[:64], far, from_z)
    from_z = swap_seq(part[128:], 12)
    part, q = after(part, q)
    o_2, top_2, sum_2 = call(
        functools.partial(local_forward_kernel, first=8),
        [((T, D // 2), F32), ((T, 128), F32), ((T, 128), F32)],
        meta, q, kv, smem=1, name="local_forward",
    )
    twin = swap_seq(part, 1)
    from_z, twin, o_2 = after(from_z, twin, o_2)
    got_kv = (part, from_z, twin, swap_seq(from_z, 1))
    att, stat, pack = call(
        remote_forward_kernel,
        [((T, D), BF), ((T, 128), F32), ((80, 2 * D + 128), BF)],
        meta, q, *got_kv, o_1, top_1, sum_1, o_2, top_2, sum_2, d_att, qd_pack,
        smem=1, name="remote_forward",
    )
    from_y = swap_seq(pack, 2)
    att_b = swap_seq(att, 1)
    grads_1 = call(
        functools.partial(local_backward_kernel, first=0),
        [((T, D // 2), F32)] * 3,
        meta, q, kv, d_att, stat, smem=1, name="local_backward",
    )
    from_y, att_b, *grads_1 = after(from_y, att_b, *grads_1)
    far = join(pack[64:], from_y[64:])
    from_z = swap_seq(far, 4)
    far, q = after(far, q)
    grads_2 = call(
        functools.partial(local_backward_kernel, first=8),
        [((T, D // 2), F32)] * 3,
        meta, q, kv, d_att, stat, smem=1, name="local_backward",
    )
    from_z, *grads_2 = after(from_z, *grads_2)
    part = join(pack[:64], from_y[:64], far, from_z)
    from_z = swap_seq(part[128:], 12)
    part, q = after(part, q)
    dq_r = call(
        query_backward_kernel, [((T, D), F32)],
        meta, q, d_att, stat, *got_kv, smem=1, name="query_backward",
    )[0]
    twin = swap_seq(part, 1)
    from_z, twin, dq_r = after(from_z, twin, dq_r)
    d_qkv, own, sent = call(
        key_backward_kernel,
        [((T, 3 * D), BF), ((T, 2 * D), BF), ((T, 2 * D), BF)],
        meta, kv, part, from_z, twin, swap_seq(from_z, 1), dq_r, *grads_1, *grads_2, cot,
        smem=1, name="key_backward",
        scratch=[pltpu.VMEM((T, D), F32), pltpu.VMEM((T, D), F32)],
    )
    keep, *sends = call(
        weight_grad_kernel,
        [((D, WIDE), F32)] + [((D, WIDE), BF)] * 3,
        meta, own, swap_seq(sent, 1), normed, norm_b, att, att_b,
        smem=1, name="weight_grad",
        scratch=[pltpu.VMEM((2, D, 2 * T), BF)],
    )
    d_tokens, ext = call(
        token_grad_kernel,
        [((T, D), BF), ((16, WIDE), BF)],
        d_qkv, w_qkv, inp, norm_gain, cot, name="token_grad",
    )
    att, _ = after(att, keep)
    layer_out = call(out_kernel, [((T, D), BF)], att, inp, w_out, name="layer_out")[0]
    dw_qkv, dw_out, d_gain, d_bias = sum_everywhere(meta, keep, sends, ext, layer_out)
    return (
        layer_out[None],
        d_tokens[None],
        dw_qkv,
        dw_out,
        d_gain,
        d_bias,
    )


def solution(mesh):
    return jax.shard_map(
        per_device,
        mesh=mesh,
        in_specs=(
            P("dp", "seq", None),
            P("dp", None, "seq"),
            P("dp", None),
            P(),
            P(),
            P(),
            P(),
            P("dp", "seq", None),
        ),
        out_specs=(P("dp", "seq", None), P("dp", "seq", None), P(), P(), P(), P()),
        check_vma=False,
    )
```

```python
import functools

import jax
import jax.numpy as jnp
import numpy as np
from jax import lax
from jax.experimental import pallas as pl
from jax.experimental.pallas import tpu as pltpu
from jax.sharding import PartitionSpec as P

HEADS = 16
HD = 48
D = 768
T = 256
SCALE = HD ** (-0.5)
NEG = -1e30
BF = jnp.bfloat16
F32 = jnp.float32
AXES = ("dp", "seq")
WIDE = 384


def iota(shape, dim):
    return lax.broadcasted_iota(jnp.int32, shape, dim)


def tile_of(i):
    return (i >> 6) + ((i >> 4) & 3) * 4 + (i & 15) * 16


def nt(a, b):
    return lax.dot_general(a, b, (((1,), (1,)), ((), ())), preferred_element_type=F32)


def nn(a, b):
    return lax.dot_general(a, b, (((1,), (0,)), ((), ())), preferred_element_type=F32)


def tn(a, b):
    return lax.dot_general(a, b, (((0,), (0,)), ((), ())), preferred_element_type=F32)


def exact(a, b):
    hi = a.astype(BF)
    rest = a - hi.astype(F32)
    mid = rest.astype(BF)
    low = (rest - mid.astype(F32)).astype(BF)
    return nn(hi, b) + nn(mid, b) + nn(low, b)


def sort_matrix():
    return jnp.where(tile_of(iota((T, T), 0)) == iota((T, T), 1), 1.0, 0.0).astype(BF)


def unsort_matrix():
    return jnp.where(iota((T, T), 0) == tile_of(iota((T, T), 1)), 1.0, 0.0).astype(BF)


def span_mask(lo, shape):
    lane = iota(shape, 1)
    return jnp.where((lane >= lo) & (lane < lo + HD), 1.0, 0.0)


def head_window(h):
    start = HD * h // 128 * 128
    width = 128 if HD * h - start + HD <= 128 else 256
    return start, width


def head_mask(h):
    start, width = head_window(h)
    return span_mask(HD * h - start, (1, width)).astype(BF)


def group_window(g):
    return 192 * g // 128 * 128


def group_mask(g):
    lo = 192 * g - group_window(g) + HD * (iota((T, 256), 0) >> 6)
    return span_mask(lo, (T, 256)).astype(BF)


def far_mask():
    row = iota((T, D), 0)
    lo = HD * ((row >> 6) + 4 * ((row >> 4) & 3))
    return span_mask(lo, (T, D)).astype(BF)


def slide_of(meta, pos):
    end = meta[1]
    out = jnp.where(pos >= end, 1, 0)
    for n in range(2, 5):
        end = end + meta[n]
        out = out + jnp.where(pos >= end, 1, 0)
    return out


def row_ids(meta):
    return slide_of(meta, meta[0] * T + tile_of(iota((T, 1), 0)))


def bias_of(meta, pos):
    return jnp.where(row_ids(meta) == slide_of(meta, pos), 0.0, NEG)


def local_bias(meta):
    return bias_of(meta, meta[0] * T + tile_of(iota((1, T), 1)))


def mid_bias(meta):
    t = iota((T, T), 1)
    slot = t >> 6
    dev = meta[0] ^ (((slot & 1) << 1) | (slot >> 1))
    pos = dev * T + ((t >> 4) & 3) * 4 + (t & 15) * 16 + (iota((T, T), 0) >> 6)
    return bias_of(meta, pos)


def far_bias(meta):
    t = iota((T, T), 1)
    s = t >> 4
    place = (((meta[0] >> 2) - (s >> 1)) & 3) * 4 + ((meta[0] & 3) ^ ((s & 1) << 1) ^ (s >> 3))
    row = iota((T, T), 0)
    pos = place * T + (t & 15) * 16 + (row >> 6) + 4 * ((row >> 4) & 3)
    return bias_of(meta, pos)


def far_head(b):
    return b // 4 + 4 * (b % 4)


def fold_mid(x, masks):
    out = x[0:64] * masks[0]
    for c in range(1, 4):
        out = out + x[64 * c : 64 * c + 64] * masks[c]
    return out


def fold_far(x, masks):
    out = x[0:16] * masks[0]
    for b in range(1, 16):
        out = out + x[16 * b : 16 * b + 16] * masks[far_head(b)]
    return out


def pack_rows(x, head_masks):
    mids = [
        head_masks[c] + head_masks[4 + c] + head_masks[8 + c] + head_masks[12 + c]
        for c in range(4)
    ]
    return jnp.concatenate([fold_mid(x, mids), fold_far(x, head_masks)], axis=0)


def norm_parts(inputs):
    mean = jnp.mean(inputs, axis=1, keepdims=True)
    centred = inputs - mean
    var = jnp.mean(centred * centred, axis=1, keepdims=True)
    inv_std = lax.rsqrt(var + 1e-05)
    return centred * inv_std, inv_std


def pack_masks():
    return [span_mask(HD * h, (1, D)).astype(BF) for h in range(HEADS)]


def key_kernel(tok_h, coords, table_h, gain, bias, w_h, inp_o, norm_o, kv_o, pack_o,
               tok, table, weight, sems):
    copies = [
        pltpu.make_async_copy(tok_h, tok, sems.at[0]),
        pltpu.make_async_copy(table_h, table, sems.at[1]),
        pltpu.make_async_copy(w_h.at[:, pl.ds(D, D)], weight.at[0], sems.at[2]),
        pltpu.make_async_copy(w_h.at[:, pl.ds(2 * D, D)], weight.at[1], sems.at[3]),
    ]
    for copy in copies:
        copy.start()
    sort = sort_matrix()
    grid = iota((T, T), 0)
    hots = []
    for axis in range(2):
        hot = jnp.where(grid == coords[axis : axis + 1, :], 1.0, 0.0).astype(BF)
        hots.append(nt(sort, hot).astype(BF))
    copies[0].wait()
    tok_s = nn(sort, tok[...])
    copies[1].wait()
    parts = []
    for hot in hots:
        found = nn(hot, table[...])
        parts.append(found[:, :384] + found[:, 384:768] + found[:, 768:])
    inputs = tok_s + jnp.concatenate(parts, axis=1)
    inp_o[...] = inputs
    unit, _ = norm_parts(inputs)
    normed = (unit * gain[...].reshape(1, D) + bias[...].reshape(1, D)).astype(BF)
    norm_o[...] = normed
    masks = pack_masks()
    for n in range(2):
        copies[2 + n].wait()
        part = nn(normed, weight[n]).astype(BF)
        kv_o[:, D * n : D * (n + 1)] = part
        pack_o[:, D * n : D * (n + 1)] = pack_rows(part, masks)


def query_kernel(normed, w_qkv, w_out, cot, q_o, da_o, cot_o, pack_o):
    cot_s = nn(sort_matrix(), cot[...]).astype(BF)
    cot_o[...] = cot_s
    q = nn(normed[...], w_qkv[...]).astype(BF)
    q_o[...] = q
    d_att = nt(cot_s, w_out[...]).astype(BF)
    da_o[...] = d_att
    masks = pack_masks()
    pack_o[:, :D] = pack_rows(q, masks)
    pack_o[:, D:] = pack_rows(d_att, masks)


def soft(scores):
    top = jnp.max(scores, axis=1, keepdims=True)
    shares = jnp.exp(scores - top)
    return top, jnp.sum(shares, axis=1, keepdims=True), shares.astype(BF)


def local_forward_kernel(meta, q_r, kv, o_o, top_o, sum_o, *, first):
    bias = local_bias(meta)
    o_o[...] = jnp.zeros_like(o_o)
    lane = iota((T, 128), 1)
    tops = jnp.full((T, 128), NEG, F32)
    sums = jnp.zeros((T, 128), F32)
    base = HD * first
    for h in range(first, first + 8):
        s, w = head_window(h)
        mask = head_mask(h)
        scores = nt(q_r[:, s : s + w] * mask, kv[:, s : s + w]) * SCALE + bias
        top, total, shares = soft(scores)
        tops = jnp.where(lane == h, top, tops)
        sums = jnp.where(lane == h, total, sums)
        o_o[:, s - base : s - base + w] += nn(shares, kv[:, D + s : D + s + w] * mask)
    top_o[...] = tops
    sum_o[...] = sums


def mid_rows(got, lo, width):
    return jnp.concatenate([got[0][:128, lo : lo + width], got[4][:128, lo : lo + width]], axis=0)


def far_rows(got, lo, width):
    at = slice(lo, lo + width)
    rows = []
    for n in (0, 4):
        rows.append(got[n][128:, at])
        rows += [got[n + d][:, at] for d in (1, 2, 3)]
    return jnp.concatenate(rows, axis=0)


def expand_matrix():
    head = iota((128, D), 0)
    lane = iota((128, D), 1)
    return jnp.where((lane >= head * HD) & (lane < head * HD + HD), 1.0, 0.0).astype(BF)


def gather_matrix():
    lane = iota((D, 128), 0)
    head = iota((D, 128), 1)
    return jnp.where((lane >= head * HD) & (lane < head * HD + HD), 1.0, 0.0).astype(BF)


def remote_forward_kernel(meta, q_r, *refs):
    got = refs[:8]
    o_1, top_1, sum_1, o_2, top_2, sum_2, d_att, pack, att_o, stat_o, send_o = refs[8:]
    lane = iota((T, 128), 1)
    row = iota((T, 128), 0)
    top_l = jnp.where(lane < 8, top_1[...], top_2[...])
    sum_l = jnp.where(lane < 8, sum_1[...], sum_2[...])
    tops_m = jnp.full((T, 128), NEG, F32)
    sums_m = jnp.zeros((T, 128), F32)
    mid = mid_bias(meta)
    mid_parts = []
    for g in range(4):
        s = group_window(g)
        mask = group_mask(g)
        q = q_r[:, s : s + 256] * mask
        scores = nt(q, mid_rows(got, s, 256)) * SCALE + mid
        top, total, shares = soft(scores)
        here = lane == 4 * g + (row >> 6)
        tops_m = jnp.where(here, top, tops_m)
        sums_m = jnp.where(here, total, sums_m)
        mid_parts.append(nn(shares, mid_rows(got, D + s, 256)))
    mask = far_mask()
    scores = nt(q_r[...] * mask, far_rows(got, 0, D)) * SCALE + far_bias(meta)
    top, total, shares = soft(scores)
    far_part = nn(shares, far_rows(got, D, D))
    here = lane == (row >> 6) + 4 * ((row >> 4) & 3)
    tops_f = jnp.where(here, top, NEG)
    sums_f = jnp.where(here, total, 0.0)
    highest = jnp.maximum(jnp.maximum(top_l, tops_m), tops_f)
    f_l = jnp.exp(top_l - highest)
    f_m = jnp.exp(tops_m - highest)
    f_f = jnp.exp(tops_f - highest)
    totals = f_l * sum_l + f_m * sums_m + f_f * sums_f
    totals = jnp.where(lane < HEADS, totals, 1.0)
    inverse = 1.0 / totals
    lse = highest + jnp.log(totals)
    w_m = f_m * inverse
    o_l = jnp.concatenate([o_1[...], o_2[...]], axis=1)
    att = o_l * exact(f_l * inverse, expand_matrix())
    w_f = jnp.sum(jnp.where(here, f_f * inverse, 0.0), axis=1, keepdims=True)
    att = att + far_part * w_f * mask.astype(F32)
    acc = [att[:, 128 * n : 128 * n + 128] for n in range(6)]
    for g in range(4):
        n = group_window(g) // 128
        w_g = jnp.sum(jnp.where(lane == 4 * g + (row >> 6), w_m, 0.0), axis=1, keepdims=True)
        add = mid_parts[g] * w_g * group_mask(g).astype(F32)
        acc[n] = acc[n] + add[:, :128]
        acc[n + 1] = acc[n + 1] + add[:, 128:]
    att = jnp.concatenate(acc, axis=1).astype(BF)
    att_o[...] = att
    prod = d_att[...].astype(F32) * att.astype(F32)
    delta = exact(prod, gather_matrix())
    stat = jnp.where(lane < HEADS, lse, pltpu.roll(delta, HEADS, 1))
    stat = jnp.where(lane < 2 * HEADS, stat, 0.0)
    stat_o[...] = stat
    one = iota((1, 128), 1)
    send_o[:, : 2 * D] = pack[...]
    mids = fold_mid(stat, [jnp.where((one & 3) == c, 1.0, 0.0) for c in range(4)])
    fars = fold_far(stat, [jnp.where((one & 15) == h, 1.0, 0.0) for h in range(HEADS)])
    send_o[:, 2 * D :] = three_parts(jnp.concatenate([mids, fars], axis=0))


def three_parts(x):
    lane = iota(x.shape, 1)
    hi = x.astype(BF).astype(F32)
    mid = (x - hi).astype(BF).astype(F32)
    low = x - hi - mid
    parts = jnp.where(lane < 64, pltpu.roll(mid, 32, 1), pltpu.roll(low, 64, 1))
    return jnp.where(lane < 32, hi, parts).astype(BF)


def out_kernel(att, inp, w_out, out_o):
    layer = (inp[...] + nn(att[...], w_out[...])).astype(BF)
    out_o[...] = nn(unsort_matrix(), layer).astype(BF)


def pick_mid_column(stat, col):
    return jnp.concatenate(
        [stat[64 * c : 64 * c + 64, col + c : col + c + 1] for c in range(4)], axis=0
    )


def pick_far_column(stat, col):
    return jnp.concatenate(
        [
            stat[16 * b : 16 * b + 16, col + far_head(b) : col + far_head(b) + 1]
            for b in range(16)
        ],
        axis=0,
    )


def local_backward_kernel(meta, q_r, kv, d_att, stat, dq_o, dk_o, dv_o, *, first):
    bias = local_bias(meta)
    dq_o[...] = jnp.zeros_like(dq_o)
    dk_o[...] = jnp.zeros_like(dk_o)
    dv_o[...] = jnp.zeros_like(dv_o)
    base = HD * first
    for h in range(first, first + 8):
        s, w = head_window(h)
        t = s - base
        mask = head_mask(h)
        q = q_r[:, s : s + w] * mask
        k = kv[:, s : s + w] * mask
        da = d_att[:, s : s + w] * mask
        scores = nt(q, k) * SCALE + bias
        shares = jnp.exp(scores - stat[:, h : h + 1])
        d_shares = nt(da, kv[:, D + s : D + s + w])
        ds = (shares * (d_shares - stat[:, HEADS + h : HEADS + h + 1])).astype(BF)
        dq_o[:, t : t + w] += nn(ds, k)
        dk_o[:, t : t + w] += tn(ds, q)
        dv_o[:, t : t + w] += tn(shares.astype(BF), da)


def query_backward_kernel(meta, q_r, d_att, stat, *refs):
    got, dq_o = refs[:8], refs[8]
    dq_o[...] = jnp.zeros_like(dq_o)
    mid = mid_bias(meta)
    for g in range(4):
        s = group_window(g)
        mask = group_mask(g)
        k = mid_rows(got, s, 256)
        scores = nt(q_r[:, s : s + 256] * mask, k) * SCALE + mid
        shares = jnp.exp(scores - pick_mid_column(stat, 4 * g))
        d_shares = nt(d_att[:, s : s + 256] * mask, mid_rows(got, D + s, 256))
        ds = (shares * (d_shares - pick_mid_column(stat, HEADS + 4 * g))).astype(BF)
        dq_o[:, s : s + 256] += nn(ds, k) * mask.astype(F32)
    mask = far_mask()
    k = far_rows(got, 0, D)
    scores = nt(q_r[...] * mask, k) * SCALE + far_bias(meta)
    shares = jnp.exp(scores - pick_far_column(stat, 0))
    d_shares = nt(d_att[...] * mask, far_rows(got, D, D))
    ds = (shares * (d_shares - pick_far_column(stat, HEADS))).astype(BF)
    dq_o[...] += nn(ds, k) * mask.astype(F32)


def spread_mid(stat_t, row):
    return jnp.concatenate(
        [jnp.broadcast_to(stat_t[row + c : row + c + 1, :], (64, T)) for c in range(4)], axis=0
    )


def spread_far(stat_t, row):
    return jnp.concatenate(
        [
            jnp.broadcast_to(stat_t[row + far_head(b) : row + far_head(b) + 1, :], (16, T))
            for b in range(16)
        ],
        axis=0,
    )


def joined_stats(rows):
    x = rows.astype(F32).T
    return x[:32] + (x[32:64] + x[64:96])


def key_backward_kernel(meta, kv, *refs):
    got = refs[:8]
    dq_r, dq_1, dk_1, dv_1, dq_2, dk_2, dv_2, cot = refs[8:16]
    all_o, kept_o, sent_o, dk_s, dv_s = refs[16:]
    half = D // 2
    dk_s[:, :half] = dk_1[...]
    dk_s[:, half:] = dk_2[...]
    dv_s[:, :half] = dv_1[...]
    dv_s[:, half:] = dv_2[...]
    stat_t = joined_stats(mid_rows(got, 2 * D, 128))
    mid = mid_bias(meta)
    for g in range(4):
        s = group_window(g)
        mask = group_mask(g)
        mask_f = mask.astype(F32)
        q = mid_rows(got, s, 256)
        da = mid_rows(got, D + s, 256)
        scores = nt(kv[:, s : s + 256] * mask, q) * SCALE + mid
        shares = jnp.exp(scores - spread_mid(stat_t, 4 * g))
        d_shares = nt(kv[:, D + s : D + s + 256] * mask, da)
        ds = (shares * (d_shares - spread_mid(stat_t, HEADS + 4 * g))).astype(BF)
        dk_s[:, s : s + 256] += nn(ds, q) * mask_f
        dv_s[:, s : s + 256] += nn(shares.astype(BF), da) * mask_f
    stat_t = joined_stats(far_rows(got, 2 * D, 128))
    mask = far_mask()
    mask_f = mask.astype(F32)
    q = far_rows(got, 0, D)
    da = far_rows(got, D, D)
    scores = nt(kv[:, :D] * mask, q) * SCALE + far_bias(meta)
    shares = jnp.exp(scores - spread_far(stat_t, 0))
    d_shares = nt(kv[:, D:] * mask, da)
    ds = (shares * (d_shares - spread_far(stat_t, HEADS))).astype(BF)
    dk_s[...] += nn(ds, q) * mask_f
    dv_s[...] += nn(shares.astype(BF), da) * mask_f
    dq = jnp.concatenate([dq_1[...], dq_2[...]], axis=1) + dq_r[...]
    d_q = (dq * SCALE).astype(BF)
    d_k = (dk_s[...] * SCALE).astype(BF)
    d_v = dv_s[...].astype(BF)
    all_o[:, :D] = d_q
    all_o[:, D : 2 * D] = d_k
    all_o[:, 2 * D :] = d_v
    first = meta[5] == 0
    kept_o[:, :D] = jnp.where(first, d_q, d_v)
    kept_o[:, D:] = jnp.where(first, d_k, cot[...])
    sent_o[:, :D] = jnp.where(first, d_v, d_q)
    sent_o[:, D:] = jnp.where(first, cot[...], d_k)


def weight_grad_kernel(meta, own, other, norm_a, norm_b, att_a, att_b, keep_o, s1, s2, s3, left):
    left[0] = jnp.concatenate([norm_a[...], norm_b[...]], axis=0).T
    left[1] = left[0]

    @pl.when(meta[5] == 1)
    def _():
        left[1] = jnp.concatenate([att_a[...], att_b[...]], axis=0).T

    for d, out in ((2, s2), (1, s1), (3, s3), (0, keep_o)):
        j = (meta[6] + d) & 3
        cols = pl.ds(pl.multiple_of(j * WIDE, 128), WIDE)
        right = jnp.concatenate([own[:, cols], other[:, cols]], axis=0)
        out[...] = nn(left[j >> 1], right).astype(out.dtype)


def token_grad_kernel(d_qkv, w_qkv, inp, gain, cot, tok_o, ext_o):
    d_normed = nt(d_qkv[...], w_qkv[...])
    unit, inv_std = norm_parts(inp[...])
    d_gain = jnp.sum(d_normed * unit, axis=0, keepdims=True)
    d_bias = jnp.sum(d_normed, axis=0, keepdims=True)
    ext_o[...] = two_parts(jnp.concatenate(
        [d_gain[:, :WIDE], d_gain[:, WIDE:], d_bias[:, :WIDE], d_bias[:, WIDE:],
         jnp.zeros((4, WIDE), F32)], axis=0))
    d_unit = d_normed * gain[...].reshape(1, D)
    mean_a = jnp.mean(d_unit, axis=1, keepdims=True)
    mean_b = jnp.mean(d_unit * unit, axis=1, keepdims=True)
    d_tok = cot[...].astype(F32) + inv_std * (d_unit - mean_a - unit * mean_b)
    tok_o[...] = nn(unsort_matrix(), d_tok.astype(BF)).astype(BF)


def two_parts(ext):
    hi = ext.astype(BF)
    return jnp.concatenate([hi, (ext - hi.astype(F32)).astype(BF)], axis=0)


def whole_of(rows):
    return rows[:8].astype(F32) + rows[8:].astype(F32)


def ring_total(meta, slot, own, got, pad):
    pad[meta[slot]] = own
    for d, piece in enumerate(got, 1):
        pad[(meta[slot] - d) & 3] = piece
    return (pad[0] + pad[1]) + (pad[2] + pad[3])


def add_a_kernel(meta, keep, r1, r2, r3, ext, keep_o, s1, s2, s3):
    rows = D // 4
    for d, out in ((2, s2), (1, s1), (3, s3), (0, keep_o)):
        at = pl.ds(pl.multiple_of(((meta[7] + d) & 3) * rows, 16), rows)
        total = keep[at, :] + (r1[at, :].astype(F32) + r2[at, :].astype(F32) + r3[at, :].astype(F32))
        if d == 0:
            out[...] = total
        else:
            out[:rows] = total.astype(BF)
            out[rows:] = ext[...]


def add_b_kernel(meta, keep, r1, r2, r3, ext, out, pad):
    rows = D // 4
    got = (r1, r2, r3)
    total = keep[...]
    for r in got:
        total = total + r[:rows].astype(F32)
    out[:rows] = total.astype(BF)
    sums = ring_total(meta, 7, whole_of(ext[...]), [whole_of(r[rows:]) for r in got], pad)
    out[rows:] = two_parts(sums)


def add_c_kernel(own, r1, r2, r3, out):
    rows = D // 4

    def total(a, b, c, d):
        return (a + c) + (b + d)

    out[:rows] = total(*[r[:rows].astype(F32) for r in (own, r1, r2, r3)]).astype(BF)
    out[rows:] = two_parts(total(*[whole_of(r[rows:]) for r in (own, r1, r2, r3)]))


def merge_kernel(meta, own, r1, r2, r3, out):
    rows = D // 4
    out[D:] = own[rows:]
    for d, piece in enumerate((own, r1, r2, r3)):
        at = pl.ds(pl.multiple_of(((meta[7] - d) & 3) * rows, 16), rows)
        out[at, :] = piece[:rows]


def finish_kernel(meta, *refs, marks, first, last):
    count = len(marks)
    pieces, refs = refs[:count], refs[count:]
    if last:
        tails, refs = refs[:8], refs[8:]
    if not first:
        refs = refs[2:]
    qkv_o, out_o, *refs = refs
    if last:
        gain_o, bias_o, *refs = refs
    sems, wide = refs[0], refs[1 : 1 + count]
    for n, (piece, (core, turn, row)) in enumerate(zip(pieces, marks)):
        chunk = (meta[5] ^ core) * 4 + ((meta[9 if core else 6] - turn) & 3)
        size = wide[n].shape[0]
        wide[n][...] = piece[:size].astype(F32)

        @pl.when(chunk < 6)
        def _(n=n, chunk=chunk, row=row, size=size):
            at = pl.ds(pl.multiple_of(chunk * WIDE, 128), WIDE)
            to = qkv_o.at[pl.ds(row, size), at]
            pltpu.make_async_copy(wide[n], to, sems.at[n]).start()

        @pl.when(chunk >= 6)
        def _(n=n, chunk=chunk, row=row, size=size):
            at = pl.ds(pl.multiple_of((chunk - 6) * WIDE, 128), WIDE)
            to = out_o.at[pl.ds(row, size), at]
            pltpu.make_async_copy(wide[n], to, sems.at[n]).start()

    if last:
        pad = refs[1 + count]
        for n, tail in enumerate(tails):
            core = n // 4
            place = (meta[9 if core else 6] - n % 4) & 3
            pad[(meta[5] ^ core) * 4 + place] = whole_of(tail[...])
        total = pad[0]
        for n in range(1, 8):
            total = total + pad[n]
        gain_o[...] = jnp.concatenate([total[0:1], total[1:2]], axis=1).reshape(D)
        bias_o[...] = jnp.concatenate([total[2:3], total[3:4]], axis=1).reshape(D)
    for n in range(count):
        to = qkv_o.at[pl.ds(0, wide[n].shape[0]), pl.ds(0, WIDE)]
        pltpu.make_async_copy(wide[n], to, sems.at[n]).wait()


def finish(meta, pieces, outs, tails=None):
    first, last = outs is None, tails is not None
    marks = tuple(piece[1:] for piece in pieces)
    arrays = [piece[0] for piece in pieces]
    smem = pl.BlockSpec(memory_space=pltpu.SMEM)
    anywhere = pl.BlockSpec(memory_space=pl.ANY)
    whole = pl.BlockSpec(memory_space=pltpu.VMEM)
    args = [meta, *arrays]
    in_specs = [smem] + [whole] * len(arrays)
    if last:
        args += tails
        for tail in tails:
            index = (tail.shape[0] // 16 - 1, 0)
            in_specs.append(pl.BlockSpec((16, WIDE), lambda i, index=index: index))
    aliases = {}
    if not first:
        aliases = {len(args): 0, len(args) + 1: 1}
        args += list(outs)
        in_specs += [anywhere] * 2
    out_shape = [jax.ShapeDtypeStruct((D, 3 * D), F32), jax.ShapeDtypeStruct((D, D), F32)]
    out_specs = [anywhere] * 2
    scratch = [pltpu.SemaphoreType.DMA((len(pieces),))]
    for array in arrays:
        scratch.append(pltpu.VMEM((array.shape[0] // WIDE * WIDE, WIDE), F32))
    if last:
        out_shape += [jax.ShapeDtypeStruct((D,), F32)] * 2
        out_specs += [pl.BlockSpec((D,), lambda i: (0,))] * 2
        scratch += [pltpu.VMEM((8, 8, WIDE), F32)]
    return pl.pallas_call(
        functools.partial(finish_kernel, marks=marks, first=first, last=last),
        grid=(1,),
        in_specs=in_specs,
        out_specs=out_specs,
        out_shape=out_shape,
        scratch_shapes=scratch,
        input_output_aliases=aliases,
        compiler_params=pltpu.CompilerParams(vmem_limit_bytes=24 << 20),
        name="finish",
    )(*args)


def call(kernel, outs, *args, smem=0, scratch=(), name=None, limit=24, windows=None,
         anywhere=()):
    specs = [pl.BlockSpec(memory_space=pltpu.SMEM)] * smem
    specs += [pl.BlockSpec(memory_space=pltpu.VMEM)] * (len(args) - smem)
    for n in anywhere:
        specs[n] = pl.BlockSpec(memory_space=pl.ANY)
    for n, (shape, index) in (windows or {}).items():
        specs[n] = pl.BlockSpec(shape, lambda i, index=index: index)
    return pl.pallas_call(
        kernel,
        grid=(1,) if windows else (),
        out_shape=[jax.ShapeDtypeStruct(shape, dtype) for shape, dtype in outs],
        in_specs=specs,
        out_specs=[pl.BlockSpec(memory_space=pltpu.VMEM)] * len(outs),
        scratch_shapes=scratch,
        compiler_params=pltpu.CompilerParams(vmem_limit_bytes=limit << 20),
        name=name,
    )(*args)


def swap_seq(block, code):
    return lax.ppermute(block, "seq", [(i, i ^ code) for i in range(16)])


def z_send(block):
    def shift(d):
        return lax.ppermute(block, "seq", [(i, (i + 4 * d) % 16) for i in range(16)])

    got = {d: shift(d) for d in (2, 1, 3)}
    return [got[1], got[2], got[3]]


def after(*values):
    return lax.optimization_barrier(values)


def join(*blocks):
    return jnp.concatenate(blocks, axis=0)


def decode(i):
    dp, seq = i // 16, i % 16
    return [dp // 2, (seq // 2) % 2 * 2 + dp % 2, seq // 4, seq % 2]


def encode(x, y, z, core):
    return (x * 2 + y % 2) * 16 + z * 4 + y // 2 * 2 + core


def ring_route(stage, d):
    route = []
    for i in range(128):
        place = decode(i)
        axis = (stage + place[3]) % 3
        place[axis] = (place[axis] + d) % 4
        route.append((i, encode(*place)))
    return route


def hop(block, stage, d):
    return lax.ppermute(block, AXES, ring_route(stage, d))


def ring_send(blocks, stage):
    got = {d: hop(blocks[d - 1], stage, d) for d in (2, 1, 3)}
    return got[1], got[2], got[3]


def place_meta(lengths):
    dp = lax.axis_index("dp").astype(jnp.int32)
    seq = lax.axis_index("seq").astype(jnp.int32)
    core = seq & 1
    coords = [dp >> 1, (seq & 2) + (dp & 1), seq >> 2]
    turns = [jnp.where(core == 0, coords[n], coords[(n + 1) % 3]) for n in range(3)]
    other = jnp.where(core == 0, coords[1], coords[0])
    values = jnp.stack([core] + turns + [other])
    return jnp.concatenate([seq[None], lengths, values, jnp.zeros((6,), jnp.int32)])


def sum_everywhere(meta, keep, sends, ext, beside):
    cut = D // 4
    got = ring_send(sends, 0)
    *got, _ = after(*got, beside)
    keep, *sends = call(
        add_a_kernel,
        [((cut, WIDE), F32)] + [((cut + 16, WIDE), BF)] * 3,
        meta, keep, *got, ext, smem=1, name="add_a",
    )
    got = ring_send(sends, 1)
    block = call(
        add_b_kernel, [((cut + 16, WIDE), BF)],
        meta, keep, *got, ext, smem=1, name="add_b", scratch=[pltpu.VMEM((4, 8, WIDE), F32)],
    )[0]
    got = ring_send([block] * 3, 2)
    block = call(add_c_kernel, [((cut + 16, WIDE), BF)], block, *got, name="add_c")[0]
    got = ring_send([block] * 3, 1)
    block = call(
        merge_kernel, [((D + 16, WIDE), BF)], meta, block, *got, smem=1, name="merge_b",
    )[0]
    ring = [block, *ring_send([block] * 3, 0)]
    twin = [swap_seq(block, 1)]
    outs = finish(meta, [(block, 0, 0, 0), (twin[0], 1, 0, 0)], None)
    *ring, first = after(*ring, outs[0])
    twin += [swap_seq(piece, 1) for piece in ring[1:]]
    outs = finish(meta, [(ring[d], 0, d, 0) for d in (1, 2, 3)], (first, outs[1]))
    return finish(meta, [(twin[d], 1, d, 0) for d in (1, 2, 3)], outs, ring + twin)


def position_table():
    quarter = D // 4
    frequency = 1.0 / 10000.0 ** (np.arange(quarter) / quarter)
    angle = np.arange(256)[:, None] * frequency[None, :]
    exact_values = np.concatenate([np.sin(angle), np.cos(angle)], axis=1).astype(np.float32)
    parts = []
    rest = exact_values
    for _ in range(3):
        part = rest.astype(jnp.bfloat16)
        parts.append(part)
        rest = rest - part.astype(np.float32)
    return np.concatenate(parts, axis=1)


def per_device(tokens, tile_coords, slide_lengths, norm_gain, norm_bias, w_qkv, w_out, cotangent):
    meta = place_meta(slide_lengths[0])
    table = jnp.asarray(position_table())
    inp, normed, kv, kv_pack = call(
        key_kernel,
        [((T, D), F32), ((T, D), BF), ((T, 2 * D), BF), ((80, 2 * D), BF)],
        tokens[0], tile_coords[0], table, norm_gain, norm_bias, w_qkv, name="keys", limit=60,
        anywhere=(0, 2, 5),
        scratch=[
            pltpu.VMEM((T, D), BF), pltpu.VMEM((T, 3 * D // 2), BF), pltpu.VMEM((2, D, D), BF),
            pltpu.SemaphoreType.DMA((4,)),
        ],
    )
    from_y = swap_seq(kv_pack, 2)
    norm_b = swap_seq(normed, 1)
    q, d_att, cot, qd_pack = call(
        query_kernel,
        [((T, D), BF), ((T, D), BF), ((T, D), BF), ((80, 2 * D), BF)],
        normed, w_qkv, w_out, cotangent[0], name="queries", limit=60,
        windows={1: ((D, D), (0, 0))},
    )
    from_y, q, norm_b = after(from_y, q, norm_b)
    far = join(kv_pack[64:], from_y[64:])
    from_z = z_send(far)
    far, q = after(far, q)
    part = join(kv_pack[:64], from_y[:64], far)
    twin = swap_seq(part, 1)
    tops = [
        call(
            functools.partial(local_forward_kernel, first=first),
            [((T, D // 2), F32), ((T, 128), F32), ((T, 128), F32)],
            meta, q, kv, smem=1, name="local_forward",
        )
        for first in (0, 8)
    ]
    *from_z, twin, _, _ = after(*from_z, twin, tops[0][0], tops[1][0])
    got_kv = (part, *from_z, twin, *[swap_seq(rows, 1) for rows in from_z])
    att, stat, pack = call(
        remote_forward_kernel,
        [((T, D), BF), ((T, 128), F32), ((80, 2 * D + 128), BF)],
        meta, q, *got_kv, *tops[0], *tops[1], d_att, qd_pack,
        smem=1, name="remote_forward",
    )
    from_y = swap_seq(pack, 2)
    att_b = swap_seq(att, 1)
    grads_1 = call(
        functools.partial(local_backward_kernel, first=0),
        [((T, D // 2), F32)] * 3,
        meta, q, kv, d_att, stat, smem=1, name="local_backward",
    )
    dq_r = call(
        query_backward_kernel, [((T, D), F32)],
        meta, q, d_att, stat, *got_kv, smem=1, name="query_backward",
    )[0]
    from_y, att_b, dq_r, *grads_1 = after(from_y, att_b, dq_r, *grads_1)
    far = join(pack[64:], from_y[64:])
    from_z = z_send(far)
    far, q = after(far, q)
    part = join(pack[:64], from_y[:64], far)
    twin = swap_seq(part, 1)
    grads_2 = call(
        functools.partial(local_backward_kernel, first=8),
        [((T, D // 2), F32)] * 3,
        meta, q, kv, d_att, stat, smem=1, name="local_backward",
    )
    *from_z, twin, _ = after(*from_z, twin, grads_2[0])
    got_qd = (part, *from_z, twin, *[swap_seq(rows, 1) for rows in from_z])
    d_qkv, own, sent = call(
        key_backward_kernel,
        [((T, 3 * D), BF), ((T, 2 * D), BF), ((T, 2 * D), BF)],
        meta, kv, *got_qd, dq_r, *grads_1, *grads_2, cot,
        smem=1, name="key_backward",
        scratch=[pltpu.VMEM((T, D), F32), pltpu.VMEM((T, D), F32)],
    )
    keep, *sends = call(
        weight_grad_kernel,
        [((D, WIDE), F32)] + [((D, WIDE), BF)] * 3,
        meta, own, swap_seq(sent, 1), normed, norm_b, att, att_b,
        smem=1, name="weight_grad",
        scratch=[pltpu.VMEM((2, D, 2 * T), BF)],
    )
    d_tokens, ext = call(
        token_grad_kernel,
        [((T, D), BF), ((16, WIDE), BF)],
        d_qkv, w_qkv, inp, norm_gain, cot, name="token_grad",
    )
    att, _ = after(att, keep)
    layer_out = call(out_kernel, [((T, D), BF)], att, inp, w_out, name="layer_out")[0]
    dw_qkv, dw_out, d_gain, d_bias = sum_everywhere(meta, keep, sends, ext, layer_out)
    return (
        layer_out[None],
        d_tokens[None],
        dw_qkv,
        dw_out,
        d_gain,
        d_bias,
    )


def solution(mesh):
    return jax.shard_map(
        per_device,
        mesh=mesh,
        in_specs=(
            P("dp", "seq", None),
            P("dp", None, "seq"),
            P("dp", None),
            P(),
            P(),
            P(),
            P(),
            P("dp", "seq", None),
        ),
        out_specs=(P("dp", "seq", None), P("dp", "seq", None), P(), P(), P(), P()),
        check_vma=False,
    )
```

```python
import functools

import jax
import jax.numpy as jnp
import numpy as np
from jax import lax
from jax.experimental import pallas as pl
from jax.experimental.pallas import tpu as pltpu
from jax.sharding import PartitionSpec as P

HEADS = 16
HD = 48
D = 768
T = 256
SCALE = HD ** (-0.5)
NEG = -1e30
BF = jnp.bfloat16
F32 = jnp.float32
AXES = ("dp", "seq")
WIDE = 384


def iota(shape, dim):
    return lax.broadcasted_iota(jnp.int32, shape, dim)


def tile_of(i):
    return (i >> 6) + ((i >> 4) & 3) * 4 + (i & 15) * 16


def nt(a, b):
    return lax.dot_general(a, b, (((1,), (1,)), ((), ())), preferred_element_type=F32)


def nn(a, b):
    return lax.dot_general(a, b, (((1,), (0,)), ((), ())), preferred_element_type=F32)


def tn(a, b):
    return lax.dot_general(a, b, (((0,), (0,)), ((), ())), preferred_element_type=F32)


def exact(a, b):
    hi = a.astype(BF)
    rest = a - hi.astype(F32)
    mid = rest.astype(BF)
    low = (rest - mid.astype(F32)).astype(BF)
    return nn(hi, b) + nn(mid, b) + nn(low, b)


def sort_matrix():
    return jnp.where(tile_of(iota((T, T), 0)) == iota((T, T), 1), 1.0, 0.0).astype(BF)


def unsort_matrix():
    return jnp.where(iota((T, T), 0) == tile_of(iota((T, T), 1)), 1.0, 0.0).astype(BF)


def span_mask(lo, shape):
    lane = iota(shape, 1)
    return jnp.where((lane >= lo) & (lane < lo + HD), 1.0, 0.0)


def head_window(h):
    start = HD * h // 128 * 128
    width = 128 if HD * h - start + HD <= 128 else 256
    return start, width


def head_mask(h):
    start, width = head_window(h)
    return span_mask(HD * h - start, (1, width)).astype(BF)


def group_window(g):
    return 192 * g // 128 * 128


def group_mask(g):
    lo = 192 * g - group_window(g) + HD * (iota((T, 256), 0) >> 6)
    return span_mask(lo, (T, 256)).astype(BF)


def far_mask():
    row = iota((T, D), 0)
    lo = HD * ((row >> 6) + 4 * ((row >> 4) & 3))
    return span_mask(lo, (T, D)).astype(BF)


def slide_of(meta, pos):
    end = meta[1]
    out = jnp.where(pos >= end, 1, 0)
    for n in range(2, 5):
        end = end + meta[n]
        out = out + jnp.where(pos >= end, 1, 0)
    return out


def row_ids(meta):
    return slide_of(meta, meta[0] * T + tile_of(iota((T, 1), 0)))


def bias_of(meta, pos):
    return jnp.where(row_ids(meta) == slide_of(meta, pos), 0.0, NEG)


def local_bias(meta):
    return bias_of(meta, meta[0] * T + tile_of(iota((1, T), 1)))


def mid_bias(meta):
    t = iota((T, T), 1)
    slot = t >> 6
    dev = meta[0] ^ (((slot & 1) << 1) | (slot >> 1))
    pos = dev * T + ((t >> 4) & 3) * 4 + (t & 15) * 16 + (iota((T, T), 0) >> 6)
    return bias_of(meta, pos)


def far_bias(meta):
    t = iota((T, T), 1)
    s = t >> 4
    place = (((meta[0] >> 2) - (s >> 1)) & 3) * 4 + ((meta[0] & 3) ^ ((s & 1) << 1) ^ (s >> 3))
    row = iota((T, T), 0)
    pos = place * T + (t & 15) * 16 + (row >> 6) + 4 * ((row >> 4) & 3)
    return bias_of(meta, pos)


def far_head(b):
    return b // 4 + 4 * (b % 4)


def fold_mid(x, masks):
    out = x[0:64] * masks[0]
    for c in range(1, 4):
        out = out + x[64 * c : 64 * c + 64] * masks[c]
    return out


def fold_far(x, masks):
    out = x[0:16] * masks[0]
    for b in range(1, 16):
        out = out + x[16 * b : 16 * b + 16] * masks[far_head(b)]
    return out


def pack_rows(x, head_masks):
    mids = [
        head_masks[c] + head_masks[4 + c] + head_masks[8 + c] + head_masks[12 + c]
        for c in range(4)
    ]
    return jnp.concatenate([fold_mid(x, mids), fold_far(x, head_masks)], axis=0)


def norm_parts(inputs):
    mean = jnp.mean(inputs, axis=1, keepdims=True)
    centred = inputs - mean
    var = jnp.mean(centred * centred, axis=1, keepdims=True)
    inv_std = lax.rsqrt(var + 1e-05)
    return centred * inv_std, inv_std


def pack_masks():
    return [span_mask(HD * h, (1, D)).astype(BF) for h in range(HEADS)]


def key_kernel(tok_h, coords, table_h, gain, bias, w_h, inp_o, norm_o, kv_o, pack_o,
               tok, table, weight, sems):
    copies = [
        pltpu.make_async_copy(tok_h, tok, sems.at[0]),
        pltpu.make_async_copy(table_h, table, sems.at[1]),
        pltpu.make_async_copy(w_h.at[:, pl.ds(D, D)], weight.at[0], sems.at[2]),
        pltpu.make_async_copy(w_h.at[:, pl.ds(2 * D, D)], weight.at[1], sems.at[3]),
    ]
    for copy in copies:
        copy.start()
    sort = sort_matrix()
    grid = iota((T, T), 0)
    hots = []
    for axis in range(2):
        hot = jnp.where(grid == coords[axis : axis + 1, :], 1.0, 0.0).astype(BF)
        hots.append(nt(sort, hot).astype(BF))
    copies[0].wait()
    tok_s = nn(sort, tok[...])
    copies[1].wait()
    parts = []
    for hot in hots:
        found = nn(hot, table[...])
        parts.append(found[:, :384] + found[:, 384:768] + found[:, 768:])
    inputs = tok_s + jnp.concatenate(parts, axis=1)
    inp_o[...] = inputs
    unit, _ = norm_parts(inputs)
    normed = (unit * gain[...].reshape(1, D) + bias[...].reshape(1, D)).astype(BF)
    norm_o[...] = normed
    masks = pack_masks()
    for n in range(2):
        copies[2 + n].wait()
        part = nn(normed, weight[n]).astype(BF)
        kv_o[:, D * n : D * (n + 1)] = part
        pack_o[:, D * n : D * (n + 1)] = pack_rows(part, masks)


def query_kernel(normed, w_qkv, w_out, cot, q_o, da_o, cot_o, pack_o):
    cot_s = nn(sort_matrix(), cot[...]).astype(BF)
    cot_o[...] = cot_s
    q = nn(normed[...], w_qkv[...]).astype(BF)
    q_o[...] = q
    d_att = nt(cot_s, w_out[...]).astype(BF)
    da_o[...] = d_att
    masks = pack_masks()
    pack_o[:, :D] = pack_rows(q, masks)
    pack_o[:, D:] = pack_rows(d_att, masks)


def soft(scores):
    top = jnp.max(scores, axis=1, keepdims=True)
    shares = jnp.exp(scores - top)
    return top, jnp.sum(shares, axis=1, keepdims=True), shares.astype(BF)


def local_forward_kernel(meta, q_r, kv, o_o, top_o, sum_o, *, first):
    bias = local_bias(meta)
    o_o[...] = jnp.zeros_like(o_o)
    lane = iota((T, 128), 1)
    tops = jnp.full((T, 128), NEG, F32)
    sums = jnp.zeros((T, 128), F32)
    base = HD * first
    for h in range(first, first + 8):
        s, w = head_window(h)
        mask = head_mask(h)
        scores = nt(q_r[:, s : s + w] * mask, kv[:, s : s + w]) * SCALE + bias
        top, total, shares = soft(scores)
        tops = jnp.where(lane == h, top, tops)
        sums = jnp.where(lane == h, total, sums)
        o_o[:, s - base : s - base + w] += nn(shares, kv[:, D + s : D + s + w] * mask)
    top_o[...] = tops
    sum_o[...] = sums


def mid_rows(got, lo, width):
    return jnp.concatenate([got[0][:128, lo : lo + width], got[4][:128, lo : lo + width]], axis=0)


def far_rows(got, lo, width):
    at = slice(lo, lo + width)
    rows = []
    for n in (0, 4):
        rows.append(got[n][128:, at])
        rows += [got[n + d][:, at] for d in (1, 2, 3)]
    return jnp.concatenate(rows, axis=0)


def expand_matrix():
    head = iota((128, D), 0)
    lane = iota((128, D), 1)
    return jnp.where((lane >= head * HD) & (lane < head * HD + HD), 1.0, 0.0).astype(BF)


def gather_matrix():
    lane = iota((D, 128), 0)
    head = iota((D, 128), 1)
    return jnp.where((lane >= head * HD) & (lane < head * HD + HD), 1.0, 0.0).astype(BF)


def remote_forward_kernel(meta, q_r, *refs):
    got = refs[:8]
    o_1, top_1, sum_1, o_2, top_2, sum_2, d_att, pack, att_o, stat_o, send_o = refs[8:]
    lane = iota((T, 128), 1)
    row = iota((T, 128), 0)
    top_l = jnp.where(lane < 8, top_1[...], top_2[...])
    sum_l = jnp.where(lane < 8, sum_1[...], sum_2[...])
    tops_m = jnp.full((T, 128), NEG, F32)
    sums_m = jnp.zeros((T, 128), F32)
    mid = mid_bias(meta)
    mid_parts = []
    for g in range(4):
        s = group_window(g)
        mask = group_mask(g)
        q = q_r[:, s : s + 256] * mask
        scores = nt(q, mid_rows(got, s, 256)) * SCALE + mid
        top, total, shares = soft(scores)
        here = lane == 4 * g + (row >> 6)
        tops_m = jnp.where(here, top, tops_m)
        sums_m = jnp.where(here, total, sums_m)
        mid_parts.append(nn(shares, mid_rows(got, D + s, 256)))
    mask = far_mask()
    scores = nt(q_r[...] * mask, far_rows(got, 0, D)) * SCALE + far_bias(meta)
    top, total, shares = soft(scores)
    far_part = nn(shares, far_rows(got, D, D))
    here = lane == (row >> 6) + 4 * ((row >> 4) & 3)
    tops_f = jnp.where(here, top, NEG)
    sums_f = jnp.where(here, total, 0.0)
    highest = jnp.maximum(jnp.maximum(top_l, tops_m), tops_f)
    f_l = jnp.exp(top_l - highest)
    f_m = jnp.exp(tops_m - highest)
    f_f = jnp.exp(tops_f - highest)
    totals = f_l * sum_l + f_m * sums_m + f_f * sums_f
    totals = jnp.where(lane < HEADS, totals, 1.0)
    inverse = 1.0 / totals
    lse = highest + jnp.log(totals)
    w_m = f_m * inverse
    o_l = jnp.concatenate([o_1[...], o_2[...]], axis=1)
    att = o_l * exact(f_l * inverse, expand_matrix())
    w_f = jnp.sum(jnp.where(here, f_f * inverse, 0.0), axis=1, keepdims=True)
    att = att + far_part * w_f * mask.astype(F32)
    acc = [att[:, 128 * n : 128 * n + 128] for n in range(6)]
    for g in range(4):
        n = group_window(g) // 128
        w_g = jnp.sum(jnp.where(lane == 4 * g + (row >> 6), w_m, 0.0), axis=1, keepdims=True)
        add = mid_parts[g] * w_g * group_mask(g).astype(F32)
        acc[n] = acc[n] + add[:, :128]
        acc[n + 1] = acc[n + 1] + add[:, 128:]
    att = jnp.concatenate(acc, axis=1).astype(BF)
    att_o[...] = att
    prod = d_att[...].astype(F32) * att.astype(F32)
    delta = exact(prod, gather_matrix())
    stat = jnp.where(lane < HEADS, lse, pltpu.roll(delta, HEADS, 1))
    stat = jnp.where(lane < 2 * HEADS, stat, 0.0)
    stat_o[...] = stat
    one = iota((1, 128), 1)
    send_o[:, : 2 * D] = pack[...]
    mids = fold_mid(stat, [jnp.where((one & 3) == c, 1.0, 0.0) for c in range(4)])
    fars = fold_far(stat, [jnp.where((one & 15) == h, 1.0, 0.0) for h in range(HEADS)])
    send_o[:, 2 * D :] = three_parts(jnp.concatenate([mids, fars], axis=0))


def three_parts(x):
    lane = iota(x.shape, 1)
    hi = x.astype(BF).astype(F32)
    mid = (x - hi).astype(BF).astype(F32)
    low = x - hi - mid
    parts = jnp.where(lane < 64, pltpu.roll(mid, 32, 1), pltpu.roll(low, 64, 1))
    return jnp.where(lane < 32, hi, parts).astype(BF)


def out_kernel(att, inp, w_out, out_o):
    layer = (inp[...] + nn(att[...], w_out[...])).astype(BF)
    out_o[...] = nn(unsort_matrix(), layer).astype(BF)


def pick_mid_column(stat, col):
    return jnp.concatenate(
        [stat[64 * c : 64 * c + 64, col + c : col + c + 1] for c in range(4)], axis=0
    )


def pick_far_column(stat, col):
    return jnp.concatenate(
        [
            stat[16 * b : 16 * b + 16, col + far_head(b) : col + far_head(b) + 1]
            for b in range(16)
        ],
        axis=0,
    )


def local_backward_kernel(meta, q_r, kv, d_att, stat, dq_o, dk_o, dv_o, *, first):
    bias = local_bias(meta)
    stat_t = stat[...].T
    dq_o[...] = jnp.zeros_like(dq_o)
    dk_o[...] = jnp.zeros_like(dk_o)
    dv_o[...] = jnp.zeros_like(dv_o)
    base = HD * first
    for h in range(first, first + 8):
        s, w = head_window(h)
        t = s - base
        mask = head_mask(h)
        q = q_r[:, s : s + w] * mask
        k = kv[:, s : s + w] * mask
        da = d_att[:, s : s + w] * mask
        scores = nt(k, q) * SCALE + bias
        shares = jnp.exp(scores - stat_t[h : h + 1, :])
        d_shares = nt(kv[:, D + s : D + s + w], da)
        ds = (shares * (d_shares - stat_t[HEADS + h : HEADS + h + 1, :])).astype(BF)
        dk_o[:, t : t + w] += nn(ds, q)
        dv_o[:, t : t + w] += nn(shares.astype(BF), da)
        dq_o[:, t : t + w] += tn(ds, k)


def query_backward_kernel(meta, q_r, d_att, stat, *refs):
    got, dq_o = refs[:8], refs[8]
    dq_o[...] = jnp.zeros_like(dq_o)
    mid = mid_bias(meta)
    for g in range(4):
        s = group_window(g)
        mask = group_mask(g)
        k = mid_rows(got, s, 256)
        scores = nt(q_r[:, s : s + 256] * mask, k) * SCALE + mid
        shares = jnp.exp(scores - pick_mid_column(stat, 4 * g))
        d_shares = nt(d_att[:, s : s + 256] * mask, mid_rows(got, D + s, 256))
        ds = (shares * (d_shares - pick_mid_column(stat, HEADS + 4 * g))).astype(BF)
        dq_o[:, s : s + 256] += nn(ds, k) * mask.astype(F32)
    mask = far_mask()
    k = far_rows(got, 0, D)
    scores = nt(q_r[...] * mask, k) * SCALE + far_bias(meta)
    shares = jnp.exp(scores - pick_far_column(stat, 0))
    d_shares = nt(d_att[...] * mask, far_rows(got, D, D))
    ds = (shares * (d_shares - pick_far_column(stat, HEADS))).astype(BF)
    dq_o[...] += nn(ds, k) * mask.astype(F32)


def spread_mid(stat_t, row):
    return jnp.concatenate(
        [jnp.broadcast_to(stat_t[row + c : row + c + 1, :], (64, T)) for c in range(4)], axis=0
    )


def spread_far(stat_t, row):
    return jnp.concatenate(
        [
            jnp.broadcast_to(stat_t[row + far_head(b) : row + far_head(b) + 1, :], (16, T))
            for b in range(16)
        ],
        axis=0,
    )


def joined_stats(rows):
    x = rows.astype(F32).T
    return x[:32] + (x[32:64] + x[64:96])


def key_backward_kernel(meta, kv, *refs):
    got = refs[:8]
    dq_r, dq_1, dk_1, dv_1, dq_2, dk_2, dv_2, cot = refs[8:16]
    all_o, kept_o, sent_o, dk_s, dv_s = refs[16:]
    half = D // 2
    dk_s[:, :half] = dk_1[...]
    dk_s[:, half:] = dk_2[...]
    dv_s[:, :half] = dv_1[...]
    dv_s[:, half:] = dv_2[...]
    stat_t = joined_stats(mid_rows(got, 2 * D, 128))
    mid = mid_bias(meta)
    for g in range(4):
        s = group_window(g)
        mask = group_mask(g)
        mask_f = mask.astype(F32)
        q = mid_rows(got, s, 256)
        da = mid_rows(got, D + s, 256)
        scores = nt(kv[:, s : s + 256] * mask, q) * SCALE + mid
        shares = jnp.exp(scores - spread_mid(stat_t, 4 * g))
        d_shares = nt(kv[:, D + s : D + s + 256] * mask, da)
        ds = (shares * (d_shares - spread_mid(stat_t, HEADS + 4 * g))).astype(BF)
        dk_s[:, s : s + 256] += nn(ds, q) * mask_f
        dv_s[:, s : s + 256] += nn(shares.astype(BF), da) * mask_f
    stat_t = joined_stats(far_rows(got, 2 * D, 128))
    mask = far_mask()
    mask_f = mask.astype(F32)
    q = far_rows(got, 0, D)
    da = far_rows(got, D, D)
    scores = nt(kv[:, :D] * mask, q) * SCALE + far_bias(meta)
    shares = jnp.exp(scores - spread_far(stat_t, 0))
    d_shares = nt(kv[:, D:] * mask, da)
    ds = (shares * (d_shares - spread_far(stat_t, HEADS))).astype(BF)
    dk_s[...] += nn(ds, q) * mask_f
    dv_s[...] += nn(shares.astype(BF), da) * mask_f
    dq = jnp.concatenate([dq_1[...], dq_2[...]], axis=1) + dq_r[...]
    d_q = (dq * SCALE).astype(BF)
    d_k = (dk_s[...] * SCALE).astype(BF)
    d_v = dv_s[...].astype(BF)
    all_o[:, :D] = d_q
    all_o[:, D : 2 * D] = d_k
    all_o[:, 2 * D :] = d_v
    first = meta[5] == 0
    kept_o[:, :D] = jnp.where(first, d_q, d_v)
    kept_o[:, D:] = jnp.where(first, d_k, cot[...])
    sent_o[:, :D] = jnp.where(first, d_v, d_q)
    sent_o[:, D:] = jnp.where(first, cot[...], d_k)


def left_kernel(meta, norm_a, norm_b, att_a, att_b, left):
    left[0] = jnp.concatenate([norm_a[...], norm_b[...]], axis=0).T
    left[1] = left[0]

    @pl.when(meta[5] == 1)
    def _():
        left[1] = jnp.concatenate([att_a[...], att_b[...]], axis=0).T


def weight_grad_kernel(meta, own, other, left, keep_o, s1, s2, s3):
    for d, out in ((2, s2), (1, s1), (3, s3), (0, keep_o)):
        j = (meta[6] + d) & 3
        cols = pl.ds(pl.multiple_of(j * WIDE, 128), WIDE)
        right = jnp.concatenate([own[:, cols], other[:, cols]], axis=0)
        out[...] = nn(left[j >> 1], right).astype(out.dtype)


def token_grad_kernel(d_qkv, w_qkv, inp, gain, cot, tok_o, ext_o):
    d_normed = nt(d_qkv[...], w_qkv[...])
    unit, inv_std = norm_parts(inp[...])
    d_gain = jnp.sum(d_normed * unit, axis=0, keepdims=True)
    d_bias = jnp.sum(d_normed, axis=0, keepdims=True)
    ext_o[...] = two_parts(jnp.concatenate(
        [d_gain[:, :WIDE], d_gain[:, WIDE:], d_bias[:, :WIDE], d_bias[:, WIDE:],
         jnp.zeros((4, WIDE), F32)], axis=0))
    d_unit = d_normed * gain[...].reshape(1, D)
    mean_a = jnp.mean(d_unit, axis=1, keepdims=True)
    mean_b = jnp.mean(d_unit * unit, axis=1, keepdims=True)
    d_tok = cot[...].astype(F32) + inv_std * (d_unit - mean_a - unit * mean_b)
    tok_o[...] = nn(unsort_matrix(), d_tok.astype(BF)).astype(BF)


def two_parts(ext):
    hi = ext.astype(BF)
    return jnp.concatenate([hi, (ext - hi.astype(F32)).astype(BF)], axis=0)


def whole_of(rows):
    return rows[:8].astype(F32) + rows[8:].astype(F32)


def ring_total(meta, slot, own, got, pad):
    pad[meta[slot]] = own
    for d, piece in enumerate(got, 1):
        pad[(meta[slot] - d) & 3] = piece
    return (pad[0] + pad[1]) + (pad[2] + pad[3])


def add_a_kernel(meta, keep, r1, r2, r3, ext, keep_o, s1, s2, s3):
    rows = D // 4
    for d, out in ((2, s2), (1, s1), (3, s3), (0, keep_o)):
        at = pl.ds(pl.multiple_of(((meta[7] + d) & 3) * rows, 16), rows)
        total = keep[at, :] + (r1[at, :].astype(F32) + r2[at, :].astype(F32) + r3[at, :].astype(F32))
        if d == 0:
            out[...] = total
        else:
            out[:rows] = total.astype(BF)
            out[rows:] = ext[...]


def add_b_kernel(meta, keep, r1, r2, r3, ext, out, pad):
    rows = D // 4
    got = (r1, r2, r3)
    total = keep[...]
    for r in got:
        total = total + r[:rows].astype(F32)
    out[:rows] = total.astype(BF)
    sums = ring_total(meta, 7, whole_of(ext[...]), [whole_of(r[rows:]) for r in got], pad)
    out[rows:] = two_parts(sums)


def add_c_kernel(own, r1, r2, r3, out):
    rows = D // 4

    def total(a, b, c, d):
        return (a + c) + (b + d)

    out[:rows] = total(*[r[:rows].astype(F32) for r in (own, r1, r2, r3)]).astype(BF)
    out[rows:] = two_parts(total(*[whole_of(r[rows:]) for r in (own, r1, r2, r3)]))


def merge_kernel(meta, own, r1, r2, r3, out):
    rows = D // 4
    out[D:] = own[rows:]
    for d, piece in enumerate((own, r1, r2, r3)):
        at = pl.ds(pl.multiple_of(((meta[7] - d) & 3) * rows, 16), rows)
        out[at, :] = piece[:rows]


def finish_kernel(meta, *refs, marks, first, last):
    count = len(marks)
    pieces, refs = refs[:count], refs[count:]
    if last:
        tails, refs = refs[:8], refs[8:]
    if not first:
        refs = refs[2:]
    qkv_o, out_o, *refs = refs
    if last:
        gain_o, bias_o, *refs = refs
    sems, wide = refs[0], refs[1 : 1 + count]
    for n, (piece, (core, turn, row)) in enumerate(zip(pieces, marks)):
        chunk = (meta[5] ^ core) * 4 + ((meta[9 if core else 6] - turn) & 3)
        size = wide[n].shape[0]
        wide[n][...] = piece[:size].astype(F32)

        @pl.when(chunk < 6)
        def _(n=n, chunk=chunk, row=row, size=size):
            at = pl.ds(pl.multiple_of(chunk * WIDE, 128), WIDE)
            to = qkv_o.at[pl.ds(row, size), at]
            pltpu.make_async_copy(wide[n], to, sems.at[n]).start()

        @pl.when(chunk >= 6)
        def _(n=n, chunk=chunk, row=row, size=size):
            at = pl.ds(pl.multiple_of((chunk - 6) * WIDE, 128), WIDE)
            to = out_o.at[pl.ds(row, size), at]
            pltpu.make_async_copy(wide[n], to, sems.at[n]).start()

    if last:
        pad = refs[1 + count]
        for n, tail in enumerate(tails):
            core = n // 4
            place = (meta[9 if core else 6] - n % 4) & 3
            pad[(meta[5] ^ core) * 4 + place] = whole_of(tail[...])
        total = pad[0]
        for n in range(1, 8):
            total = total + pad[n]
        gain_o[...] = jnp.concatenate([total[0:1], total[1:2]], axis=1).reshape(D)
        bias_o[...] = jnp.concatenate([total[2:3], total[3:4]], axis=1).reshape(D)
    for n in range(count):
        to = qkv_o.at[pl.ds(0, wide[n].shape[0]), pl.ds(0, WIDE)]
        pltpu.make_async_copy(wide[n], to, sems.at[n]).wait()


def finish(meta, pieces, outs, tails=None):
    first, last = outs is None, tails is not None
    marks = tuple(piece[1:] for piece in pieces)
    arrays = [piece[0] for piece in pieces]
    smem = pl.BlockSpec(memory_space=pltpu.SMEM)
    anywhere = pl.BlockSpec(memory_space=pl.ANY)
    whole = pl.BlockSpec(memory_space=pltpu.VMEM)
    args = [meta, *arrays]
    in_specs = [smem] + [whole] * len(arrays)
    if last:
        args += tails
        for tail in tails:
            index = (tail.shape[0] // 16 - 1, 0)
            in_specs.append(pl.BlockSpec((16, WIDE), lambda i, index=index: index))
    aliases = {}
    if not first:
        aliases = {len(args): 0, len(args) + 1: 1}
        args += list(outs)
        in_specs += [anywhere] * 2
    out_shape = [jax.ShapeDtypeStruct((D, 3 * D), F32), jax.ShapeDtypeStruct((D, D), F32)]
    out_specs = [anywhere] * 2
    scratch = [pltpu.SemaphoreType.DMA((len(pieces),))]
    for array in arrays:
        scratch.append(pltpu.VMEM((array.shape[0] // WIDE * WIDE, WIDE), F32))
    if last:
        out_shape += [jax.ShapeDtypeStruct((D,), F32)] * 2
        out_specs += [pl.BlockSpec((D,), lambda i: (0,))] * 2
        scratch += [pltpu.VMEM((8, 8, WIDE), F32)]
    return pl.pallas_call(
        functools.partial(finish_kernel, marks=marks, first=first, last=last),
        grid=(1,),
        in_specs=in_specs,
        out_specs=out_specs,
        out_shape=out_shape,
        scratch_shapes=scratch,
        input_output_aliases=aliases,
        compiler_params=pltpu.CompilerParams(vmem_limit_bytes=24 << 20),
        name="finish",
    )(*args)


def call(kernel, outs, *args, smem=0, scratch=(), name=None, limit=24, windows=None,
         anywhere=()):
    specs = [pl.BlockSpec(memory_space=pltpu.SMEM)] * smem
    specs += [pl.BlockSpec(memory_space=pltpu.VMEM)] * (len(args) - smem)
    for n in anywhere:
        specs[n] = pl.BlockSpec(memory_space=pl.ANY)
    for n, (shape, index) in (windows or {}).items():
        specs[n] = pl.BlockSpec(shape, lambda i, index=index: index)
    return pl.pallas_call(
        kernel,
        grid=(1,) if windows else (),
        out_shape=[jax.ShapeDtypeStruct(shape, dtype) for shape, dtype in outs],
        in_specs=specs,
        out_specs=[pl.BlockSpec(memory_space=pltpu.VMEM)] * len(outs),
        scratch_shapes=scratch,
        compiler_params=pltpu.CompilerParams(vmem_limit_bytes=limit << 20),
        name=name,
    )(*args)


def swap_seq(block, code):
    return lax.ppermute(block, "seq", [(i, i ^ code) for i in range(16)])


def z_send(block):
    def shift(d):
        return lax.ppermute(block, "seq", [(i, (i + 4 * d) % 16) for i in range(16)])

    got = {d: shift(d) for d in (2, 1, 3)}
    return [got[1], got[2], got[3]]


def after(*values):
    return lax.optimization_barrier(values)


def join(*blocks):
    return jnp.concatenate(blocks, axis=0)


def decode(i):
    dp, seq = i // 16, i % 16
    return [dp // 2, (seq // 2) % 2 * 2 + dp % 2, seq // 4, seq % 2]


def encode(x, y, z, core):
    return (x * 2 + y % 2) * 16 + z * 4 + y // 2 * 2 + core


def ring_route(stage, d):
    route = []
    for i in range(128):
        place = decode(i)
        axis = (stage + place[3]) % 3
        place[axis] = (place[axis] + d) % 4
        route.append((i, encode(*place)))
    return route


def hop(block, stage, d):
    return lax.ppermute(block, AXES, ring_route(stage, d))


def ring_send(blocks, stage):
    got = {d: hop(blocks[d - 1], stage, d) for d in (2, 1, 3)}
    return got[1], got[2], got[3]


def place_meta(lengths):
    dp = lax.axis_index("dp").astype(jnp.int32)
    seq = lax.axis_index("seq").astype(jnp.int32)
    core = seq & 1
    coords = [dp >> 1, (seq & 2) + (dp & 1), seq >> 2]
    turns = [jnp.where(core == 0, coords[n], coords[(n + 1) % 3]) for n in range(3)]
    other = jnp.where(core == 0, coords[1], coords[0])
    values = jnp.stack([core] + turns + [other])
    return jnp.concatenate([seq[None], lengths, values, jnp.zeros((6,), jnp.int32)])


def sum_everywhere(meta, keep, sends, ext, beside):
    cut = D // 4
    got = ring_send(sends, 0)
    *got, _ = after(*got, beside)
    keep, *sends = call(
        add_a_kernel,
        [((cut, WIDE), F32)] + [((cut + 16, WIDE), BF)] * 3,
        meta, keep, *got, ext, smem=1, name="add_a",
    )
    got = ring_send(sends, 1)
    block = call(
        add_b_kernel, [((cut + 16, WIDE), BF)],
        meta, keep, *got, ext, smem=1, name="add_b", scratch=[pltpu.VMEM((4, 8, WIDE), F32)],
    )[0]
    got = ring_send([block] * 3, 2)
    block = call(add_c_kernel, [((cut + 16, WIDE), BF)], block, *got, name="add_c")[0]
    got = ring_send([block] * 3, 1)
    block = call(
        merge_kernel, [((D + 16, WIDE), BF)], meta, block, *got, smem=1, name="merge_b",
    )[0]
    ring = [block, *ring_send([block] * 3, 0)]
    twin = [swap_seq(block, 1)]
    outs = finish(meta, [(block, 0, 0, 0), (twin[0], 1, 0, 0)], None)
    ring[2], first = after(ring[2], outs[0])
    twin += [None, swap_seq(ring[2], 1), None]
    outs = finish(meta, [(ring[2], 0, 2, 0)], (first, outs[1]))
    ring[1], ring[3], *outs = after(ring[1], ring[3], *outs)
    twin[1], twin[3] = swap_seq(ring[1], 1), swap_seq(ring[3], 1)
    outs = finish(meta, [(ring[1], 0, 1, 0), (ring[3], 0, 3, 0), (twin[2], 1, 2, 0)], outs)
    return finish(meta, [(twin[1], 1, 1, 0), (twin[3], 1, 3, 0)], outs, ring + twin)


def position_table():
    quarter = D // 4
    frequency = 1.0 / 10000.0 ** (np.arange(quarter) / quarter)
    angle = np.arange(256)[:, None] * frequency[None, :]
    exact_values = np.concatenate([np.sin(angle), np.cos(angle)], axis=1).astype(np.float32)
    parts = []
    rest = exact_values
    for _ in range(3):
        part = rest.astype(jnp.bfloat16)
        parts.append(part)
        rest = rest - part.astype(np.float32)
    return np.concatenate(parts, axis=1)


def per_device(tokens, tile_coords, slide_lengths, norm_gain, norm_bias, w_qkv, w_out, cotangent):
    meta = place_meta(slide_lengths[0])
    table = jnp.asarray(position_table())
    inp, normed, kv, kv_pack = call(
        key_kernel,
        [((T, D), F32), ((T, D), BF), ((T, 2 * D), BF), ((80, 2 * D), BF)],
        tokens[0], tile_coords[0], table, norm_gain, norm_bias, w_qkv, name="keys", limit=60,
        anywhere=(0, 2, 5),
        scratch=[
            pltpu.VMEM((T, D), BF), pltpu.VMEM((T, 3 * D // 2), BF), pltpu.VMEM((2, D, D), BF),
            pltpu.SemaphoreType.DMA((4,)),
        ],
    )
    from_y = swap_seq(kv_pack, 2)
    norm_b = swap_seq(normed, 1)
    q, d_att, cot, qd_pack = call(
        query_kernel,
        [((T, D), BF), ((T, D), BF), ((T, D), BF), ((80, 2 * D), BF)],
        normed, w_qkv, w_out, cotangent[0], name="queries", limit=60,
        windows={1: ((D, D), (0, 0))},
    )
    from_y, q, norm_b = after(from_y, q, norm_b)
    far = join(kv_pack[64:], from_y[64:])
    from_z = z_send(far)
    far, q = after(far, q)
    part = join(kv_pack[:64], from_y[:64], far)
    twin = swap_seq(part, 1)
    tops = [
        call(
            functools.partial(local_forward_kernel, first=first),
            [((T, D // 2), F32), ((T, 128), F32), ((T, 128), F32)],
            meta, q, kv, smem=1, name="local_forward",
        )
        for first in (0, 8)
    ]
    *from_z, twin, _, _ = after(*from_z, twin, tops[0][0], tops[1][0])
    got_kv = (part, *from_z, twin, *[swap_seq(rows, 1) for rows in from_z])
    att, stat, pack = call(
        remote_forward_kernel,
        [((T, D), BF), ((T, 128), F32), ((80, 2 * D + 128), BF)],
        meta, q, *got_kv, *tops[0], *tops[1], d_att, qd_pack,
        smem=1, name="remote_forward",
    )
    from_y = swap_seq(pack, 2)
    att_b = swap_seq(att, 1)
    grads_1 = call(
        functools.partial(local_backward_kernel, first=0),
        [((T, D // 2), F32)] * 3,
        meta, q, kv, d_att, stat, smem=1, name="local_backward",
    )
    dq_r = call(
        query_backward_kernel, [((T, D), F32)],
        meta, q, d_att, stat, *got_kv, smem=1, name="query_backward",
    )[0]
    from_y, att_b, dq_r, *grads_1 = after(from_y, att_b, dq_r, *grads_1)
    far = join(pack[64:], from_y[64:])
    from_z = z_send(far)
    far, q = after(far, q)
    part = join(pack[:64], from_y[:64], far)
    twin = swap_seq(part, 1)
    grads_2 = call(
        functools.partial(local_backward_kernel, first=8),
        [((T, D // 2), F32)] * 3,
        meta, q, kv, d_att, stat, smem=1, name="local_backward",
    )
    *from_z, twin, _ = after(*from_z, twin, grads_2[0])
    got_qd = (part, *from_z, twin, *[swap_seq(rows, 1) for rows in from_z])
    d_qkv, own, sent = call(
        key_backward_kernel,
        [((T, 3 * D), BF), ((T, 2 * D), BF), ((T, 2 * D), BF)],
        meta, kv, *got_qd, dq_r, *grads_1, *grads_2, cot,
        smem=1, name="key_backward",
        scratch=[pltpu.VMEM((T, D), F32), pltpu.VMEM((T, D), F32)],
    )
    left = call(
        left_kernel, [((2, D, 2 * T), BF)],
        meta, normed, norm_b, att, att_b, smem=1, name="left",
    )[0]
    other, left = after(swap_seq(sent, 1), left)
    keep, *sends = call(
        weight_grad_kernel,
        [((D, WIDE), F32)] + [((D, WIDE), BF)] * 3,
        meta, own, other, left, smem=1, name="weight_grad",
    )
    d_tokens, ext = call(
        token_grad_kernel,
        [((T, D), BF), ((16, WIDE), BF)],
        d_qkv, w_qkv, inp, norm_gain, cot, name="token_grad",
    )
    att, _ = after(att, keep)
    layer_out = call(out_kernel, [((T, D), BF)], att, inp, w_out, name="layer_out")[0]
    dw_qkv, dw_out, d_gain, d_bias = sum_everywhere(meta, keep, sends, ext, layer_out)
    return (
        layer_out[None],
        d_tokens[None],
        dw_qkv,
        dw_out,
        d_gain,
        d_bias,
    )


def solution(mesh):
    return jax.shard_map(
        per_device,
        mesh=mesh,
        in_specs=(
            P("dp", "seq", None),
            P("dp", None, "seq"),
            P("dp", None),
            P(),
            P(),
            P(),
            P(),
            P("dp", "seq", None),
        ),
        out_specs=(P("dp", "seq", None), P("dp", "seq", None), P(), P(), P(), P()),
        check_vma=False,
    )
```

```python
import functools

import jax
import jax.numpy as jnp
import numpy as np
from jax import lax
from jax.experimental import pallas as pl
from jax.experimental.pallas import tpu as pltpu
from jax.sharding import PartitionSpec as P

HEADS = 16
HD = 48
D = 768
T = 256
SCALE = HD ** (-0.5)
NEG = -1e30
BF = jnp.bfloat16
F32 = jnp.float32
AXES = ("dp", "seq")
WIDE = 384
ROWS = 192


def iota(shape, dim):
    return lax.broadcasted_iota(jnp.int32, shape, dim)


def tile_of(i):
    return (i >> 6) + ((i >> 4) & 3) * 4 + (i & 15) * 16


def nt(a, b):
    return lax.dot_general(a, b, (((1,), (1,)), ((), ())), preferred_element_type=F32)


def nn(a, b):
    return lax.dot_general(a, b, (((1,), (0,)), ((), ())), preferred_element_type=F32)


def tn(a, b):
    return lax.dot_general(a, b, (((0,), (0,)), ((), ())), preferred_element_type=F32)


def exact(a, b):
    hi = a.astype(BF)
    rest = a - hi.astype(F32)
    mid = rest.astype(BF)
    low = (rest - mid.astype(F32)).astype(BF)
    return nn(hi, b) + nn(mid, b) + nn(low, b)


def sort_matrix():
    return jnp.where(tile_of(iota((T, T), 0)) == iota((T, T), 1), 1.0, 0.0).astype(BF)


def unsort_matrix():
    return jnp.where(iota((T, T), 0) == tile_of(iota((T, T), 1)), 1.0, 0.0).astype(BF)


def span_mask(lo, shape):
    lane = iota(shape, 1)
    return jnp.where((lane >= lo) & (lane < lo + HD), 1.0, 0.0)


def head_window(h):
    start = HD * h // 128 * 128
    width = 128 if HD * h - start + HD <= 128 else 256
    return start, width


def head_mask(h):
    start, width = head_window(h)
    return span_mask(HD * h - start, (1, width)).astype(BF)


def group_window(g):
    return 192 * g // 128 * 128


def group_mask(g):
    lo = 192 * g - group_window(g) + HD * (iota((T, 256), 0) >> 6)
    return span_mask(lo, (T, 256)).astype(BF)


def far_mask():
    row = iota((T, D), 0)
    lo = HD * ((row >> 6) + 4 * ((row >> 4) & 3))
    return span_mask(lo, (T, D)).astype(BF)


def slide_of(meta, pos):
    end = meta[1]
    out = jnp.where(pos >= end, 1, 0)
    for n in range(2, 5):
        end = end + meta[n]
        out = out + jnp.where(pos >= end, 1, 0)
    return out


def row_ids(meta):
    return slide_of(meta, meta[0] * T + tile_of(iota((T, 1), 0)))


def bias_of(meta, pos):
    return jnp.where(row_ids(meta) == slide_of(meta, pos), 0.0, NEG)


def local_bias(meta):
    return bias_of(meta, meta[0] * T + tile_of(iota((1, T), 1)))


def mid_bias(meta):
    t = iota((T, T), 1)
    slot = t >> 6
    dev = meta[0] ^ (((slot & 1) << 1) | (slot >> 1))
    pos = dev * T + ((t >> 4) & 3) * 4 + (t & 15) * 16 + (iota((T, T), 0) >> 6)
    return bias_of(meta, pos)


def far_bias(meta):
    t = iota((T, T), 1)
    s = t >> 4
    place = (((meta[0] >> 2) - (s >> 1)) & 3) * 4 + ((meta[0] & 3) ^ ((s & 1) << 1) ^ (s >> 3))
    row = iota((T, T), 0)
    pos = place * T + (t & 15) * 16 + (row >> 6) + 4 * ((row >> 4) & 3)
    return bias_of(meta, pos)


def far_head(b):
    return b // 4 + 4 * (b % 4)


def fold_mid(x, masks):
    out = x[0:64] * masks[0]
    for c in range(1, 4):
        out = out + x[64 * c : 64 * c + 64] * masks[c]
    return out


def fold_far(x, masks):
    out = x[0:16] * masks[0]
    for b in range(1, 16):
        out = out + x[16 * b : 16 * b + 16] * masks[far_head(b)]
    return out


def pack_rows(x, head_masks):
    mids = [
        head_masks[c] + head_masks[4 + c] + head_masks[8 + c] + head_masks[12 + c]
        for c in range(4)
    ]
    return jnp.concatenate([fold_mid(x, mids), fold_far(x, head_masks)], axis=0)


def norm_parts(inputs):
    mean = jnp.mean(inputs, axis=1, keepdims=True)
    centred = inputs - mean
    var = jnp.mean(centred * centred, axis=1, keepdims=True)
    inv_std = lax.rsqrt(var + 1e-05)
    return centred * inv_std, inv_std


def pack_masks():
    return [span_mask(HD * h, (1, D)).astype(BF) for h in range(HEADS)]


def key_kernel(tok_h, coords, table_h, gain, bias, w_h, inp_o, norm_o, kv_o, pack_o,
               tok, table, weight, sems):
    copies = [
        pltpu.make_async_copy(tok_h, tok, sems.at[0]),
        pltpu.make_async_copy(table_h, table, sems.at[1]),
        pltpu.make_async_copy(w_h.at[:, pl.ds(D, D)], weight.at[0], sems.at[2]),
        pltpu.make_async_copy(w_h.at[:, pl.ds(2 * D, D)], weight.at[1], sems.at[3]),
    ]
    for copy in copies:
        copy.start()
    sort = sort_matrix()
    grid = iota((T, T), 0)
    hots = []
    for axis in range(2):
        hot = jnp.where(grid == coords[axis : axis + 1, :], 1.0, 0.0).astype(BF)
        hots.append(nt(sort, hot).astype(BF))
    copies[0].wait()
    tok_s = nn(sort, tok[...])
    copies[1].wait()
    parts = []
    for hot in hots:
        found = nn(hot, table[...])
        parts.append(found[:, :384] + found[:, 384:768] + found[:, 768:])
    inputs = tok_s + jnp.concatenate(parts, axis=1)
    inp_o[...] = inputs
    unit, _ = norm_parts(inputs)
    normed = (unit * gain[...].reshape(1, D) + bias[...].reshape(1, D)).astype(BF)
    norm_o[...] = normed
    masks = pack_masks()
    for n in range(2):
        copies[2 + n].wait()
        part = nn(normed, weight[n]).astype(BF)
        kv_o[:, D * n : D * (n + 1)] = part
        pack_o[:, D * n : D * (n + 1)] = pack_rows(part, masks)


def query_kernel(normed, w_qkv, w_out, cot, q_o, da_o, cot_o, pack_o):
    cot_s = nn(sort_matrix(), cot[...]).astype(BF)
    cot_o[...] = cot_s
    q = nn(normed[...], w_qkv[...]).astype(BF)
    q_o[...] = q
    d_att = nt(cot_s, w_out[...]).astype(BF)
    da_o[...] = d_att
    masks = pack_masks()
    pack_o[:, :D] = pack_rows(q, masks)
    pack_o[:, D:] = pack_rows(d_att, masks)


def soft(scores):
    top = jnp.max(scores, axis=1, keepdims=True)
    shares = jnp.exp(scores - top)
    return top, jnp.sum(shares, axis=1, keepdims=True), shares.astype(BF)


def local_forward_kernel(meta, q_r, kv, o_o, top_o, sum_o, *, first):
    bias = local_bias(meta)
    o_o[...] = jnp.zeros_like(o_o)
    lane = iota((T, 128), 1)
    tops = jnp.full((T, 128), NEG, F32)
    sums = jnp.zeros((T, 128), F32)
    base = HD * first
    for h in range(first, first + 8):
        s, w = head_window(h)
        mask = head_mask(h)
        scores = nt(q_r[:, s : s + w] * mask, kv[:, s : s + w]) * SCALE + bias
        top, total, shares = soft(scores)
        tops = jnp.where(lane == h, top, tops)
        sums = jnp.where(lane == h, total, sums)
        o_o[:, s - base : s - base + w] += nn(shares, kv[:, D + s : D + s + w] * mask)
    top_o[...] = tops
    sum_o[...] = sums


def mid_rows(got, lo, width):
    return jnp.concatenate([got[0][:128, lo : lo + width], got[4][:128, lo : lo + width]], axis=0)


def far_rows(got, lo, width):
    at = slice(lo, lo + width)
    rows = []
    for n in (0, 4):
        rows.append(got[n][128:, at])
        rows += [got[n + d][:, at] for d in (1, 2, 3)]
    return jnp.concatenate(rows, axis=0)


def expand_matrix():
    head = iota((128, D), 0)
    lane = iota((128, D), 1)
    return jnp.where((lane >= head * HD) & (lane < head * HD + HD), 1.0, 0.0).astype(BF)


def gather_matrix():
    lane = iota((D, 128), 0)
    head = iota((D, 128), 1)
    return jnp.where((lane >= head * HD) & (lane < head * HD + HD), 1.0, 0.0).astype(BF)


def remote_forward_kernel(meta, q_r, *refs):
    got = refs[:8]
    o_1, top_1, sum_1, o_2, top_2, sum_2, d_att, pack, att_o, stat_o, send_o = refs[8:]
    lane = iota((T, 128), 1)
    row = iota((T, 128), 0)
    top_l = jnp.where(lane < 8, top_1[...], top_2[...])
    sum_l = jnp.where(lane < 8, sum_1[...], sum_2[...])
    tops_m = jnp.full((T, 128), NEG, F32)
    sums_m = jnp.zeros((T, 128), F32)
    mid = mid_bias(meta)
    mid_parts = []
    for g in range(4):
        s = group_window(g)
        mask = group_mask(g)
        q = q_r[:, s : s + 256] * mask
        scores = nt(q, mid_rows(got, s, 256)) * SCALE + mid
        top, total, shares = soft(scores)
        here = lane == 4 * g + (row >> 6)
        tops_m = jnp.where(here, top, tops_m)
        sums_m = jnp.where(here, total, sums_m)
        mid_parts.append(nn(shares, mid_rows(got, D + s, 256)))
    mask = far_mask()
    scores = nt(q_r[...] * mask, far_rows(got, 0, D)) * SCALE + far_bias(meta)
    top, total, shares = soft(scores)
    far_part = nn(shares, far_rows(got, D, D))
    here = lane == (row >> 6) + 4 * ((row >> 4) & 3)
    tops_f = jnp.where(here, top, NEG)
    sums_f = jnp.where(here, total, 0.0)
    highest = jnp.maximum(jnp.maximum(top_l, tops_m), tops_f)
    f_l = jnp.exp(top_l - highest)
    f_m = jnp.exp(tops_m - highest)
    f_f = jnp.exp(tops_f - highest)
    totals = f_l * sum_l + f_m * sums_m + f_f * sums_f
    totals = jnp.where(lane < HEADS, totals, 1.0)
    inverse = 1.0 / totals
    lse = highest + jnp.log(totals)
    w_m = f_m * inverse
    o_l = jnp.concatenate([o_1[...], o_2[...]], axis=1)
    att = o_l * exact(f_l * inverse, expand_matrix())
    w_f = jnp.sum(jnp.where(here, f_f * inverse, 0.0), axis=1, keepdims=True)
    att = att + far_part * w_f * mask.astype(F32)
    acc = [att[:, 128 * n : 128 * n + 128] for n in range(6)]
    for g in range(4):
        n = group_window(g) // 128
        w_g = jnp.sum(jnp.where(lane == 4 * g + (row >> 6), w_m, 0.0), axis=1, keepdims=True)
        add = mid_parts[g] * w_g * group_mask(g).astype(F32)
        acc[n] = acc[n] + add[:, :128]
        acc[n + 1] = acc[n + 1] + add[:, 128:]
    att = jnp.concatenate(acc, axis=1).astype(BF)
    att_o[...] = att
    prod = d_att[...].astype(F32) * att.astype(F32)
    delta = exact(prod, gather_matrix())
    stat = jnp.where(lane < HEADS, lse, pltpu.roll(delta, HEADS, 1))
    stat = jnp.where(lane < 2 * HEADS, stat, 0.0)
    stat_o[...] = stat
    one = iota((1, 128), 1)
    send_o[:, : 2 * D] = pack[...]
    mids = fold_mid(stat, [jnp.where((one & 3) == c, 1.0, 0.0) for c in range(4)])
    fars = fold_far(stat, [jnp.where((one & 15) == h, 1.0, 0.0) for h in range(HEADS)])
    send_o[:, 2 * D :] = three_parts(jnp.concatenate([mids, fars], axis=0))


def three_parts(x):
    lane = iota(x.shape, 1)
    hi = x.astype(BF).astype(F32)
    mid = (x - hi).astype(BF).astype(F32)
    low = x - hi - mid
    parts = jnp.where(lane < 64, pltpu.roll(mid, 32, 1), pltpu.roll(low, 64, 1))
    return jnp.where(lane < 32, hi, parts).astype(BF)


def out_kernel(att, inp, w_out, out_o):
    layer = (inp[...] + nn(att[...], w_out[...])).astype(BF)
    out_o[...] = nn(unsort_matrix(), layer).astype(BF)


def pick_mid_column(stat, col):
    return jnp.concatenate(
        [stat[64 * c : 64 * c + 64, col + c : col + c + 1] for c in range(4)], axis=0
    )


def pick_far_column(stat, col):
    return jnp.concatenate(
        [
            stat[16 * b : 16 * b + 16, col + far_head(b) : col + far_head(b) + 1]
            for b in range(16)
        ],
        axis=0,
    )


def local_backward_kernel(meta, q_r, kv, d_att, stat, dq_o, dk_o, dv_o, *, first):
    bias = local_bias(meta)
    stat_t = stat[...].T
    dq_o[...] = jnp.zeros_like(dq_o)
    dk_o[...] = jnp.zeros_like(dk_o)
    dv_o[...] = jnp.zeros_like(dv_o)
    base = HD * first
    for h in range(first, first + 8):
        s, w = head_window(h)
        t = s - base
        mask = head_mask(h)
        q = q_r[:, s : s + w] * mask
        k = kv[:, s : s + w] * mask
        da = d_att[:, s : s + w] * mask
        scores = nt(k, q) * SCALE + bias
        shares = jnp.exp(scores - stat_t[h : h + 1, :])
        d_shares = nt(kv[:, D + s : D + s + w], da)
        ds = (shares * (d_shares - stat_t[HEADS + h : HEADS + h + 1, :])).astype(BF)
        dk_o[:, t : t + w] += nn(ds, q)
        dv_o[:, t : t + w] += nn(shares.astype(BF), da)
        dq_o[:, t : t + w] += tn(ds, k)


def query_backward_kernel(meta, q_r, d_att, stat, *refs):
    got, dq_o = refs[:8], refs[8]
    dq_o[...] = jnp.zeros_like(dq_o)
    mid = mid_bias(meta)
    for g in range(4):
        s = group_window(g)
        mask = group_mask(g)
        k = mid_rows(got, s, 256)
        scores = nt(q_r[:, s : s + 256] * mask, k) * SCALE + mid
        shares = jnp.exp(scores - pick_mid_column(stat, 4 * g))
        d_shares = nt(d_att[:, s : s + 256] * mask, mid_rows(got, D + s, 256))
        ds = (shares * (d_shares - pick_mid_column(stat, HEADS + 4 * g))).astype(BF)
        dq_o[:, s : s + 256] += nn(ds, k) * mask.astype(F32)
    mask = far_mask()
    k = far_rows(got, 0, D)
    scores = nt(q_r[...] * mask, k) * SCALE + far_bias(meta)
    shares = jnp.exp(scores - pick_far_column(stat, 0))
    d_shares = nt(d_att[...] * mask, far_rows(got, D, D))
    ds = (shares * (d_shares - pick_far_column(stat, HEADS))).astype(BF)
    dq_o[...] += nn(ds, k) * mask.astype(F32)


def spread_mid(stat_t, row):
    return jnp.concatenate(
        [jnp.broadcast_to(stat_t[row + c : row + c + 1, :], (64, T)) for c in range(4)], axis=0
    )


def spread_far(stat_t, row):
    return jnp.concatenate(
        [
            jnp.broadcast_to(stat_t[row + far_head(b) : row + far_head(b) + 1, :], (16, T))
            for b in range(16)
        ],
        axis=0,
    )


def joined_stats(rows):
    x = rows.astype(F32).T
    return x[:32] + (x[32:64] + x[64:96])


def key_backward_kernel(meta, kv, *refs):
    got = refs[:8]
    dq_r, dq_1, dk_1, dv_1, dq_2, dk_2, dv_2, cot = refs[8:16]
    all_o, kept_o, sent_o, dk_s, dv_s = refs[16:]
    half = D // 2
    dk_s[:, :half] = dk_1[...]
    dk_s[:, half:] = dk_2[...]
    dv_s[:, :half] = dv_1[...]
    dv_s[:, half:] = dv_2[...]
    stat_t = joined_stats(mid_rows(got, 2 * D, 128))
    mid = mid_bias(meta)
    for g in range(4):
        s = group_window(g)
        mask = group_mask(g)
        mask_f = mask.astype(F32)
        q = mid_rows(got, s, 256)
        da = mid_rows(got, D + s, 256)
        scores = nt(kv[:, s : s + 256] * mask, q) * SCALE + mid
        shares = jnp.exp(scores - spread_mid(stat_t, 4 * g))
        d_shares = nt(kv[:, D + s : D + s + 256] * mask, da)
        ds = (shares * (d_shares - spread_mid(stat_t, HEADS + 4 * g))).astype(BF)
        dk_s[:, s : s + 256] += nn(ds, q) * mask_f
        dv_s[:, s : s + 256] += nn(shares.astype(BF), da) * mask_f
    stat_t = joined_stats(far_rows(got, 2 * D, 128))
    mask = far_mask()
    mask_f = mask.astype(F32)
    q = far_rows(got, 0, D)
    da = far_rows(got, D, D)
    scores = nt(kv[:, :D] * mask, q) * SCALE + far_bias(meta)
    shares = jnp.exp(scores - spread_far(stat_t, 0))
    d_shares = nt(kv[:, D:] * mask, da)
    ds = (shares * (d_shares - spread_far(stat_t, HEADS))).astype(BF)
    dk_s[...] += nn(ds, q) * mask_f
    dv_s[...] += nn(shares.astype(BF), da) * mask_f
    dq = jnp.concatenate([dq_1[...], dq_2[...]], axis=1) + dq_r[...]
    d_q = (dq * SCALE).astype(BF)
    d_k = (dk_s[...] * SCALE).astype(BF)
    d_v = dv_s[...].astype(BF)
    all_o[:, :D] = d_q
    all_o[:, D : 2 * D] = d_k
    all_o[:, 2 * D :] = d_v
    first = meta[5] == 0
    kept_o[:, :D] = jnp.where(first, d_q, cot[...])
    kept_o[:, D:] = jnp.where(first, d_k, d_v)
    sent_o[:, :D] = jnp.where(first, cot[...], d_q)
    sent_o[:, D:] = jnp.where(first, d_v, d_k)


def left_kernel(meta, norm_a, norm_b, att_a, att_b, early, late):
    late[...] = jnp.concatenate([norm_a[...], norm_b[...]], axis=0).T
    early[...] = late[...]

    @pl.when(meta[5] == 1)
    def _():
        early[...] = jnp.concatenate([att_a[...], att_b[...]], axis=0).T


def weight_grad_kernel(meta, own, other, left_a, left_b, keep_o, s1, s2, s3):
    for d, out in ((2, s2), (1, s1), (3, s3), (0, keep_o)):
        at = pl.ds(pl.multiple_of(((meta[6] + d) & 3) * ROWS, 16), ROWS)
        for n, left in enumerate((left_a, left_b)):
            cols = slice(D * n, D * (n + 1))
            right = jnp.concatenate([own[:, cols], other[:, cols]], axis=0)
            out[:, cols] = nn(left[at, :], right).astype(out.dtype)


def token_grad_kernel(d_qkv, w_qkv, inp, gain, cot, tok_o, ext_o):
    d_normed = nt(d_qkv[...], w_qkv[...])
    unit, inv_std = norm_parts(inp[...])
    d_gain = jnp.sum(d_normed * unit, axis=0, keepdims=True)
    d_bias = jnp.sum(d_normed, axis=0, keepdims=True)
    ext_o[...] = two_parts(jnp.concatenate(
        [d_gain[:, :WIDE], d_gain[:, WIDE:], d_bias[:, :WIDE], d_bias[:, WIDE:],
         jnp.zeros((4, WIDE), F32)], axis=0))
    d_unit = d_normed * gain[...].reshape(1, D)
    mean_a = jnp.mean(d_unit, axis=1, keepdims=True)
    mean_b = jnp.mean(d_unit * unit, axis=1, keepdims=True)
    d_tok = cot[...].astype(F32) + inv_std * (d_unit - mean_a - unit * mean_b)
    tok_o[...] = nn(unsort_matrix(), d_tok.astype(BF)).astype(BF)


def two_parts(ext):
    hi = ext.astype(BF)
    return jnp.concatenate([hi, (ext - hi.astype(F32)).astype(BF)], axis=0)


def whole_of(rows):
    return rows[:8].astype(F32) + rows[8:].astype(F32)


def ring_total(meta, slot, own, got, pad):
    pad[meta[slot]] = own
    for d, piece in enumerate(got, 1):
        pad[(meta[slot] - d) & 3] = piece
    return (pad[0] + pad[1]) + (pad[2] + pad[3])


def add_a_kernel(meta, keep, r1, r2, r3, ext, keep_o, s1, s2, s3):
    for d, out in ((2, s2), (1, s1), (3, s3), (0, keep_o)):
        at = pl.ds(pl.multiple_of(((meta[7] + d) & 3) * WIDE, 128), WIDE)
        total = keep[:, at] + (r1[:, at].astype(F32) + r2[:, at].astype(F32) + r3[:, at].astype(F32))
        if d == 0:
            out[...] = total
        else:
            out[:ROWS] = total.astype(BF)
            out[ROWS:] = ext[...]


def add_b_kernel(meta, keep, r1, r2, r3, ext, out, pad):
    got = (r1, r2, r3)
    total = keep[...]
    for r in got:
        total = total + r[:ROWS].astype(F32)
    out[:ROWS] = total.astype(BF)
    sums = ring_total(meta, 7, whole_of(ext[...]), [whole_of(r[ROWS:]) for r in got], pad)
    out[ROWS:] = two_parts(sums)


def add_c_kernel(own, r1, r2, r3, out):
    def total(a, b, c, d):
        return (a + c) + (b + d)

    out[:ROWS] = total(*[r[:ROWS].astype(F32) for r in (own, r1, r2, r3)]).astype(BF)
    out[ROWS:] = two_parts(total(*[whole_of(r[ROWS:]) for r in (own, r1, r2, r3)]))


def stack_kernel(r1, r2, r3, out):
    for n, r in enumerate((r1, r2, r3)):
        out[ROWS * n : ROWS * (n + 1)] = r[:ROWS]


def finish_kernel(meta, *refs, marks, first, last):
    count = 1 + max(mark[0] for mark in marks)
    pieces, refs = refs[:count], refs[count:]
    if last:
        tails, refs = refs[:8], refs[8:]
    if not first:
        refs = refs[2:]
    qkv_o, out_o, *refs = refs
    if last:
        gain_o, bias_o, *refs = refs
    sems, wide = refs[:2]
    for n, (piece, start, core, turn, back) in enumerate(marks):
        wide[n] = pieces[piece][start : start + ROWS].astype(F32)
        row = pl.multiple_of(((meta[9 if core else 6] - turn) & 3) * ROWS, 8)
        quarter = (meta[10 if core else 7] - back) & 3
        second = (meta[5] ^ core) == 1

        @pl.when(jnp.logical_and(second, quarter < 2))
        def _(n=n, row=row, quarter=quarter):
            at = pl.ds(pl.multiple_of(quarter * WIDE, 128), WIDE)
            pltpu.make_async_copy(wide.at[n], out_o.at[pl.ds(row, ROWS), at], sems.at[n]).start()

        @pl.when(jnp.logical_not(jnp.logical_and(second, quarter < 2)))
        def _(n=n, row=row, quarter=quarter, second=second):
            at = jnp.where(second, quarter + 2, quarter) * WIDE
            at = pl.ds(pl.multiple_of(at, 128), WIDE)
            pltpu.make_async_copy(wide.at[n], qkv_o.at[pl.ds(row, ROWS), at], sems.at[n]).start()

    if last:
        pad = refs[2]
        for n, tail in enumerate(tails):
            core = n // 4
            place = (meta[9 if core else 6] - n % 4) & 3
            pad[(meta[5] ^ core) * 4 + place] = whole_of(tail[...])
        total = pad[0]
        for n in range(1, 8):
            total = total + pad[n]
        gain_o[...] = jnp.concatenate([total[0:1], total[1:2]], axis=1).reshape(D)
        bias_o[...] = jnp.concatenate([total[2:3], total[3:4]], axis=1).reshape(D)
    for n in range(len(marks)):
        to = qkv_o.at[pl.ds(0, ROWS), pl.ds(0, WIDE)]
        pltpu.make_async_copy(wide.at[n], to, sems.at[n]).wait()


def finish(meta, pieces, outs, tails=None):
    first, last = outs is None, tails is not None
    marks = []
    for n, (array, core, turn) in enumerate(pieces):
        if array.shape[0] == 3 * ROWS:
            marks += [(n, ROWS * (back - 1), core, turn, back) for back in (1, 2, 3)]
        else:
            marks.append((n, 0, core, turn, 0))
    smem = pl.BlockSpec(memory_space=pltpu.SMEM)
    anywhere = pl.BlockSpec(memory_space=pl.ANY)
    whole = pl.BlockSpec(memory_space=pltpu.VMEM)
    args = [meta] + [piece[0] for piece in pieces]
    in_specs = [smem] + [whole] * len(pieces)
    if last:
        args += tails
        in_specs += [pl.BlockSpec((16, WIDE), lambda i: (ROWS // 16, 0))] * 8
    aliases = {}
    if not first:
        aliases = {len(args): 0, len(args) + 1: 1}
        args += list(outs)
        in_specs += [anywhere] * 2
    out_shape = [jax.ShapeDtypeStruct((D, 3 * D), F32), jax.ShapeDtypeStruct((D, D), F32)]
    out_specs = [anywhere] * 2
    scratch = [
        pltpu.SemaphoreType.DMA((len(marks),)), pltpu.VMEM((len(marks), ROWS, WIDE), F32),
    ]
    if last:
        out_shape += [jax.ShapeDtypeStruct((D,), F32)] * 2
        out_specs += [pl.BlockSpec((D,), lambda i: (0,))] * 2
        scratch += [pltpu.VMEM((8, 8, WIDE), F32)]
    return pl.pallas_call(
        functools.partial(finish_kernel, marks=tuple(marks), first=first, last=last),
        grid=(1,),
        in_specs=in_specs,
        out_specs=out_specs,
        out_shape=out_shape,
        scratch_shapes=scratch,
        input_output_aliases=aliases,
        compiler_params=pltpu.CompilerParams(vmem_limit_bytes=24 << 20),
        name="finish",
    )(*args)


def call(kernel, outs, *args, smem=0, scratch=(), name=None, limit=24, windows=None,
         anywhere=()):
    specs = [pl.BlockSpec(memory_space=pltpu.SMEM)] * smem
    specs += [pl.BlockSpec(memory_space=pltpu.VMEM)] * (len(args) - smem)
    for n in anywhere:
        specs[n] = pl.BlockSpec(memory_space=pl.ANY)
    for n, (shape, index) in (windows or {}).items():
        specs[n] = pl.BlockSpec(shape, lambda i, index=index: index)
    return pl.pallas_call(
        kernel,
        grid=(1,) if windows else (),
        out_shape=[jax.ShapeDtypeStruct(shape, dtype) for shape, dtype in outs],
        in_specs=specs,
        out_specs=[pl.BlockSpec(memory_space=pltpu.VMEM)] * len(outs),
        scratch_shapes=scratch,
        compiler_params=pltpu.CompilerParams(vmem_limit_bytes=limit << 20),
        name=name,
    )(*args)


def swap_seq(block, code):
    return lax.ppermute(block, "seq", [(i, i ^ code) for i in range(16)])


def z_send(block):
    def shift(d):
        return lax.ppermute(block, "seq", [(i, (i + 4 * d) % 16) for i in range(16)])

    got = {d: shift(d) for d in (2, 1, 3)}
    return [got[1], got[2], got[3]]


def after(*values):
    return lax.optimization_barrier(values)


def join(*blocks):
    return jnp.concatenate(blocks, axis=0)


def decode(i):
    dp, seq = i // 16, i % 16
    return [dp // 2, (seq // 2) % 2 * 2 + dp % 2, seq // 4, seq % 2]


def encode(x, y, z, core):
    return (x * 2 + y % 2) * 16 + z * 4 + y // 2 * 2 + core


def ring_route(stage, d):
    route = []
    for i in range(128):
        place = decode(i)
        axis = (stage + place[3]) % 3
        place[axis] = (place[axis] + d) % 4
        route.append((i, encode(*place)))
    return route


def hop(block, stage, d):
    return lax.ppermute(block, AXES, ring_route(stage, d))


def ring_send(blocks, stage):
    got = {d: hop(blocks[d - 1], stage, d) for d in (2, 1, 3)}
    return got[1], got[2], got[3]


def place_meta(lengths):
    dp = lax.axis_index("dp").astype(jnp.int32)
    seq = lax.axis_index("seq").astype(jnp.int32)
    core = seq & 1
    coords = [dp >> 1, (seq & 2) + (dp & 1), seq >> 2]
    turns = [jnp.where(core == 0, coords[n], coords[(n + 1) % 3]) for n in range(3)]
    twins = [jnp.where(core == 0, coords[(n + 1) % 3], coords[n]) for n in range(2)]
    values = jnp.stack([core] + turns + twins)
    return jnp.concatenate([seq[None], lengths, values, jnp.zeros((5,), jnp.int32)])


def sum_everywhere(meta, keep, got, ext):
    block = ((ROWS + 16, WIDE), BF)
    keep, *sends = call(
        add_a_kernel, [((ROWS, WIDE), F32)] + [block] * 3,
        meta, keep, *got, ext, smem=1, name="add_a",
    )
    got = ring_send(sends, 1)
    own = call(
        add_b_kernel, [block], meta, keep, *got, ext, smem=1, name="add_b",
        scratch=[pltpu.VMEM((4, 8, WIDE), F32)],
    )[0]
    got = ring_send([own] * 3, 2)
    own = call(add_c_kernel, [block], own, *got, name="add_c")[0]
    got = ring_send([own] * 3, 1)
    blocks = [own, *ring_send([own] * 3, 0)]
    rest = call(stack_kernel, [((3 * ROWS, WIDE), BF)], *got, name="stack")[0]
    rests = [rest, *ring_send([rest] * 3, 0)]
    twin_blocks = [swap_seq(piece, 1) for piece in blocks]
    twin_rests = [swap_seq(rest, 1)]
    outs = finish(meta, [(rest, 0, 0)] + [(blocks[d], 0, d) for d in range(4)], None)
    pieces = [(twin_rests[0], 1, 0)] + [(twin_blocks[d], 1, d) for d in range(4)]
    *outs, d_gain, d_bias = finish(meta, pieces, outs, blocks + twin_blocks)
    rests[2], *outs = after(rests[2], *outs)
    twin_rests += [None, swap_seq(rests[2], 1), None]
    outs = finish(meta, [(rests[2], 0, 2)], outs)
    rests[1], rests[3], *outs = after(rests[1], rests[3], *outs)
    twin_rests[1], twin_rests[3] = swap_seq(rests[1], 1), swap_seq(rests[3], 1)
    outs = finish(meta, [(rests[1], 0, 1), (rests[3], 0, 3), (twin_rests[2], 1, 2)], outs)
    outs = finish(meta, [(twin_rests[1], 1, 1), (twin_rests[3], 1, 3)], outs)
    return *outs, d_gain, d_bias


def position_table():
    quarter = D // 4
    frequency = 1.0 / 10000.0 ** (np.arange(quarter) / quarter)
    angle = np.arange(256)[:, None] * frequency[None, :]
    exact_values = np.concatenate([np.sin(angle), np.cos(angle)], axis=1).astype(np.float32)
    parts = []
    rest = exact_values
    for _ in range(3):
        part = rest.astype(jnp.bfloat16)
        parts.append(part)
        rest = rest - part.astype(np.float32)
    return np.concatenate(parts, axis=1)


def per_device(tokens, tile_coords, slide_lengths, norm_gain, norm_bias, w_qkv, w_out, cotangent):
    meta = place_meta(slide_lengths[0])
    table = jnp.asarray(position_table())
    inp, normed, kv, kv_pack = call(
        key_kernel,
        [((T, D), F32), ((T, D), BF), ((T, 2 * D), BF), ((80, 2 * D), BF)],
        tokens[0], tile_coords[0], table, norm_gain, norm_bias, w_qkv, name="keys", limit=60,
        anywhere=(0, 2, 5),
        scratch=[
            pltpu.VMEM((T, D), BF), pltpu.VMEM((T, 3 * D // 2), BF), pltpu.VMEM((2, D, D), BF),
            pltpu.SemaphoreType.DMA((4,)),
        ],
    )
    from_y = swap_seq(kv_pack, 2)
    norm_b = swap_seq(normed, 1)
    q, d_att, cot, qd_pack = call(
        query_kernel,
        [((T, D), BF), ((T, D), BF), ((T, D), BF), ((80, 2 * D), BF)],
        normed, w_qkv, w_out, cotangent[0], name="queries", limit=60,
        windows={1: ((D, D), (0, 0))},
    )
    from_y, q, norm_b = after(from_y, q, norm_b)
    far = join(kv_pack[64:], from_y[64:])
    from_z = z_send(far)
    far, q = after(far, q)
    part = join(kv_pack[:64], from_y[:64], far)
    twin = swap_seq(part, 1)
    tops = [
        call(
            functools.partial(local_forward_kernel, first=first),
            [((T, D // 2), F32), ((T, 128), F32), ((T, 128), F32)],
            meta, q, kv, smem=1, name="local_forward",
        )
        for first in (0, 8)
    ]
    *from_z, twin, _, _ = after(*from_z, twin, tops[0][0], tops[1][0])
    got_kv = (part, *from_z, twin, *[swap_seq(rows, 1) for rows in from_z])
    att, stat, pack = call(
        remote_forward_kernel,
        [((T, D), BF), ((T, 128), F32), ((80, 2 * D + 128), BF)],
        meta, q, *got_kv, *tops[0], *tops[1], d_att, qd_pack,
        smem=1, name="remote_forward",
    )
    from_y = swap_seq(pack, 2)
    att_b = swap_seq(att, 1)
    grads_1 = call(
        functools.partial(local_backward_kernel, first=0),
        [((T, D // 2), F32)] * 3,
        meta, q, kv, d_att, stat, smem=1, name="local_backward",
    )
    dq_r = call(
        query_backward_kernel, [((T, D), F32)],
        meta, q, d_att, stat, *got_kv, smem=1, name="query_backward",
    )[0]
    from_y, att_b, dq_r, *grads_1 = after(from_y, att_b, dq_r, *grads_1)
    far = join(pack[64:], from_y[64:])
    from_z = z_send(far)
    far, q = after(far, q)
    part = join(pack[:64], from_y[:64], far)
    twin = swap_seq(part, 1)
    grads_2 = call(
        functools.partial(local_backward_kernel, first=8),
        [((T, D // 2), F32)] * 3,
        meta, q, kv, d_att, stat, smem=1, name="local_backward",
    )
    *from_z, twin, _ = after(*from_z, twin, grads_2[0])
    got_qd = (part, *from_z, twin, *[swap_seq(rows, 1) for rows in from_z])
    d_qkv, own, sent = call(
        key_backward_kernel,
        [((T, 3 * D), BF), ((T, 2 * D), BF), ((T, 2 * D), BF)],
        meta, kv, *got_qd, dq_r, *grads_1, *grads_2, cot,
        smem=1, name="key_backward",
        scratch=[pltpu.VMEM((T, D), F32), pltpu.VMEM((T, D), F32)],
    )
    left_a, left_b = call(
        left_kernel, [((D, 2 * T), BF)] * 2,
        meta, normed, norm_b, att, att_b, smem=1, name="left",
    )
    other, left_a = after(swap_seq(sent, 1), left_a)
    chunk = ((ROWS, 2 * D), BF)
    keep, *sends = call(
        weight_grad_kernel, [((ROWS, 2 * D), F32), chunk, chunk, chunk],
        meta, own, other, left_a, left_b, smem=1, name="weight_grad",
    )
    got = ring_send(sends, 0)
    d_tokens, ext = call(
        token_grad_kernel,
        [((T, D), BF), ((16, WIDE), BF)],
        d_qkv, w_qkv, inp, norm_gain, cot, name="token_grad",
    )
    att, _ = after(att, keep)
    layer_out = call(out_kernel, [((T, D), BF)], att, inp, w_out, name="layer_out")[0]
    *got, _ = after(*got, layer_out)
    dw_qkv, dw_out, d_gain, d_bias = sum_everywhere(meta, keep, got, ext)
    return (
        layer_out[None],
        d_tokens[None],
        dw_qkv,
        dw_out,
        d_gain,
        d_bias,
    )


def solution(mesh):
    return jax.shard_map(
        per_device,
        mesh=mesh,
        in_specs=(
            P("dp", "seq", None),
            P("dp", None, "seq"),
            P("dp", None),
            P(),
            P(),
            P(),
            P(),
            P("dp", "seq", None),
        ),
        out_specs=(P("dp", "seq", None), P("dp", "seq", None), P(), P(), P(), P()),
        check_vma=False,
    )
```

```python
import functools

import jax
import jax.numpy as jnp
import numpy as np
from jax import lax
from jax.experimental import pallas as pl
from jax.experimental.pallas import tpu as pltpu
from jax.sharding import PartitionSpec as P

HEADS = 16
HD = 48
D = 768
T = 256
SCALE = HD ** (-0.5)
NEG = -1e30
BF = jnp.bfloat16
F32 = jnp.float32
AXES = ("dp", "seq")
WIDE = 384


def iota(shape, dim):
    return lax.broadcasted_iota(jnp.int32, shape, dim)


def tile_of(i):
    return (i >> 6) + ((i >> 4) & 3) * 4 + (i & 15) * 16


def nt(a, b):
    return lax.dot_general(a, b, (((1,), (1,)), ((), ())), preferred_element_type=F32)


def nn(a, b):
    return lax.dot_general(a, b, (((1,), (0,)), ((), ())), preferred_element_type=F32)


def tn(a, b):
    return lax.dot_general(a, b, (((0,), (0,)), ((), ())), preferred_element_type=F32)


def exact(a, b):
    hi = a.astype(BF)
    rest = a - hi.astype(F32)
    mid = rest.astype(BF)
    low = (rest - mid.astype(F32)).astype(BF)
    return nn(hi, b) + nn(mid, b) + nn(low, b)


def sort_matrix():
    return jnp.where(tile_of(iota((T, T), 0)) == iota((T, T), 1), 1.0, 0.0).astype(BF)


def unsort_matrix():
    return jnp.where(iota((T, T), 0) == tile_of(iota((T, T), 1)), 1.0, 0.0).astype(BF)


def span_mask(lo, shape):
    lane = iota(shape, 1)
    return jnp.where((lane >= lo) & (lane < lo + HD), 1.0, 0.0)


def head_window(h):
    start = HD * h // 128 * 128
    width = 128 if HD * h - start + HD <= 128 else 256
    return start, width


def head_mask(h):
    start, width = head_window(h)
    return span_mask(HD * h - start, (1, width)).astype(BF)


def group_window(g):
    return 192 * g // 128 * 128


def group_mask(g):
    lo = 192 * g - group_window(g) + HD * (iota((T, 256), 0) >> 6)
    return span_mask(lo, (T, 256)).astype(BF)


def far_mask():
    row = iota((T, D), 0)
    lo = HD * ((row >> 6) + 4 * ((row >> 4) & 3))
    return span_mask(lo, (T, D)).astype(BF)


def slide_of(meta, pos):
    end = meta[1]
    out = jnp.where(pos >= end, 1, 0)
    for n in range(2, 5):
        end = end + meta[n]
        out = out + jnp.where(pos >= end, 1, 0)
    return out


def row_ids(meta):
    return slide_of(meta, meta[0] * T + tile_of(iota((T, 1), 0)))


def bias_of(meta, pos):
    return jnp.where(row_ids(meta) == slide_of(meta, pos), 0.0, NEG)


def local_bias(meta):
    return bias_of(meta, meta[0] * T + tile_of(iota((1, T), 1)))


def mid_bias(meta):
    t = iota((T, T), 1)
    slot = t >> 6
    dev = meta[0] ^ (((slot & 1) << 1) | (slot >> 1))
    pos = dev * T + ((t >> 4) & 3) * 4 + (t & 15) * 16 + (iota((T, T), 0) >> 6)
    return bias_of(meta, pos)


def far_bias(meta):
    t = iota((T, T), 1)
    s = t >> 4
    place = (((meta[0] >> 2) - (s >> 1)) & 3) * 4 + ((meta[0] & 3) ^ ((s & 1) << 1) ^ (s >> 3))
    row = iota((T, T), 0)
    pos = place * T + (t & 15) * 16 + (row >> 6) + 4 * ((row >> 4) & 3)
    return bias_of(meta, pos)


def far_head(b):
    return b // 4 + 4 * (b % 4)


def fold_mid(x, masks):
    out = x[0:64] * masks[0]
    for c in range(1, 4):
        out = out + x[64 * c : 64 * c + 64] * masks[c]
    return out


def fold_far(x, masks):
    out = x[0:16] * masks[0]
    for b in range(1, 16):
        out = out + x[16 * b : 16 * b + 16] * masks[far_head(b)]
    return out


def pack_rows(x, head_masks):
    mids = [
        head_masks[c] + head_masks[4 + c] + head_masks[8 + c] + head_masks[12 + c]
        for c in range(4)
    ]
    return jnp.concatenate([fold_mid(x, mids), fold_far(x, head_masks)], axis=0)


def norm_parts(inputs):
    mean = jnp.mean(inputs, axis=1, keepdims=True)
    centred = inputs - mean
    var = jnp.mean(centred * centred, axis=1, keepdims=True)
    inv_std = lax.rsqrt(var + 1e-05)
    return centred * inv_std, inv_std


def pack_masks():
    return [span_mask(HD * h, (1, D)).astype(BF) for h in range(HEADS)]


def key_kernel(tok_h, coords, table_h, gain, bias, w_h, inp_o, norm_o, kv_o, pack_o,
               tok, table, weight, sems):
    copies = [
        pltpu.make_async_copy(tok_h, tok, sems.at[0]),
        pltpu.make_async_copy(table_h, table, sems.at[1]),
        pltpu.make_async_copy(w_h.at[:, pl.ds(D, D)], weight.at[0], sems.at[2]),
        pltpu.make_async_copy(w_h.at[:, pl.ds(2 * D, D)], weight.at[1], sems.at[3]),
    ]
    for copy in copies:
        copy.start()
    sort = sort_matrix()
    grid = iota((T, T), 0)
    hots = []
    for axis in range(2):
        hot = jnp.where(grid == coords[axis : axis + 1, :], 1.0, 0.0).astype(BF)
        hots.append(nt(sort, hot).astype(BF))
    copies[0].wait()
    tok_s = nn(sort, tok[...])
    copies[1].wait()
    parts = []
    for hot in hots:
        found = nn(hot, table[...])
        parts.append(found[:, :384] + found[:, 384:768] + found[:, 768:])
    inputs = tok_s + jnp.concatenate(parts, axis=1)
    inp_o[...] = inputs
    unit, _ = norm_parts(inputs)
    normed = (unit * gain[...].reshape(1, D) + bias[...].reshape(1, D)).astype(BF)
    norm_o[...] = normed
    masks = pack_masks()
    for n in range(2):
        copies[2 + n].wait()
        part = nn(normed, weight[n]).astype(BF)
        kv_o[:, D * n : D * (n + 1)] = part
        pack_o[:, D * n : D * (n + 1)] = pack_rows(part, masks)


def query_kernel(normed, w_qkv, w_out, cot, q_o, da_o, cot_o, pack_o):
    cot_s = nn(sort_matrix(), cot[...]).astype(BF)
    cot_o[...] = cot_s
    q = nn(normed[...], w_qkv[...]).astype(BF)
    q_o[...] = q
    d_att = nt(cot_s, w_out[...]).astype(BF)
    da_o[...] = d_att
    masks = pack_masks()
    pack_o[:, :D] = pack_rows(q, masks)
    pack_o[:, D:] = pack_rows(d_att, masks)


def soft(scores):
    top = jnp.max(scores, axis=1, keepdims=True)
    shares = jnp.exp(scores - top)
    return top, jnp.sum(shares, axis=1, keepdims=True), shares.astype(BF)


def local_forward_kernel(meta, q_r, kv, *refs, first):
    o_o, top_o, sum_o = refs[-3:]
    bias = local_bias(meta)
    o_o[...] = jnp.zeros_like(o_o)
    lane = iota((T, 128), 1)
    tops = jnp.full((T, 128), NEG, F32)
    sums = jnp.zeros((T, 128), F32)
    base = HD * first
    for h in range(first, first + 8):
        s, w = head_window(h)
        mask = head_mask(h)
        scores = nt(q_r[:, s : s + w] * mask, kv[:, s : s + w]) * SCALE + bias
        top, total, shares = soft(scores)
        tops = jnp.where(lane == h, top, tops)
        sums = jnp.where(lane == h, total, sums)
        o_o[:, s - base : s - base + w] += nn(shares, kv[:, D + s : D + s + w] * mask)
    top_o[...] = tops
    sum_o[...] = sums
    if first:
        mid_forward(meta, q_r, *refs[:-3])


def mid_forward(meta, q_r, part, twin, mid_o, top_o, sum_o):
    lane = iota((T, 128), 1)
    row = iota((T, 128), 0)
    got = (part, None, None, None, twin)
    tops = jnp.full((T, 128), NEG, F32)
    sums = jnp.zeros((T, 128), F32)
    bias = mid_bias(meta)
    for g in range(4):
        s = group_window(g)
        q = q_r[:, s : s + 256] * group_mask(g)
        top, total, shares = soft(nt(q, mid_rows(got, s, 256)) * SCALE + bias)
        here = lane == 4 * g + (row >> 6)
        tops = jnp.where(here, top, tops)
        sums = jnp.where(here, total, sums)
        mid_o[g] = nn(shares, mid_rows(got, D + s, 256))
    top_o[...] = tops
    sum_o[...] = sums


def mid_rows(got, lo, width):
    return jnp.concatenate([got[0][:128, lo : lo + width], got[4][:128, lo : lo + width]], axis=0)


def far_rows(got, lo, width):
    at = slice(lo, lo + width)
    rows = []
    for n in (0, 4):
        rows.append(got[n][128:, at])
        rows += [got[n + d][:, at] for d in (1, 2, 3)]
    return jnp.concatenate(rows, axis=0)


def expand_matrix():
    head = iota((128, D), 0)
    lane = iota((128, D), 1)
    return jnp.where((lane >= head * HD) & (lane < head * HD + HD), 1.0, 0.0).astype(BF)


def gather_matrix():
    lane = iota((D, 128), 0)
    head = iota((D, 128), 1)
    return jnp.where((lane >= head * HD) & (lane < head * HD + HD), 1.0, 0.0).astype(BF)


def remote_forward_kernel(meta, q_r, *refs):
    got = refs[:8]
    o_1, top_1, sum_1, mid_parts, top_m, sum_m, o_2, top_2, sum_2 = refs[8:17]
    d_att, pack, att_o, stat_o, send_o = refs[17:]
    lane = iota((T, 128), 1)
    row = iota((T, 128), 0)
    top_l = jnp.where(lane < 8, top_1[...], top_2[...])
    sum_l = jnp.where(lane < 8, sum_1[...], sum_2[...])
    tops_m = top_m[...]
    sums_m = sum_m[...]
    mask = far_mask()
    scores = nt(q_r[...] * mask, far_rows(got, 0, D)) * SCALE + far_bias(meta)
    top, total, shares = soft(scores)
    far_part = nn(shares, far_rows(got, D, D))
    here = lane == (row >> 6) + 4 * ((row >> 4) & 3)
    tops_f = jnp.where(here, top, NEG)
    sums_f = jnp.where(here, total, 0.0)
    highest = jnp.maximum(jnp.maximum(top_l, tops_m), tops_f)
    f_l = jnp.exp(top_l - highest)
    f_m = jnp.exp(tops_m - highest)
    f_f = jnp.exp(tops_f - highest)
    totals = f_l * sum_l + f_m * sums_m + f_f * sums_f
    totals = jnp.where(lane < HEADS, totals, 1.0)
    inverse = 1.0 / totals
    lse = highest + jnp.log(totals)
    w_m = f_m * inverse
    o_l = jnp.concatenate([o_1[...], o_2[...]], axis=1)
    att = o_l * exact(f_l * inverse, expand_matrix())
    w_f = jnp.sum(jnp.where(here, f_f * inverse, 0.0), axis=1, keepdims=True)
    att = att + far_part * w_f * mask.astype(F32)
    acc = [att[:, 128 * n : 128 * n + 128] for n in range(6)]
    for g in range(4):
        n = group_window(g) // 128
        w_g = jnp.sum(jnp.where(lane == 4 * g + (row >> 6), w_m, 0.0), axis=1, keepdims=True)
        add = mid_parts[g] * w_g * group_mask(g).astype(F32)
        acc[n] = acc[n] + add[:, :128]
        acc[n + 1] = acc[n + 1] + add[:, 128:]
    att = jnp.concatenate(acc, axis=1).astype(BF)
    att_o[...] = att
    prod = d_att[...].astype(F32) * att.astype(F32)
    delta = exact(prod, gather_matrix())
    stat = jnp.where(lane < HEADS, lse, pltpu.roll(delta, HEADS, 1))
    stat = jnp.where(lane < 2 * HEADS, stat, 0.0)
    stat_o[...] = stat
    one = iota((1, 128), 1)
    send_o[:, : 2 * D] = pack[...]
    mids = fold_mid(stat, [jnp.where((one & 3) == c, 1.0, 0.0) for c in range(4)])
    fars = fold_far(stat, [jnp.where((one & 15) == h, 1.0, 0.0) for h in range(HEADS)])
    send_o[:, 2 * D :] = three_parts(jnp.concatenate([mids, fars], axis=0))


def three_parts(x):
    lane = iota(x.shape, 1)
    hi = x.astype(BF).astype(F32)
    mid = (x - hi).astype(BF).astype(F32)
    low = x - hi - mid
    parts = jnp.where(lane < 64, pltpu.roll(mid, 32, 1), pltpu.roll(low, 64, 1))
    return jnp.where(lane < 32, hi, parts).astype(BF)


def out_kernel(att, inp, w_out, out_o):
    layer = (inp[...] + nn(att[...], w_out[...])).astype(BF)
    out_o[...] = nn(unsort_matrix(), layer).astype(BF)


def pick_mid_column(stat, col):
    return jnp.concatenate(
        [stat[64 * c : 64 * c + 64, col + c : col + c + 1] for c in range(4)], axis=0
    )


def pick_far_column(stat, col):
    return jnp.concatenate(
        [
            stat[16 * b : 16 * b + 16, col + far_head(b) : col + far_head(b) + 1]
            for b in range(16)
        ],
        axis=0,
    )


def local_backward_kernel(meta, q_r, kv, d_att, stat, *refs, first):
    dq_o, dk_o, dv_o = refs[-3:]
    bias = local_bias(meta)
    stat_t = stat[...].T
    dq_o[...] = jnp.zeros_like(dq_o)
    dk_o[...] = jnp.zeros_like(dk_o)
    dv_o[...] = jnp.zeros_like(dv_o)
    base = HD * first
    for h in range(first, first + 8):
        s, w = head_window(h)
        t = s - base
        mask = head_mask(h)
        q = q_r[:, s : s + w] * mask
        k = kv[:, s : s + w] * mask
        da = d_att[:, s : s + w] * mask
        scores = nt(k, q) * SCALE + bias
        shares = jnp.exp(scores - stat_t[h : h + 1, :])
        d_shares = nt(kv[:, D + s : D + s + w], da)
        ds = (shares * (d_shares - stat_t[HEADS + h : HEADS + h + 1, :])).astype(BF)
        dk_o[:, t : t + w] += nn(ds, q)
        dv_o[:, t : t + w] += nn(shares.astype(BF), da)
        dq_o[:, t : t + w] += tn(ds, k)
    if first:
        mid_key_backward(meta, kv, *refs[:-3])


def mid_key_backward(meta, kv, part, twin, dk_o, dv_o):
    got = (part, None, None, None, twin)
    stat_t = joined_stats(mid_rows(got, 2 * D, 128))
    dk_o[...] = jnp.zeros_like(dk_o)
    dv_o[...] = jnp.zeros_like(dv_o)
    bias = mid_bias(meta)
    for g in range(4):
        s = group_window(g)
        mask = group_mask(g)
        mask_f = mask.astype(F32)
        q = mid_rows(got, s, 256)
        da = mid_rows(got, D + s, 256)
        scores = nt(kv[:, s : s + 256] * mask, q) * SCALE + bias
        shares = jnp.exp(scores - spread_mid(stat_t, 4 * g))
        d_shares = nt(kv[:, D + s : D + s + 256] * mask, da)
        ds = (shares * (d_shares - spread_mid(stat_t, HEADS + 4 * g))).astype(BF)
        dk_o[:, s : s + 256] += nn(ds, q) * mask_f
        dv_o[:, s : s + 256] += nn(shares.astype(BF), da) * mask_f


def query_backward_kernel(meta, q_r, d_att, stat, *refs):
    got, dq_o = refs[:8], refs[8]
    dq_o[...] = jnp.zeros_like(dq_o)
    mid = mid_bias(meta)
    for g in range(4):
        s = group_window(g)
        mask = group_mask(g)
        k = mid_rows(got, s, 256)
        scores = nt(q_r[:, s : s + 256] * mask, k) * SCALE + mid
        shares = jnp.exp(scores - pick_mid_column(stat, 4 * g))
        d_shares = nt(d_att[:, s : s + 256] * mask, mid_rows(got, D + s, 256))
        ds = (shares * (d_shares - pick_mid_column(stat, HEADS + 4 * g))).astype(BF)
        dq_o[:, s : s + 256] += nn(ds, k) * mask.astype(F32)
    mask = far_mask()
    k = far_rows(got, 0, D)
    scores = nt(q_r[...] * mask, k) * SCALE + far_bias(meta)
    shares = jnp.exp(scores - pick_far_column(stat, 0))
    d_shares = nt(d_att[...] * mask, far_rows(got, D, D))
    ds = (shares * (d_shares - pick_far_column(stat, HEADS))).astype(BF)
    dq_o[...] += nn(ds, k) * mask.astype(F32)


def spread_mid(stat_t, row):
    return jnp.concatenate(
        [jnp.broadcast_to(stat_t[row + c : row + c + 1, :], (64, T)) for c in range(4)], axis=0
    )


def spread_far(stat_t, row):
    return jnp.concatenate(
        [
            jnp.broadcast_to(stat_t[row + far_head(b) : row + far_head(b) + 1, :], (16, T))
            for b in range(16)
        ],
        axis=0,
    )


def joined_stats(rows):
    x = rows.astype(F32).T
    return x[:32] + (x[32:64] + x[64:96])


def key_backward_kernel(meta, kv, *refs):
    got = refs[:8]
    dq_r, dq_1, dk_1, dv_1, dk_m, dv_m, dq_2, dk_2, dv_2, cot = refs[8:18]
    all_o, kept_o, sent_o, dk_s, dv_s = refs[18:]
    dk_s[...] = jnp.concatenate([dk_1[...], dk_2[...]], axis=1) + dk_m[...]
    dv_s[...] = jnp.concatenate([dv_1[...], dv_2[...]], axis=1) + dv_m[...]
    stat_t = joined_stats(far_rows(got, 2 * D, 128))
    mask = far_mask()
    mask_f = mask.astype(F32)
    q = far_rows(got, 0, D)
    da = far_rows(got, D, D)
    scores = nt(kv[:, :D] * mask, q) * SCALE + far_bias(meta)
    shares = jnp.exp(scores - spread_far(stat_t, 0))
    d_shares = nt(kv[:, D:] * mask, da)
    ds = (shares * (d_shares - spread_far(stat_t, HEADS))).astype(BF)
    dk_s[...] += nn(ds, q) * mask_f
    dv_s[...] += nn(shares.astype(BF), da) * mask_f
    dq = jnp.concatenate([dq_1[...], dq_2[...]], axis=1) + dq_r[...]
    d_q = (dq * SCALE).astype(BF)
    d_k = (dk_s[...] * SCALE).astype(BF)
    d_v = dv_s[...].astype(BF)
    all_o[:, :D] = d_q
    all_o[:, D : 2 * D] = d_k
    all_o[:, 2 * D :] = d_v
    first = meta[5] == 0
    kept_o[:, :D] = jnp.where(first, d_q, d_v)
    kept_o[:, D:] = jnp.where(first, d_k, cot[...])
    sent_o[:, :D] = jnp.where(first, d_v, d_q)
    sent_o[:, D:] = jnp.where(first, cot[...], d_k)


def left_kernel(meta, norm_a, norm_b, att_a, att_b, left):
    left[0] = jnp.concatenate([norm_a[...], norm_b[...]], axis=0).T
    left[1] = left[0]

    @pl.when(meta[5] == 1)
    def _():
        left[1] = jnp.concatenate([att_a[...], att_b[...]], axis=0).T


def weight_grad_kernel(meta, own, other, left, keep_o, s1, s2, s3):
    for d, out in ((2, s2), (1, s1), (3, s3), (0, keep_o)):
        j = (meta[6] + d) & 3
        cols = pl.ds(pl.multiple_of(j * WIDE, 128), WIDE)
        right = jnp.concatenate([own[:, cols], other[:, cols]], axis=0)
        out[...] = nn(left[j >> 1], right).astype(out.dtype)


def token_grad_kernel(d_qkv, w_qkv, inp, gain, cot, tok_o, ext_o):
    d_normed = nt(d_qkv[...], w_qkv[...])
    unit, inv_std = norm_parts(inp[...])
    d_gain = jnp.sum(d_normed * unit, axis=0, keepdims=True)
    d_bias = jnp.sum(d_normed, axis=0, keepdims=True)
    ext_o[...] = two_parts(jnp.concatenate(
        [d_gain[:, :WIDE], d_gain[:, WIDE:], d_bias[:, :WIDE], d_bias[:, WIDE:],
         jnp.zeros((4, WIDE), F32)], axis=0))
    d_unit = d_normed * gain[...].reshape(1, D)
    mean_a = jnp.mean(d_unit, axis=1, keepdims=True)
    mean_b = jnp.mean(d_unit * unit, axis=1, keepdims=True)
    d_tok = cot[...].astype(F32) + inv_std * (d_unit - mean_a - unit * mean_b)
    tok_o[...] = nn(unsort_matrix(), d_tok.astype(BF)).astype(BF)


def two_parts(ext):
    hi = ext.astype(BF)
    return jnp.concatenate([hi, (ext - hi.astype(F32)).astype(BF)], axis=0)


def whole_of(rows):
    return rows[:8].astype(F32) + rows[8:].astype(F32)


def ring_total(meta, slot, own, got, pad):
    pad[meta[slot]] = own
    for d, piece in enumerate(got, 1):
        pad[(meta[slot] - d) & 3] = piece
    return (pad[0] + pad[1]) + (pad[2] + pad[3])


def add_a_kernel(meta, keep, r1, r2, r3, ext, keep_o, s1, s2, s3):
    rows = D // 4
    for d, out in ((2, s2), (1, s1), (3, s3), (0, keep_o)):
        at = pl.ds(pl.multiple_of(((meta[7] + d) & 3) * rows, 16), rows)
        total = keep[at, :] + (r1[at, :].astype(F32) + r2[at, :].astype(F32) + r3[at, :].astype(F32))
        if d == 0:
            out[...] = total
        else:
            out[:rows] = total.astype(BF)
            out[rows:] = ext[...]


def add_b_kernel(meta, keep, r1, r2, r3, ext, out, pad):
    rows = D // 4
    got = (r1, r2, r3)
    total = keep[...]
    for r in got:
        total = total + r[:rows].astype(F32)
    out[:rows] = total.astype(BF)
    sums = ring_total(meta, 7, whole_of(ext[...]), [whole_of(r[rows:]) for r in got], pad)
    out[rows:] = two_parts(sums)


def add_c_kernel(own, r1, r2, r3, out):
    rows = D // 4

    def total(a, b, c, d):
        return (a + c) + (b + d)

    out[:rows] = total(*[r[:rows].astype(F32) for r in (own, r1, r2, r3)]).astype(BF)
    out[rows:] = two_parts(total(*[whole_of(r[rows:]) for r in (own, r1, r2, r3)]))


def merge_kernel(meta, own, r1, r2, r3, out):
    rows = D // 4
    out[D:] = own[rows:]
    for d, piece in enumerate((own, r1, r2, r3)):
        at = pl.ds(pl.multiple_of(((meta[7] - d) & 3) * rows, 16), rows)
        out[at, :] = piece[:rows]


def finish_kernel(meta, *refs, marks, first, last):
    count = len(marks)
    pieces, refs = refs[:count], refs[count:]
    if last:
        tails, refs = refs[:8], refs[8:]
    if not first:
        refs = refs[2:]
    qkv_o, out_o, *refs = refs
    if last:
        gain_o, bias_o, *refs = refs
    sems, wide = refs[0], refs[1 : 1 + count]
    for n, (piece, (core, turn, row)) in enumerate(zip(pieces, marks)):
        chunk = (meta[5] ^ core) * 4 + ((meta[9 if core else 6] - turn) & 3)
        size = wide[n].shape[0]
        wide[n][...] = piece[:size].astype(F32)

        @pl.when(chunk < 6)
        def _(n=n, chunk=chunk, row=row, size=size):
            at = pl.ds(pl.multiple_of(chunk * WIDE, 128), WIDE)
            to = qkv_o.at[pl.ds(row, size), at]
            pltpu.make_async_copy(wide[n], to, sems.at[n]).start()

        @pl.when(chunk >= 6)
        def _(n=n, chunk=chunk, row=row, size=size):
            at = pl.ds(pl.multiple_of((chunk - 6) * WIDE, 128), WIDE)
            to = out_o.at[pl.ds(row, size), at]
            pltpu.make_async_copy(wide[n], to, sems.at[n]).start()

    if last:
        pad = refs[1 + count]
        for n, tail in enumerate(tails):
            core = n // 4
            place = (meta[9 if core else 6] - n % 4) & 3
            pad[(meta[5] ^ core) * 4 + place] = whole_of(tail[...])
        total = pad[0]
        for n in range(1, 8):
            total = total + pad[n]
        gain_o[...] = jnp.concatenate([total[0:1], total[1:2]], axis=1).reshape(D)
        bias_o[...] = jnp.concatenate([total[2:3], total[3:4]], axis=1).reshape(D)
    for n in range(count):
        to = qkv_o.at[pl.ds(0, wide[n].shape[0]), pl.ds(0, WIDE)]
        pltpu.make_async_copy(wide[n], to, sems.at[n]).wait()


def finish(meta, pieces, outs, tails=None):
    first, last = outs is None, tails is not None
    marks = tuple(piece[1:] for piece in pieces)
    arrays = [piece[0] for piece in pieces]
    smem = pl.BlockSpec(memory_space=pltpu.SMEM)
    anywhere = pl.BlockSpec(memory_space=pl.ANY)
    whole = pl.BlockSpec(memory_space=pltpu.VMEM)
    args = [meta, *arrays]
    in_specs = [smem] + [whole] * len(arrays)
    if last:
        args += tails
        for tail in tails:
            index = (tail.shape[0] // 16 - 1, 0)
            in_specs.append(pl.BlockSpec((16, WIDE), lambda i, index=index: index))
    aliases = {}
    if not first:
        aliases = {len(args): 0, len(args) + 1: 1}
        args += list(outs)
        in_specs += [anywhere] * 2
    out_shape = [jax.ShapeDtypeStruct((D, 3 * D), F32), jax.ShapeDtypeStruct((D, D), F32)]
    out_specs = [anywhere] * 2
    scratch = [pltpu.SemaphoreType.DMA((len(pieces),))]
    for array in arrays:
        scratch.append(pltpu.VMEM((array.shape[0] // WIDE * WIDE, WIDE), F32))
    if last:
        out_shape += [jax.ShapeDtypeStruct((D,), F32)] * 2
        out_specs += [pl.BlockSpec((D,), lambda i: (0,))] * 2
        scratch += [pltpu.VMEM((8, 8, WIDE), F32)]
    return pl.pallas_call(
        functools.partial(finish_kernel, marks=marks, first=first, last=last),
        grid=(1,),
        in_specs=in_specs,
        out_specs=out_specs,
        out_shape=out_shape,
        scratch_shapes=scratch,
        input_output_aliases=aliases,
        compiler_params=pltpu.CompilerParams(vmem_limit_bytes=24 << 20),
        name="finish",
    )(*args)


def call(kernel, outs, *args, smem=0, scratch=(), name=None, limit=24, windows=None,
         anywhere=()):
    specs = [pl.BlockSpec(memory_space=pltpu.SMEM)] * smem
    specs += [pl.BlockSpec(memory_space=pltpu.VMEM)] * (len(args) - smem)
    for n in anywhere:
        specs[n] = pl.BlockSpec(memory_space=pl.ANY)
    for n, (shape, index) in (windows or {}).items():
        specs[n] = pl.BlockSpec(shape, lambda i, index=index: index)
    return pl.pallas_call(
        kernel,
        grid=(1,) if windows else (),
        out_shape=[jax.ShapeDtypeStruct(shape, dtype) for shape, dtype in outs],
        in_specs=specs,
        out_specs=[pl.BlockSpec(memory_space=pltpu.VMEM)] * len(outs),
        scratch_shapes=scratch,
        compiler_params=pltpu.CompilerParams(vmem_limit_bytes=limit << 20),
        name=name,
    )(*args)


def swap_seq(block, code):
    return lax.ppermute(block, "seq", [(i, i ^ code) for i in range(16)])


def z_send(block):
    def shift(d):
        return lax.ppermute(block, "seq", [(i, (i + 4 * d) % 16) for i in range(16)])

    got = {d: shift(d) for d in (2, 1, 3)}
    return [got[1], got[2], got[3]]


def after(*values):
    return lax.optimization_barrier(values)


def join(*blocks):
    return jnp.concatenate(blocks, axis=0)


def decode(i):
    dp, seq = i // 16, i % 16
    return [dp // 2, (seq // 2) % 2 * 2 + dp % 2, seq // 4, seq % 2]


def encode(x, y, z, core):
    return (x * 2 + y % 2) * 16 + z * 4 + y // 2 * 2 + core


def ring_route(stage, d):
    route = []
    for i in range(128):
        place = decode(i)
        axis = (stage + place[3]) % 3
        place[axis] = (place[axis] + d) % 4
        route.append((i, encode(*place)))
    return route


def hop(block, stage, d):
    return lax.ppermute(block, AXES, ring_route(stage, d))


def ring_send(blocks, stage):
    got = {d: hop(blocks[d - 1], stage, d) for d in (2, 1, 3)}
    return got[1], got[2], got[3]


def place_meta(lengths):
    dp = lax.axis_index("dp").astype(jnp.int32)
    seq = lax.axis_index("seq").astype(jnp.int32)
    core = seq & 1
    coords = [dp >> 1, (seq & 2) + (dp & 1), seq >> 2]
    turns = [jnp.where(core == 0, coords[n], coords[(n + 1) % 3]) for n in range(3)]
    other = jnp.where(core == 0, coords[1], coords[0])
    values = jnp.stack([core] + turns + [other])
    return jnp.concatenate([seq[None], lengths, values, jnp.zeros((6,), jnp.int32)])


def sum_everywhere(meta, keep, sends, ext, beside):
    cut = D // 4
    got = ring_send(sends, 0)
    *got, _ = after(*got, beside)
    keep, *sends = call(
        add_a_kernel,
        [((cut, WIDE), F32)] + [((cut + 16, WIDE), BF)] * 3,
        meta, keep, *got, ext, smem=1, name="add_a",
    )
    got = ring_send(sends, 1)
    block = call(
        add_b_kernel, [((cut + 16, WIDE), BF)],
        meta, keep, *got, ext, smem=1, name="add_b", scratch=[pltpu.VMEM((4, 8, WIDE), F32)],
    )[0]
    got = ring_send([block] * 3, 2)
    block = call(add_c_kernel, [((cut + 16, WIDE), BF)], block, *got, name="add_c")[0]
    got = ring_send([block] * 3, 1)
    block = call(
        merge_kernel, [((D + 16, WIDE), BF)], meta, block, *got, smem=1, name="merge_b",
    )[0]
    ring = [block, *ring_send([block] * 3, 0)]
    twin = [swap_seq(block, 1)]
    outs = finish(meta, [(block, 0, 0, 0), (twin[0], 1, 0, 0)], None)
    ring[2], first = after(ring[2], outs[0])
    twin += [None, swap_seq(ring[2], 1), None]
    outs = finish(meta, [(ring[2], 0, 2, 0)], (first, outs[1]))
    ring[1], ring[3], *outs = after(ring[1], ring[3], *outs)
    twin[1], twin[3] = swap_seq(ring[1], 1), swap_seq(ring[3], 1)
    outs = finish(meta, [(ring[1], 0, 1, 0), (ring[3], 0, 3, 0), (twin[2], 1, 2, 0)], outs)
    return finish(meta, [(twin[1], 1, 1, 0), (twin[3], 1, 3, 0)], outs, ring + twin)


def position_table():
    quarter = D // 4
    frequency = 1.0 / 10000.0 ** (np.arange(quarter) / quarter)
    angle = np.arange(256)[:, None] * frequency[None, :]
    exact_values = np.concatenate([np.sin(angle), np.cos(angle)], axis=1).astype(np.float32)
    parts = []
    rest = exact_values
    for _ in range(3):
        part = rest.astype(jnp.bfloat16)
        parts.append(part)
        rest = rest - part.astype(np.float32)
    return np.concatenate(parts, axis=1)


def per_device(tokens, tile_coords, slide_lengths, norm_gain, norm_bias, w_qkv, w_out, cotangent):
    meta = place_meta(slide_lengths[0])
    table = jnp.asarray(position_table())
    inp, normed, kv, kv_pack = call(
        key_kernel,
        [((T, D), F32), ((T, D), BF), ((T, 2 * D), BF), ((80, 2 * D), BF)],
        tokens[0], tile_coords[0], table, norm_gain, norm_bias, w_qkv, name="keys", limit=60,
        anywhere=(0, 2, 5),
        scratch=[
            pltpu.VMEM((T, D), BF), pltpu.VMEM((T, 3 * D // 2), BF), pltpu.VMEM((2, D, D), BF),
            pltpu.SemaphoreType.DMA((4,)),
        ],
    )
    from_y = swap_seq(kv_pack, 2)
    norm_b = swap_seq(normed, 1)
    q, d_att, cot, qd_pack = call(
        query_kernel,
        [((T, D), BF), ((T, D), BF), ((T, D), BF), ((80, 2 * D), BF)],
        normed, w_qkv, w_out, cotangent[0], name="queries", limit=60,
        windows={1: ((D, D), (0, 0))},
    )
    from_y, q, norm_b = after(from_y, q, norm_b)
    far = join(kv_pack[64:], from_y[64:])
    from_z = z_send(far)
    far, q = after(far, q)
    part = join(kv_pack[:64], from_y[:64], far)
    twin = swap_seq(part, 1)
    stat_shape = ((T, 128), F32)
    out_1 = call(
        functools.partial(local_forward_kernel, first=0),
        [((T, D // 2), F32), stat_shape, stat_shape],
        meta, q, kv, smem=1, name="local_forward",
    )
    out_2 = call(
        functools.partial(local_forward_kernel, first=8),
        [((4, T, 256), F32), stat_shape, stat_shape, ((T, D // 2), F32), stat_shape, stat_shape],
        meta, q, kv, part, twin, smem=1, name="local_forward",
    )
    *from_z, _, _ = after(*from_z, out_1[0], out_2[0])
    got_kv = (part, *from_z, twin, *[swap_seq(rows, 1) for rows in from_z])
    att, stat, pack = call(
        remote_forward_kernel,
        [((T, D), BF), ((T, 128), F32), ((80, 2 * D + 128), BF)],
        meta, q, *got_kv, *out_1, *out_2, d_att, qd_pack,
        smem=1, name="remote_forward",
    )
    from_y = swap_seq(pack, 2)
    att_b = swap_seq(att, 1)
    grads_1 = call(
        functools.partial(local_backward_kernel, first=0),
        [((T, D // 2), F32)] * 3,
        meta, q, kv, d_att, stat, smem=1, name="local_backward",
    )
    dq_r = call(
        query_backward_kernel, [((T, D), F32)],
        meta, q, d_att, stat, *got_kv, smem=1, name="query_backward",
    )[0]
    from_y, att_b, dq_r, *grads_1 = after(from_y, att_b, dq_r, *grads_1)
    far = join(pack[64:], from_y[64:])
    from_z = z_send(far)
    far, q = after(far, q)
    part = join(pack[:64], from_y[:64], far)
    twin = swap_seq(part, 1)
    grads_2 = call(
        functools.partial(local_backward_kernel, first=8),
        [((T, D), F32)] * 2 + [((T, D // 2), F32)] * 3,
        meta, q, kv, d_att, stat, part, twin, smem=1, name="local_backward",
    )
    *from_z, _ = after(*from_z, grads_2[0])
    got_qd = (part, *from_z, twin, *[swap_seq(rows, 1) for rows in from_z])
    d_qkv, own, sent = call(
        key_backward_kernel,
        [((T, 3 * D), BF), ((T, 2 * D), BF), ((T, 2 * D), BF)],
        meta, kv, *got_qd, dq_r, *grads_1, *grads_2, cot,
        smem=1, name="key_backward",
        scratch=[pltpu.VMEM((T, D), F32), pltpu.VMEM((T, D), F32)],
    )
    left = call(
        left_kernel, [((2, D, 2 * T), BF)],
        meta, normed, norm_b, att, att_b, smem=1, name="left",
    )[0]
    other, left = after(swap_seq(sent, 1), left)
    keep, *sends = call(
        weight_grad_kernel,
        [((D, WIDE), F32)] + [((D, WIDE), BF)] * 3,
        meta, own, other, left, smem=1, name="weight_grad",
    )
    d_tokens, ext = call(
        token_grad_kernel,
        [((T, D), BF), ((16, WIDE), BF)],
        d_qkv, w_qkv, inp, norm_gain, cot, name="token_grad",
    )
    att, _ = after(att, keep)
    layer_out = call(out_kernel, [((T, D), BF)], att, inp, w_out, name="layer_out")[0]
    dw_qkv, dw_out, d_gain, d_bias = sum_everywhere(meta, keep, sends, ext, layer_out)
    return (
        layer_out[None],
        d_tokens[None],
        dw_qkv,
        dw_out,
        d_gain,
        d_bias,
    )


def solution(mesh):
    return jax.shard_map(
        per_device,
        mesh=mesh,
        in_specs=(
            P("dp", "seq", None),
            P("dp", None, "seq"),
            P("dp", None),
            P(),
            P(),
            P(),
            P(),
            P("dp", "seq", None),
        ),
        out_specs=(P("dp", "seq", None), P("dp", "seq", None), P(), P(), P(), P()),
        check_vma=False,
    )
```

```python
import functools

import jax
import jax.numpy as jnp
import numpy as np
from jax import lax
from jax.experimental import pallas as pl
from jax.experimental.pallas import tpu as pltpu
from jax.sharding import PartitionSpec as P

HEADS = 16
HD = 48
D = 768
T = 256
SCALE = HD ** (-0.5)
NEG = -1e30
BF = jnp.bfloat16
F32 = jnp.float32
AXES = ("dp", "seq")
WIDE = 384


def iota(shape, dim):
    return lax.broadcasted_iota(jnp.int32, shape, dim)


def tile_of(i):
    return (i >> 6) + ((i >> 4) & 3) * 4 + (i & 15) * 16


def nt(a, b):
    return lax.dot_general(a, b, (((1,), (1,)), ((), ())), preferred_element_type=F32)


def nn(a, b):
    return lax.dot_general(a, b, (((1,), (0,)), ((), ())), preferred_element_type=F32)


def tn(a, b):
    return lax.dot_general(a, b, (((0,), (0,)), ((), ())), preferred_element_type=F32)


def exact(a, b):
    hi = a.astype(BF)
    rest = a - hi.astype(F32)
    mid = rest.astype(BF)
    low = (rest - mid.astype(F32)).astype(BF)
    return nn(hi, b) + nn(mid, b) + nn(low, b)


def sort_matrix():
    return jnp.where(tile_of(iota((T, T), 0)) == iota((T, T), 1), 1.0, 0.0).astype(BF)


def unsort_matrix():
    return jnp.where(iota((T, T), 0) == tile_of(iota((T, T), 1)), 1.0, 0.0).astype(BF)


def span_mask(lo, shape):
    lane = iota(shape, 1)
    return jnp.where((lane >= lo) & (lane < lo + HD), 1.0, 0.0)


def head_window(h):
    start = HD * h // 128 * 128
    width = 128 if HD * h - start + HD <= 128 else 256
    return start, width


def head_mask(h):
    start, width = head_window(h)
    return span_mask(HD * h - start, (1, width)).astype(BF)


def group_window(g):
    return 192 * g // 128 * 128


def group_mask(g):
    lo = 192 * g - group_window(g) + HD * (iota((T, 256), 0) >> 6)
    return span_mask(lo, (T, 256)).astype(BF)


def far_mask():
    row = iota((T, D), 0)
    lo = HD * ((row >> 6) + 4 * ((row >> 4) & 3))
    return span_mask(lo, (T, D)).astype(BF)


def slide_of(meta, pos):
    end = meta[1]
    out = jnp.where(pos >= end, 1, 0)
    for n in range(2, 5):
        end = end + meta[n]
        out = out + jnp.where(pos >= end, 1, 0)
    return out


def row_ids(meta):
    return slide_of(meta, meta[0] * T + tile_of(iota((T, 1), 0)))


def bias_of(meta, pos):
    return jnp.where(row_ids(meta) == slide_of(meta, pos), 0.0, NEG)


def local_bias(meta):
    return bias_of(meta, meta[0] * T + tile_of(iota((1, T), 1)))


def mid_bias(meta):
    t = iota((T, T), 1)
    slot = t >> 6
    dev = meta[0] ^ (((slot & 1) << 1) | (slot >> 1))
    pos = dev * T + ((t >> 4) & 3) * 4 + (t & 15) * 16 + (iota((T, T), 0) >> 6)
    return bias_of(meta, pos)


def far_bias(meta):
    t = iota((T, T), 1)
    s = t >> 4
    place = (((meta[0] >> 2) - (s >> 1)) & 3) * 4 + ((meta[0] & 3) ^ ((s & 1) << 1) ^ (s >> 3))
    row = iota((T, T), 0)
    pos = place * T + (t & 15) * 16 + (row >> 6) + 4 * ((row >> 4) & 3)
    return bias_of(meta, pos)


def far_head(b):
    return b // 4 + 4 * (b % 4)


def fold_mid(x, masks):
    out = x[0:64] * masks[0]
    for c in range(1, 4):
        out = out + x[64 * c : 64 * c + 64] * masks[c]
    return out


def fold_far(x, masks):
    out = x[0:16] * masks[0]
    for b in range(1, 16):
        out = out + x[16 * b : 16 * b + 16] * masks[far_head(b)]
    return out


def pack_rows(x, head_masks):
    mids = [
        head_masks[c] + head_masks[4 + c] + head_masks[8 + c] + head_masks[12 + c]
        for c in range(4)
    ]
    return jnp.concatenate([fold_mid(x, mids), fold_far(x, head_masks)], axis=0)


def norm_parts(inputs):
    mean = jnp.mean(inputs, axis=1, keepdims=True)
    centred = inputs - mean
    var = jnp.mean(centred * centred, axis=1, keepdims=True)
    inv_std = lax.rsqrt(var + 1e-05)
    return centred * inv_std, inv_std


def pack_masks():
    return [span_mask(HD * h, (1, D)).astype(BF) for h in range(HEADS)]


def key_kernel(tok_h, coords, table_h, gain, bias, w_h, inp_o, norm_o, kv_o, pack_o,
               tok, table, weight, sems):
    copies = [
        pltpu.make_async_copy(tok_h, tok, sems.at[0]),
        pltpu.make_async_copy(table_h, table, sems.at[1]),
        pltpu.make_async_copy(w_h.at[:, pl.ds(D, D)], weight.at[0], sems.at[2]),
        pltpu.make_async_copy(w_h.at[:, pl.ds(2 * D, D)], weight.at[1], sems.at[3]),
    ]
    for copy in copies:
        copy.start()
    sort = sort_matrix()
    grid = iota((T, T), 0)
    hots = []
    for axis in range(2):
        hot = jnp.where(grid == coords[axis : axis + 1, :], 1.0, 0.0).astype(BF)
        hots.append(nt(sort, hot).astype(BF))
    copies[0].wait()
    tok_s = nn(sort, tok[...])
    copies[1].wait()
    parts = []
    for hot in hots:
        found = nn(hot, table[...])
        parts.append(found[:, :384] + found[:, 384:768] + found[:, 768:])
    inputs = tok_s + jnp.concatenate(parts, axis=1)
    inp_o[...] = inputs
    unit, _ = norm_parts(inputs)
    normed = (unit * gain[...].reshape(1, D) + bias[...].reshape(1, D)).astype(BF)
    norm_o[...] = normed
    masks = pack_masks()
    for n in range(2):
        copies[2 + n].wait()
        part = nn(normed, weight[n]).astype(BF)
        kv_o[:, D * n : D * (n + 1)] = part
        pack_o[:, D * n : D * (n + 1)] = pack_rows(part, masks)


def query_kernel(normed, w_qkv, w_out, cot, q_o, da_o, cot_o, pack_o):
    cot_s = nn(sort_matrix(), cot[...]).astype(BF)
    cot_o[...] = cot_s
    q = nn(normed[...], w_qkv[...]).astype(BF)
    q_o[...] = q
    d_att = nt(cot_s, w_out[...]).astype(BF)
    da_o[...] = d_att
    masks = pack_masks()
    pack_o[:, :D] = pack_rows(q, masks)
    pack_o[:, D:] = pack_rows(d_att, masks)


def soft(scores):
    top = jnp.max(scores, axis=1, keepdims=True)
    shares = jnp.exp(scores - top)
    return top, jnp.sum(shares, axis=1, keepdims=True), shares.astype(BF)


def local_forward_kernel(meta, q_r, kv, *refs, first):
    o_o, top_o, sum_o = refs[-3:]
    bias = local_bias(meta)
    o_o[...] = jnp.zeros_like(o_o)
    lane = iota((T, 128), 1)
    tops = jnp.full((T, 128), NEG, F32)
    sums = jnp.zeros((T, 128), F32)
    base = HD * first
    for h in range(first, first + 8):
        s, w = head_window(h)
        mask = head_mask(h)
        scores = nt(q_r[:, s : s + w] * mask, kv[:, s : s + w]) * SCALE + bias
        top, total, shares = soft(scores)
        tops = jnp.where(lane == h, top, tops)
        sums = jnp.where(lane == h, total, sums)
        o_o[:, s - base : s - base + w] += nn(shares, kv[:, D + s : D + s + w] * mask)
    top_o[...] = tops
    sum_o[...] = sums
    if first:
        mid_forward(meta, q_r, *refs[:-3])


def mid_forward(meta, q_r, part, twin, mid_o, top_o, sum_o):
    lane = iota((T, 128), 1)
    row = iota((T, 128), 0)
    got = (part, None, None, None, twin)
    tops = jnp.full((T, 128), NEG, F32)
    sums = jnp.zeros((T, 128), F32)
    bias = mid_bias(meta)
    for g in range(4):
        s = group_window(g)
        q = q_r[:, s : s + 256] * group_mask(g)
        top, total, shares = soft(nt(q, mid_rows(got, s, 256)) * SCALE + bias)
        here = lane == 4 * g + (row >> 6)
        tops = jnp.where(here, top, tops)
        sums = jnp.where(here, total, sums)
        mid_o[g] = nn(shares, mid_rows(got, D + s, 256))
    top_o[...] = tops
    sum_o[...] = sums


def mid_rows(got, lo, width):
    return jnp.concatenate([got[0][:128, lo : lo + width], got[4][:128, lo : lo + width]], axis=0)


def far_rows(got, lo, width):
    at = slice(lo, lo + width)
    rows = []
    for n in (0, 4):
        rows.append(got[n][128:, at])
        rows += [got[n + d][:, at] for d in (1, 2, 3)]
    return jnp.concatenate(rows, axis=0)


def expand_matrix():
    head = iota((128, D), 0)
    lane = iota((128, D), 1)
    return jnp.where((lane >= head * HD) & (lane < head * HD + HD), 1.0, 0.0).astype(BF)


def gather_matrix():
    lane = iota((D, 128), 0)
    head = iota((D, 128), 1)
    return jnp.where((lane >= head * HD) & (lane < head * HD + HD), 1.0, 0.0).astype(BF)


def remote_forward_kernel(meta, q_r, *refs):
    got = refs[:8]
    o_1, top_1, sum_1, mid_parts, top_m, sum_m, o_2, top_2, sum_2 = refs[8:17]
    d_att, pack, att_o, stat_o, send_o = refs[17:]
    lane = iota((T, 128), 1)
    row = iota((T, 128), 0)
    top_l = jnp.where(lane < 8, top_1[...], top_2[...])
    sum_l = jnp.where(lane < 8, sum_1[...], sum_2[...])
    tops_m = top_m[...]
    sums_m = sum_m[...]
    mask = far_mask()
    scores = nt(q_r[...] * mask, far_rows(got, 0, D)) * SCALE + far_bias(meta)
    top, total, shares = soft(scores)
    far_part = nn(shares, far_rows(got, D, D))
    here = lane == (row >> 6) + 4 * ((row >> 4) & 3)
    tops_f = jnp.where(here, top, NEG)
    sums_f = jnp.where(here, total, 0.0)
    highest = jnp.maximum(jnp.maximum(top_l, tops_m), tops_f)
    f_l = jnp.exp(top_l - highest)
    f_m = jnp.exp(tops_m - highest)
    f_f = jnp.exp(tops_f - highest)
    totals = f_l * sum_l + f_m * sums_m + f_f * sums_f
    totals = jnp.where(lane < HEADS, totals, 1.0)
    inverse = 1.0 / totals
    lse = highest + jnp.log(totals)
    w_m = f_m * inverse
    o_l = jnp.concatenate([o_1[...], o_2[...]], axis=1)
    att = o_l * exact(f_l * inverse, expand_matrix())
    w_f = jnp.sum(jnp.where(here, f_f * inverse, 0.0), axis=1, keepdims=True)
    att = att + far_part * w_f * mask.astype(F32)
    acc = [att[:, 128 * n : 128 * n + 128] for n in range(6)]
    for g in range(4):
        n = group_window(g) // 128
        w_g = jnp.sum(jnp.where(lane == 4 * g + (row >> 6), w_m, 0.0), axis=1, keepdims=True)
        add = mid_parts[g] * w_g * group_mask(g).astype(F32)
        acc[n] = acc[n] + add[:, :128]
        acc[n + 1] = acc[n + 1] + add[:, 128:]
    att = jnp.concatenate(acc, axis=1).astype(BF)
    att_o[...] = att
    prod = d_att[...].astype(F32) * att.astype(F32)
    delta = exact(prod, gather_matrix())
    stat = jnp.where(lane < HEADS, lse, pltpu.roll(delta, HEADS, 1))
    stat = jnp.where(lane < 2 * HEADS, stat, 0.0)
    stat_o[...] = stat
    one = iota((1, 128), 1)
    send_o[:, : 2 * D] = pack[...]
    mids = fold_mid(stat, [jnp.where((one & 3) == c, 1.0, 0.0) for c in range(4)])
    fars = fold_far(stat, [jnp.where((one & 15) == h, 1.0, 0.0) for h in range(HEADS)])
    send_o[:, 2 * D :] = three_parts(jnp.concatenate([mids, fars], axis=0))


def three_parts(x):
    lane = iota(x.shape, 1)
    hi = x.astype(BF).astype(F32)
    mid = (x - hi).astype(BF).astype(F32)
    low = x - hi - mid
    parts = jnp.where(lane < 64, pltpu.roll(mid, 32, 1), pltpu.roll(low, 64, 1))
    return jnp.where(lane < 32, hi, parts).astype(BF)


def out_kernel(att, inp, w_out, out_o):
    layer = (inp[...] + nn(att[...], w_out[...])).astype(BF)
    out_o[...] = nn(unsort_matrix(), layer).astype(BF)


def pick_mid_column(stat, col):
    return jnp.concatenate(
        [stat[64 * c : 64 * c + 64, col + c : col + c + 1] for c in range(4)], axis=0
    )


def pick_far_column(stat, col):
    return jnp.concatenate(
        [
            stat[16 * b : 16 * b + 16, col + far_head(b) : col + far_head(b) + 1]
            for b in range(16)
        ],
        axis=0,
    )


def local_backward_kernel(meta, q_r, kv, d_att, stat, *refs, first):
    dq_o, dk_o, dv_o = refs[-3:]
    bias = local_bias(meta)
    stat_t = stat[...].T
    dq_o[...] = jnp.zeros_like(dq_o)
    dk_o[...] = jnp.zeros_like(dk_o)
    dv_o[...] = jnp.zeros_like(dv_o)
    base = HD * first
    for h in range(first, first + 8):
        s, w = head_window(h)
        t = s - base
        mask = head_mask(h)
        q = q_r[:, s : s + w] * mask
        k = kv[:, s : s + w] * mask
        da = d_att[:, s : s + w] * mask
        scores = nt(k, q) * SCALE + bias
        shares = jnp.exp(scores - stat_t[h : h + 1, :])
        d_shares = nt(kv[:, D + s : D + s + w], da)
        ds = (shares * (d_shares - stat_t[HEADS + h : HEADS + h + 1, :])).astype(BF)
        dk_o[:, t : t + w] += nn(ds, q)
        dv_o[:, t : t + w] += nn(shares.astype(BF), da)
        dq_o[:, t : t + w] += tn(ds, k)
    if first:
        mid_key_backward(meta, kv, *refs[:-3])


def mid_key_backward(meta, kv, part, twin, dk_o, dv_o):
    got = (part, None, None, None, twin)
    stat_t = joined_stats(mid_rows(got, 2 * D, 128))
    dk_o[...] = jnp.zeros_like(dk_o)
    dv_o[...] = jnp.zeros_like(dv_o)
    bias = mid_bias(meta)
    for g in range(4):
        s = group_window(g)
        mask = group_mask(g)
        mask_f = mask.astype(F32)
        q = mid_rows(got, s, 256)
        da = mid_rows(got, D + s, 256)
        scores = nt(kv[:, s : s + 256] * mask, q) * SCALE + bias
        shares = jnp.exp(scores - spread_mid(stat_t, 4 * g))
        d_shares = nt(kv[:, D + s : D + s + 256] * mask, da)
        ds = (shares * (d_shares - spread_mid(stat_t, HEADS + 4 * g))).astype(BF)
        dk_o[:, s : s + 256] += nn(ds, q) * mask_f
        dv_o[:, s : s + 256] += nn(shares.astype(BF), da) * mask_f


def query_backward_kernel(meta, q_r, d_att, stat, *refs):
    got, dq_o = refs[:8], refs[8]
    dq_o[...] = jnp.zeros_like(dq_o)
    mid = mid_bias(meta)
    for g in range(4):
        s = group_window(g)
        mask = group_mask(g)
        k = mid_rows(got, s, 256)
        scores = nt(q_r[:, s : s + 256] * mask, k) * SCALE + mid
        shares = jnp.exp(scores - pick_mid_column(stat, 4 * g))
        d_shares = nt(d_att[:, s : s + 256] * mask, mid_rows(got, D + s, 256))
        ds = (shares * (d_shares - pick_mid_column(stat, HEADS + 4 * g))).astype(BF)
        dq_o[:, s : s + 256] += nn(ds, k) * mask.astype(F32)
    mask = far_mask()
    k = far_rows(got, 0, D)
    scores = nt(q_r[...] * mask, k) * SCALE + far_bias(meta)
    shares = jnp.exp(scores - pick_far_column(stat, 0))
    d_shares = nt(d_att[...] * mask, far_rows(got, D, D))
    ds = (shares * (d_shares - pick_far_column(stat, HEADS))).astype(BF)
    dq_o[...] += nn(ds, k) * mask.astype(F32)


def spread_mid(stat_t, row):
    return jnp.concatenate(
        [jnp.broadcast_to(stat_t[row + c : row + c + 1, :], (64, T)) for c in range(4)], axis=0
    )


def spread_far(stat_t, row):
    return jnp.concatenate(
        [
            jnp.broadcast_to(stat_t[row + far_head(b) : row + far_head(b) + 1, :], (16, T))
            for b in range(16)
        ],
        axis=0,
    )


def joined_stats(rows):
    x = rows.astype(F32).T
    return x[:32] + (x[32:64] + x[64:96])


def key_backward_kernel(meta, kv, *refs):
    got = refs[:8]
    dq_r, dq_1, dk_1, dv_1, dk_m, dv_m, dq_2, dk_2, dv_2, cot = refs[8:18]
    all_o, kept_o, sent_o, dk_s, dv_s = refs[18:]
    dk_s[...] = jnp.concatenate([dk_1[...], dk_2[...]], axis=1) + dk_m[...]
    dv_s[...] = jnp.concatenate([dv_1[...], dv_2[...]], axis=1) + dv_m[...]
    stat_t = joined_stats(far_rows(got, 2 * D, 128))
    mask = far_mask()
    mask_f = mask.astype(F32)
    q = far_rows(got, 0, D)
    da = far_rows(got, D, D)
    scores = nt(kv[:, :D] * mask, q) * SCALE + far_bias(meta)
    shares = jnp.exp(scores - spread_far(stat_t, 0))
    d_shares = nt(kv[:, D:] * mask, da)
    ds = (shares * (d_shares - spread_far(stat_t, HEADS))).astype(BF)
    dk_s[...] += nn(ds, q) * mask_f
    dv_s[...] += nn(shares.astype(BF), da) * mask_f
    dq = jnp.concatenate([dq_1[...], dq_2[...]], axis=1) + dq_r[...]
    d_q = (dq * SCALE).astype(BF)
    d_k = (dk_s[...] * SCALE).astype(BF)
    d_v = dv_s[...].astype(BF)
    all_o[:, :D] = d_q
    all_o[:, D : 2 * D] = d_k
    all_o[:, 2 * D :] = d_v
    first = meta[5] == 0
    kept_o[:, :D] = jnp.where(first, d_q, d_v)
    kept_o[:, D:] = jnp.where(first, d_k, cot[...])
    sent_o[:, :D] = jnp.where(first, d_v, d_q)
    sent_o[:, D:] = jnp.where(first, cot[...], d_k)


def left_kernel(meta, norm_a, norm_b, att_a, att_b, left):
    left[0] = jnp.concatenate([norm_a[...], norm_b[...]], axis=0).T
    left[1] = left[0]

    @pl.when(meta[5] == 1)
    def _():
        left[1] = jnp.concatenate([att_a[...], att_b[...]], axis=0).T


def weight_grad_kernel(meta, own, other, left, keep_o, s1, s2, s3):
    for d, out in ((2, s2), (1, s1), (3, s3), (0, keep_o)):
        j = (meta[6] + d) & 3
        cols = pl.ds(pl.multiple_of(j * WIDE, 128), WIDE)
        right = jnp.concatenate([own[:, cols], other[:, cols]], axis=0)
        out[...] = nn(left[j >> 1], right).astype(out.dtype)


def token_grad_kernel(d_qkv, w_qkv, inp, gain, cot, tok_o, ext_o):
    d_normed = nt(d_qkv[...], w_qkv[...])
    unit, inv_std = norm_parts(inp[...])
    d_gain = jnp.sum(d_normed * unit, axis=0, keepdims=True)
    d_bias = jnp.sum(d_normed, axis=0, keepdims=True)
    ext_o[...] = two_parts(jnp.concatenate(
        [d_gain[:, :WIDE], d_gain[:, WIDE:], d_bias[:, :WIDE], d_bias[:, WIDE:],
         jnp.zeros((4, WIDE), F32)], axis=0))
    d_unit = d_normed * gain[...].reshape(1, D)
    mean_a = jnp.mean(d_unit, axis=1, keepdims=True)
    mean_b = jnp.mean(d_unit * unit, axis=1, keepdims=True)
    d_tok = cot[...].astype(F32) + inv_std * (d_unit - mean_a - unit * mean_b)
    tok_o[...] = nn(unsort_matrix(), d_tok.astype(BF)).astype(BF)


def two_parts(ext):
    hi = ext.astype(BF)
    return jnp.concatenate([hi, (ext - hi.astype(F32)).astype(BF)], axis=0)


def whole_of(rows):
    return rows[:8].astype(F32) + rows[8:].astype(F32)


def ring_total(meta, slot, own, got, pad):
    pad[meta[slot]] = own
    for d, piece in enumerate(got, 1):
        pad[(meta[slot] - d) & 3] = piece
    return (pad[0] + pad[1]) + (pad[2] + pad[3])


def add_a_kernel(meta, keep, r1, r2, r3, ext, keep_o, s1, s2, s3):
    rows = D // 4
    for d, out in ((2, s2), (1, s1), (3, s3), (0, keep_o)):
        at = pl.ds(pl.multiple_of(((meta[7] + d) & 3) * rows, 16), rows)
        total = keep[at, :] + (r1[at, :].astype(F32) + r2[at, :].astype(F32) + r3[at, :].astype(F32))
        if d == 0:
            out[...] = total
        else:
            out[:rows] = total.astype(BF)
            out[rows:] = ext[...]


def add_b_kernel(meta, keep, r1, r2, r3, ext, out, pad):
    rows = D // 4
    got = (r1, r2, r3)
    total = keep[...]
    for r in got:
        total = total + r[:rows].astype(F32)
    out[:rows] = total.astype(BF)
    sums = ring_total(meta, 7, whole_of(ext[...]), [whole_of(r[rows:]) for r in got], pad)
    out[rows:] = two_parts(sums)


def add_c_kernel(own, r1, r2, r3, out):
    rows = D // 4

    def total(a, b, c, d):
        return (a + c) + (b + d)

    out[:rows] = total(*[r[:rows].astype(F32) for r in (own, r1, r2, r3)]).astype(BF)
    out[rows:] = two_parts(total(*[whole_of(r[rows:]) for r in (own, r1, r2, r3)]))


def merge_kernel(meta, own, r1, r2, r3, out):
    rows = D // 4
    out[D:] = own[rows:]
    for d, piece in enumerate((own, r1, r2, r3)):
        at = pl.ds(pl.multiple_of(((meta[7] - d) & 3) * rows, 16), rows)
        out[at, :] = piece[:rows]


def finish_kernel(meta, *refs, marks, first, last):
    count = len(marks)
    pieces, refs = refs[:count], refs[count:]
    if last:
        tails, refs = refs[:8], refs[8:]
    if not first:
        refs = refs[2:]
    qkv_o, out_o, *refs = refs
    if last:
        gain_o, bias_o, *refs = refs
    sems, wide = refs[0], refs[1 : 1 + count]
    for n, (piece, (core, turn, row)) in enumerate(zip(pieces, marks)):
        chunk = (meta[5] ^ core) * 4 + ((meta[9 if core else 6] - turn) & 3)
        size = wide[n].shape[0]
        wide[n][...] = piece[:size].astype(F32)

        @pl.when(chunk < 6)
        def _(n=n, chunk=chunk, row=row, size=size):
            at = pl.ds(pl.multiple_of(chunk * WIDE, 128), WIDE)
            to = qkv_o.at[pl.ds(row, size), at]
            pltpu.make_async_copy(wide[n], to, sems.at[n]).start()

        @pl.when(chunk >= 6)
        def _(n=n, chunk=chunk, row=row, size=size):
            at = pl.ds(pl.multiple_of((chunk - 6) * WIDE, 128), WIDE)
            to = out_o.at[pl.ds(row, size), at]
            pltpu.make_async_copy(wide[n], to, sems.at[n]).start()

    if last:
        pad = refs[1 + count]
        for n, tail in enumerate(tails):
            core = n // 4
            place = (meta[9 if core else 6] - n % 4) & 3
            pad[(meta[5] ^ core) * 4 + place] = whole_of(tail[...])
        total = pad[0]
        for n in range(1, 8):
            total = total + pad[n]
        gain_o[...] = jnp.concatenate([total[0:1], total[1:2]], axis=1).reshape(D)
        bias_o[...] = jnp.concatenate([total[2:3], total[3:4]], axis=1).reshape(D)
    for n in range(count):
        to = qkv_o.at[pl.ds(0, wide[n].shape[0]), pl.ds(0, WIDE)]
        pltpu.make_async_copy(wide[n], to, sems.at[n]).wait()


def finish(meta, pieces, outs, tails=None):
    first, last = outs is None, tails is not None
    marks = tuple(piece[1:] for piece in pieces)
    arrays = [piece[0] for piece in pieces]
    smem = pl.BlockSpec(memory_space=pltpu.SMEM)
    anywhere = pl.BlockSpec(memory_space=pl.ANY)
    whole = pl.BlockSpec(memory_space=pltpu.VMEM)
    args = [meta, *arrays]
    in_specs = [smem] + [whole] * len(arrays)
    if last:
        args += tails
        for tail in tails:
            index = (tail.shape[0] // 16 - 1, 0)
            in_specs.append(pl.BlockSpec((16, WIDE), lambda i, index=index: index))
    aliases = {}
    if not first:
        aliases = {len(args): 0, len(args) + 1: 1}
        args += list(outs)
        in_specs += [anywhere] * 2
    out_shape = [jax.ShapeDtypeStruct((D, 3 * D), F32), jax.ShapeDtypeStruct((D, D), F32)]
    out_specs = [anywhere] * 2
    scratch = [pltpu.SemaphoreType.DMA((len(pieces),))]
    for array in arrays:
        scratch.append(pltpu.VMEM((array.shape[0] // WIDE * WIDE, WIDE), F32))
    if last:
        out_shape += [jax.ShapeDtypeStruct((D,), F32)] * 2
        out_specs += [pl.BlockSpec((D,), lambda i: (0,))] * 2
        scratch += [pltpu.VMEM((8, 8, WIDE), F32)]
    return pl.pallas_call(
        functools.partial(finish_kernel, marks=marks, first=first, last=last),
        grid=(1,),
        in_specs=in_specs,
        out_specs=out_specs,
        out_shape=out_shape,
        scratch_shapes=scratch,
        input_output_aliases=aliases,
        compiler_params=pltpu.CompilerParams(vmem_limit_bytes=24 << 20),
        name="finish",
    )(*args)


def call(kernel, outs, *args, smem=0, scratch=(), name=None, limit=24, windows=None,
         anywhere=()):
    specs = [pl.BlockSpec(memory_space=pltpu.SMEM)] * smem
    specs += [pl.BlockSpec(memory_space=pltpu.VMEM)] * (len(args) - smem)
    for n in anywhere:
        specs[n] = pl.BlockSpec(memory_space=pl.ANY)
    for n, (shape, index) in (windows or {}).items():
        specs[n] = pl.BlockSpec(shape, lambda i, index=index: index)
    return pl.pallas_call(
        kernel,
        grid=(1,) if windows else (),
        out_shape=[jax.ShapeDtypeStruct(shape, dtype) for shape, dtype in outs],
        in_specs=specs,
        out_specs=[pl.BlockSpec(memory_space=pltpu.VMEM)] * len(outs),
        scratch_shapes=scratch,
        compiler_params=pltpu.CompilerParams(vmem_limit_bytes=limit << 20),
        name=name,
    )(*args)


def swap_seq(block, code):
    return lax.ppermute(block, "seq", [(i, i ^ code) for i in range(16)])


def z_send(block):
    def shift(d):
        return lax.ppermute(block, "seq", [(i, (i + 4 * d) % 16) for i in range(16)])

    got = {d: shift(d) for d in (2, 1, 3)}
    return [got[1], got[2], got[3]]


def after(*values):
    return lax.optimization_barrier(values)


def join(*blocks):
    return jnp.concatenate(blocks, axis=0)


def decode(i):
    dp, seq = i // 16, i % 16
    return [dp // 2, (seq // 2) % 2 * 2 + dp % 2, seq // 4, seq % 2]


def encode(x, y, z, core):
    return (x * 2 + y % 2) * 16 + z * 4 + y // 2 * 2 + core


def ring_route(stage, d):
    route = []
    for i in range(128):
        place = decode(i)
        axis = (stage + place[3]) % 3
        place[axis] = (place[axis] + d) % 4
        route.append((i, encode(*place)))
    return route


def hop(block, stage, d):
    return lax.ppermute(block, AXES, ring_route(stage, d))


def ring_send(blocks, stage):
    got = {d: hop(blocks[d - 1], stage, d) for d in (2, 1, 3)}
    return got[1], got[2], got[3]


def place_meta(lengths):
    dp = lax.axis_index("dp").astype(jnp.int32)
    seq = lax.axis_index("seq").astype(jnp.int32)
    core = seq & 1
    coords = [dp >> 1, (seq & 2) + (dp & 1), seq >> 2]
    turns = [jnp.where(core == 0, coords[n], coords[(n + 1) % 3]) for n in range(3)]
    other = jnp.where(core == 0, coords[1], coords[0])
    values = jnp.stack([core] + turns + [other])
    return jnp.concatenate([seq[None], lengths, values, jnp.zeros((6,), jnp.int32)])


def sum_everywhere(meta, keep, sends, ext, beside):
    cut = D // 4
    got = ring_send(sends, 0)
    *got, _ = after(*got, beside)
    keep, *sends = call(
        add_a_kernel,
        [((cut, WIDE), F32)] + [((cut + 16, WIDE), BF)] * 3,
        meta, keep, *got, ext, smem=1, name="add_a",
    )
    got = ring_send(sends, 1)
    block = call(
        add_b_kernel, [((cut + 16, WIDE), BF)],
        meta, keep, *got, ext, smem=1, name="add_b", scratch=[pltpu.VMEM((4, 8, WIDE), F32)],
    )[0]
    got = ring_send([block] * 3, 2)
    block = call(add_c_kernel, [((cut + 16, WIDE), BF)], block, *got, name="add_c")[0]
    got = ring_send([block] * 3, 1)
    block = call(
        merge_kernel, [((D + 16, WIDE), BF)], meta, block, *got, smem=1, name="merge_b",
    )[0]
    ring = [block, *ring_send([block] * 3, 0)]
    twin = [swap_seq(block, 1)]
    outs = finish(meta, [(block, 0, 0, 0), (twin[0], 1, 0, 0)], None)
    ring[2], first = after(ring[2], outs[0])
    twin += [None, swap_seq(ring[2], 1), None]
    outs = finish(meta, [(ring[2], 0, 2, 0)], (first, outs[1]))
    ring[1], ring[3], *outs = after(ring[1], ring[3], *outs)
    twin[1], twin[3] = swap_seq(ring[1], 1), swap_seq(ring[3], 1)
    pieces = [(ring[1], 0, 1, 0), (ring[3], 0, 3, 0), (twin[2], 1, 2, 0)]
    pieces += [(twin[1], 1, 1, 0), (twin[3], 1, 3, 0)]
    return finish(meta, pieces, outs, ring + twin)


def position_table():
    quarter = D // 4
    frequency = 1.0 / 10000.0 ** (np.arange(quarter) / quarter)
    angle = np.arange(256)[:, None] * frequency[None, :]
    exact_values = np.concatenate([np.sin(angle), np.cos(angle)], axis=1).astype(np.float32)
    parts = []
    rest = exact_values
    for _ in range(3):
        part = rest.astype(jnp.bfloat16)
        parts.append(part)
        rest = rest - part.astype(np.float32)
    return np.concatenate(parts, axis=1)


def per_device(tokens, tile_coords, slide_lengths, norm_gain, norm_bias, w_qkv, w_out, cotangent):
    meta = place_meta(slide_lengths[0])
    table = jnp.asarray(position_table())
    inp, normed, kv, kv_pack = call(
        key_kernel,
        [((T, D), F32), ((T, D), BF), ((T, 2 * D), BF), ((80, 2 * D), BF)],
        tokens[0], tile_coords[0], table, norm_gain, norm_bias, w_qkv, name="keys", limit=60,
        anywhere=(0, 2, 5),
        scratch=[
            pltpu.VMEM((T, D), BF), pltpu.VMEM((T, 3 * D // 2), BF), pltpu.VMEM((2, D, D), BF),
            pltpu.SemaphoreType.DMA((4,)),
        ],
    )
    from_y = swap_seq(kv_pack, 2)
    norm_b = swap_seq(normed, 1)
    q, d_att, cot, qd_pack = call(
        query_kernel,
        [((T, D), BF), ((T, D), BF), ((T, D), BF), ((80, 2 * D), BF)],
        normed, w_qkv, w_out, cotangent[0], name="queries", limit=60,
        windows={1: ((D, D), (0, 0))},
    )
    from_y, q, norm_b = after(from_y, q, norm_b)
    far = join(kv_pack[64:], from_y[64:])
    from_z = z_send(far)
    far, q = after(far, q)
    part = join(kv_pack[:64], from_y[:64], far)
    twin = swap_seq(part, 1)
    stat_shape = ((T, 128), F32)
    out_1 = call(
        functools.partial(local_forward_kernel, first=0),
        [((T, D // 2), F32), stat_shape, stat_shape],
        meta, q, kv, smem=1, name="local_forward",
    )
    out_2 = call(
        functools.partial(local_forward_kernel, first=8),
        [((4, T, 256), F32), stat_shape, stat_shape, ((T, D // 2), F32), stat_shape, stat_shape],
        meta, q, kv, part, twin, smem=1, name="local_forward",
    )
    *from_z, _, _ = after(*from_z, out_1[0], out_2[0])
    got_kv = (part, *from_z, twin, *[swap_seq(rows, 1) for rows in from_z])
    att, stat, pack = call(
        remote_forward_kernel,
        [((T, D), BF), ((T, 128), F32), ((80, 2 * D + 128), BF)],
        meta, q, *got_kv, *out_1, *out_2, d_att, qd_pack,
        smem=1, name="remote_forward",
    )
    from_y = swap_seq(pack, 2)
    att_b = swap_seq(att, 1)
    grads_1 = call(
        functools.partial(local_backward_kernel, first=0),
        [((T, D // 2), F32)] * 3,
        meta, q, kv, d_att, stat, smem=1, name="local_backward",
    )
    dq_r = call(
        query_backward_kernel, [((T, D), F32)],
        meta, q, d_att, stat, *got_kv, smem=1, name="query_backward",
    )[0]
    from_y, att_b, dq_r, *grads_1 = after(from_y, att_b, dq_r, *grads_1)
    far = join(pack[64:], from_y[64:])
    from_z = z_send(far)
    far, q = after(far, q)
    part = join(pack[:64], from_y[:64], far)
    twin = swap_seq(part, 1)
    grads_2 = call(
        functools.partial(local_backward_kernel, first=8),
        [((T, D), F32)] * 2 + [((T, D // 2), F32)] * 3,
        meta, q, kv, d_att, stat, part, twin, smem=1, name="local_backward",
    )
    *from_z, _ = after(*from_z, grads_2[0])
    got_qd = (part, *from_z, twin, *[swap_seq(rows, 1) for rows in from_z])
    d_qkv, own, sent = call(
        key_backward_kernel,
        [((T, 3 * D), BF), ((T, 2 * D), BF), ((T, 2 * D), BF)],
        meta, kv, *got_qd, dq_r, *grads_1, *grads_2, cot,
        smem=1, name="key_backward",
        scratch=[pltpu.VMEM((T, D), F32), pltpu.VMEM((T, D), F32)],
    )
    left = call(
        left_kernel, [((2, D, 2 * T), BF)],
        meta, normed, norm_b, att, att_b, smem=1, name="left",
    )[0]
    other, left = after(swap_seq(sent, 1), left)
    keep, *sends = call(
        weight_grad_kernel,
        [((D, WIDE), F32)] + [((D, WIDE), BF)] * 3,
        meta, own, other, left, smem=1, name="weight_grad",
    )
    d_tokens, ext = call(
        token_grad_kernel,
        [((T, D), BF), ((16, WIDE), BF)],
        d_qkv, w_qkv, inp, norm_gain, cot, name="token_grad",
    )
    att, _ = after(att, keep)
    layer_out = call(out_kernel, [((T, D), BF)], att, inp, w_out, name="layer_out")[0]
    dw_qkv, dw_out, d_gain, d_bias = sum_everywhere(meta, keep, sends, ext, layer_out)
    return (
        layer_out[None],
        d_tokens[None],
        dw_qkv,
        dw_out,
        d_gain,
        d_bias,
    )


def solution(mesh):
    return jax.shard_map(
        per_device,
        mesh=mesh,
        in_specs=(
            P("dp", "seq", None),
            P("dp", None, "seq"),
            P("dp", None),
            P(),
            P(),
            P(),
            P(),
            P("dp", "seq", None),
        ),
        out_specs=(P("dp", "seq", None), P("dp", "seq", None), P(), P(), P(), P()),
        check_vma=False,
    )
```
